32 devices in a mesh: dp: 8 (over y, x, core), shard: 4 (over z).
Axes of the slice: x: 2, y: 2, z: 4, core: 2. Of those that a mesh axis runs over, the one named last changes fastest.
Arguments:
- tokens: bfloat16 [64, 64, 768], P(('dp', 'shard')), may hold values from -6 to 6
- cotangent: bfloat16 [64, 64, 768], P(('dp', 'shard')), may hold values from -6 to 6
- doc_lengths: int32 [64, 3], P(('dp', 'shard')), may hold values from 0 to 64, as said below
- qkv_w: float32 [3, 768, 768], P(None, 'dp', 'shard'), may hold values from -0.21875 to 0.21875
- out_w: float32 [768, 768], P('dp', 'shard'), may hold values from -0.625 to 0.625
- ffn_w: float32 [2, 768, 3072], P(None, 'dp', 'shard'), may hold values from -0.21875 to 0.21875
- vecs: float32 [12, 768], P(None, ('dp', 'shard')), may hold values from -0.6 to 1.5
- qkv_mom: float32 [3, 768, 768], P(None, 'dp', 'shard'), may hold values from -112 to 112
- out_mom: float32 [768, 768], P('dp', 'shard'), may hold values from -112 to 112
- ffn_mom: float32 [2, 768, 3072], P(None, 'dp', 'shard'), may hold values from -112 to 112
- vec_mom: float32 [12, 768], P(None, ('dp', 'shard')), may hold values from -160 to 160
Outputs:
- layer_out: bfloat16 [64, 64, 768], P(('dp', 'shard'))
- tokens_grad: float32 [64, 64, 768], P(('dp', 'shard'))
- qkv_grad: float32 [3, 768, 768], P(None, 'dp', 'shard')
- out_grad: float32 [768, 768], P('dp', 'shard')
- ffn_grad: float32 [2, 768, 3072], P(None, 'dp', 'shard')
- vec_grad: float32 [12, 768], P(None, ('dp', 'shard'))
- qkv_mom_new: float32 [3, 768, 768], P(None, 'dp', 'shard')
- out_mom_new: float32 [768, 768], P('dp', 'shard')
- ffn_mom_new: float32 [2, 768, 3072], P(None, 'dp', 'shard')
- vec_mom_new: float32 [12, 768], P(None, ('dp', 'shard'))
- qkv_new: float32 [3, 768, 768], P(None, 'dp', 'shard')
- out_new: float32 [768, 768], P('dp', 'shard')
- ffn_new: float32 [2, 768, 3072], P(None, 'dp', 'shard')
- vec_new: float32 [12, 768], P(None, ('dp', 'shard'))
The draws below stay inside these ranges and needn't reach their ends.
Inputs may be any that keep to these rules, and one draw needn't show every extreme that they name: `doc_lengths`: row s lists the lengths of the documents packed from the start of slot s; a length may be 0; the lengths of a row sum to at most 64 and the rest of the slot is padding; in every draw some slot holds a single document of 64 tokens.
All inputs are finite; a program needn't handle non-finite values.
Results may differ from the reference program's by a relative error of at most 0.018.
Values may be sent and summed in bfloat16 or wider, within the bound.
No kernel may reach another device: no remote copies, remote signals or barrier semaphores. Data moves between devices by JAX's collectives and lax.ppermute only.
A program may use at most 128 MiB of HBM per device.

```python
import math
import jax
import jax.numpy as jnp
from jax import lax

D = 768
HEADS = 12
HEAD = 64
FF = 3072
ROWS = 64
DOCS = 3
NS_STEPS = 3
VEC = 12
SLOTS = 64
TOKENS = 4096
N_SHARD = 4


def draw_doc_lengths(key, part):
    key = jax.random.fold_in(key, 11)
    key_fill, key_shares, key_full = jax.random.split(key, 3)
    level = jax.random.randint(key_fill, (SLOTS,), 3, 9)
    totals = jnp.maximum(ROWS * level * level // 64, 1)
    shares = jax.random.randint(key_shares, (SLOTS, DOCS), 1, 8)
    running = jnp.cumsum(shares, axis=1)
    edges = totals[:, None] * running // running[:, -1:]
    starts = jnp.concatenate([jnp.zeros((SLOTS, 1), jnp.int32), edges[:, :-1]], axis=1)
    lengths = edges - starts
    chosen = jax.random.randint(key_full, (), 0, SLOTS)
    single = jnp.zeros((DOCS,), jnp.int32).at[0].set(ROWS)
    is_full = jnp.arange(SLOTS) == chosen
    return jnp.where(is_full[:, None], single[None, :], lengths).astype(jnp.int32)


def draw_vecs(key, part):
    key = jax.random.fold_in(key, 12)
    key_bias, key_norm_gain = jax.random.split(key)
    biases = jax.random.uniform(key_bias, (VEC, D), jnp.float32, -0.6, 0.6)
    gains = jax.random.uniform(key_norm_gain, (VEC, D), jnp.float32, 0.5, 1.5)
    row = jnp.arange(VEC)[:, None]
    is_gain = (row == 3) | (row == 6)
    return jnp.where(is_gain, gains, biases).astype(jnp.float32)


def levels(rng, shape, shards, low, largest):
    def one(axis_at, shards_of):
        draws = jax.random.uniform(jax.random.fold_in(jax.random.fold_in(rng, 6), axis_at), (shards_of,), jnp.float32, low / len(shards), largest / len(shards))
        return jnp.repeat(jnp.exp(draws), shape[axis_at] // shards_of).reshape((-1,) + (1,) * (len(shape) - axis_at - 1))

    level = one(*shards[0])
    for cut in shards[1:]:
        level = level * one(*cut)
    return level


def gaussian(key, shape, scale, most, cuts=(), kind=jnp.bfloat16):
    loudness = levels(key, shape, cuts, -0.22, 0.18) if cuts else 1.0
    values = jax.random.normal(key, shape, jnp.float32) * scale * loudness
    return jnp.minimum(jnp.maximum(values, -most), most).astype(kind)


def setup_inputs(seed: int = 0) -> dict:
    key_of = jax.random.split(jax.random.key(seed), 12)
    return {
        "tokens": gaussian(key_of[0], (SLOTS, ROWS, D), 1.0, 6.0, ((0, 32),)),
        "cotangent": gaussian(key_of[1], (SLOTS, ROWS, D), 1.0, 6.0, ((0, 32),)),
        "doc_lengths": draw_doc_lengths(jax.random.fold_in(key_of[11], 71), 0),
        "qkv_w": gaussian(key_of[3], (3, D, D), D ** -0.5, 0.21875, ((1, 8), (2, 4)), jnp.float32),
        "out_w": gaussian(key_of[4], (D, D), (D // 8) ** -0.5, 0.625, ((0, 8), (1, 4)), jnp.float32),
        "ffn_w": gaussian(key_of[5], (2, D, FF), D ** -0.5, 0.21875, ((1, 8), (2, 4)), jnp.float32),
        "vecs": draw_vecs(jax.random.fold_in(key_of[11], 71), 0),
        "qkv_mom": gaussian(key_of[7], (3, D, D), (0.3 * TOKENS ** 0.5), 112.0, ((1, 8), (2, 4)), jnp.float32),
        "out_mom": gaussian(key_of[8], (D, D), (0.3 * TOKENS ** 0.5), 112.0, ((0, 8), (1, 4)), jnp.float32),
        "ffn_mom": gaussian(key_of[9], (2, D, FF), (0.3 * TOKENS ** 0.5), 112.0, ((1, 8), (2, 4)), jnp.float32),
        "vec_mom": gaussian(key_of[10], (VEC, D), (0.4 * TOKENS ** 0.5), 160.0, ((1, 32),), jnp.float32),
    }


@jax.custom_vjp
def low(v):
    return lax.optimization_barrier(v.astype(jnp.bfloat16)).astype(jnp.float32)

@jax.custom_vjp
def low_back(v):
    return v

def low_keep(v):
    return (low(v), None)

def low_pass(kept, grad):
    return (grad,)

def back_keep(v):
    return (v, None)

def back_low(kept, grad):
    return (low(grad),)
low.defvjp(low_keep, low_pass)
low_back.defvjp(back_keep, back_low)
highest = lax.Precision.HIGHEST
masked_score = -1e+30
norm_eps = 1e-12
momentum_decay = 0.9
muon_rate = 0.8
vec_rate = 0.5
coef_first = 3.4445
coef_second = -4.775
coef_third = 2.0315
ortho_eps = 1e-07

def segments(lengths, rows):
    position = jnp.arange(rows, dtype=jnp.int32)
    ends = jnp.cumsum(lengths).astype(jnp.int32)
    segment = lax.optimization_barrier(jnp.sum((position[:, None] >= ends[None, :]).astype(jnp.int32), axis=1))
    valid = position < ends[-1]
    same = segment[:, None] == segment[None, :]
    allowed = same & valid[:, None] | (position[:, None] == position[None, :])
    return (valid, allowed)

def layer_norm(inputs, gain, bias):
    center = inputs - lax.optimization_barrier(jnp.mean(inputs, axis=-1, keepdims=True))
    spread = lax.optimization_barrier(jnp.mean(center * center, axis=-1, keepdims=True))
    return center * lax.rsqrt(spread + norm_eps) * gain + bias

def layer_rows(inputs, lengths, qkv, outw, ffn, vec):
    rows = inputs.shape[0]
    valid, allowed = segments(lengths, rows)
    projected = jnp.einsum('rd,kde->kre', inputs, qkv, precision=highest)
    queries = low(low_back(projected[0] + vec[0])).reshape(rows, HEADS, HEAD)
    key_rows_packed = low(low_back(projected[1])).reshape(rows, HEADS, HEAD)
    valrows = low(low_back(projected[2] + vec[1])).reshape(rows, HEADS, HEAD)
    scores = jnp.einsum('qhd,khd->hqk', queries, key_rows_packed, precision=highest) * HEAD ** (-0.5)
    scores = low_back(jnp.where(allowed[None], scores, masked_score))
    probs = low(jax.nn.softmax(scores, axis=-1))
    mixed = jnp.einsum('hqk,khd->qhd', probs, valrows, precision=highest).reshape(rows, D)
    mixed = low(low_back(mixed))
    attended = low_back(jnp.dot(mixed, outw, precision=highest) + vec[2])
    first = layer_norm(inputs + attended, vec[3], vec[4])
    inner = low_back(jnp.dot(low(first), ffn[0], precision=highest) + vec[8:].reshape(FF))
    activ = low(jax.nn.gelu(inner, approximate=False))
    branch = low_back(jnp.dot(activ, ffn[1].T, precision=highest) + vec[5])
    result = layer_norm(first + branch, vec[6], vec[7])
    return result * valid[:, None].astype(jnp.float32)

def orthogonalize(matrix):
    width = matrix.shape[1] // N_SHARD

    def gram(present):
        blocks = present.reshape(D, N_SHARD, width)
        partial_value = jnp.einsum('ikw,jkw->kij', blocks, blocks, precision=highest)
        return lax.optimization_barrier(jnp.sum(low(partial_value), axis=0))
    present = low(matrix)
    state = matrix
    for step in range(NS_STEPS):
        total = gram(present)
        if step == 0:
            scale = jnp.sqrt(jnp.trace(total)) + ortho_eps
            total = total / (scale * scale)
            present = low(matrix / scale)
        square_b = low(total)
        once = jnp.dot(square_b, present, precision=highest)
        twice = jnp.dot(square_b, low(once), precision=highest)
        state = coef_first * present + coef_second * once + coef_third * twice
        present = low(state)
    return state

def reference(tokens, cotangent, doc_lengths, qkv_w, out_w, ffn_w, vecs, qkv_mom, out_mom, ffn_mom, vec_mom):
    group = math.gcd(SLOTS, max(1, 4096 // ROWS))
    blocks = SLOTS // group
    length_blocks = doc_lengths.reshape(blocks, group, DOCS)

    def forward(qkv, outw, ffn, vec, inputs):
        qkv, outw, ffn, vec = (low(qkv), low(outw), low(ffn), low(vec))

        def one_block(item):
            rows_block, len_block = item
            return jax.vmap(layer_rows, in_axes=(0, 0, None, None, None, None))(rows_block, len_block, qkv, outw, ffn, vec)
        result = lax.map(jax.checkpoint(one_block), (inputs.reshape(blocks, group, ROWS, D), length_blocks))
        return result.reshape(SLOTS, ROWS, D)
    outputs, pullback = jax.vjp(forward, qkv_w, out_w, ffn_w, vecs, tokens.astype(jnp.float32))
    grad_qkv, grad_out, grad_ffn, grad_vec, token_gradient = pullback(cotangent.astype(jnp.float32))
    new_qkv_mom = momentum_decay * qkv_mom + grad_qkv
    new_out_mom = momentum_decay * out_mom + grad_out
    new_ffn_mom = momentum_decay * ffn_mom + grad_ffn
    qkv_dir = jnp.stack([orthogonalize(new_qkv_mom[place]) for place in range(3)])
    out_dir = orthogonalize(new_out_mom)
    ffn_dir = jnp.stack([orthogonalize(new_ffn_mom[place]) for place in range(2)])
    qkv_new = qkv_w - muon_rate * qkv_dir
    out_new = out_w - muon_rate * out_dir
    ffn_new = ffn_w - muon_rate * (FF / D) ** 0.5 * ffn_dir
    new_vec_mom = momentum_decay * vec_mom + grad_vec
    vec_new = vecs - vec_rate * TOKENS ** (-0.5) * new_vec_mom
    return (outputs.astype(jnp.bfloat16), token_gradient, grad_qkv, grad_out, grad_ffn, grad_vec, new_qkv_mom, new_out_mom, new_ffn_mom, new_vec_mom, qkv_new, out_new, ffn_new, vec_new)
```

```python
import math
import jax
import jax.numpy as jnp
from jax import lax
from jax.experimental import pallas as pl
from jax.experimental.pallas import tpu as pltpu
from jax.sharding import PartitionSpec as P

D = 768
HEADS = 12
HEAD = 64
FF = 3072
NS_STEPS = 3


masked_score = -1e30
norm_eps = 1e-12
momentum_decay = 0.9
muon_rate = 0.8
vec_rate = 0.5
coef_first = 3.4445
coef_second = -4.775
coef_third = 2.0315
ortho_eps = 1e-07


def spread_2(block, axis, owner):
    block = jnp.where(lax.axis_index(axis) == owner, block, jnp.zeros_like(block))
    return lax.psum(block, axis)


def segments(lengths, rows):
    position = jnp.arange(rows, dtype=jnp.int32)
    ends = jnp.cumsum(lengths)
    segment = jnp.sum((position[:, None] >= ends[None, :]).astype(jnp.int32), axis=1)
    valid = position < ends[-1]
    same = segment[:, None] == segment[None, :]
    allowed = same & valid[:, None] | (position[:, None] == position[None, :])
    return (valid, allowed)


def layer_norm(inputs, gain, bias):
    center = inputs - jnp.mean(inputs, axis=-1, keepdims=True)
    spread = jnp.mean(center * center, axis=-1, keepdims=True)
    return center * lax.rsqrt(spread + norm_eps) * gain + bias


def gelu_exact(inputs):
    return jax.nn.gelu(inputs, approximate=False)


def split_heads(matrix):
    return matrix.reshape(matrix.shape[0], HEADS, HEAD)


def gather_weights(qkv_w, out_w, ffn_w, vecs):
    pieces = (
        qkv_w.astype(jnp.bfloat16),
        out_w.astype(jnp.bfloat16),
        ffn_w.astype(jnp.bfloat16),
        vecs.astype(jnp.bfloat16),
    )
    across = (
        lax.all_gather(pieces[0], "shard", axis=2, tiled=True),
        lax.all_gather(pieces[1], "shard", axis=1, tiled=True),
        lax.all_gather(pieces[2], "shard", axis=2, tiled=True),
        lax.all_gather(pieces[3], "shard", axis=1, tiled=True),
    )
    return (
        lax.all_gather(across[0], "dp", axis=1, tiled=True),
        lax.all_gather(across[1], "dp", axis=0, tiled=True),
        lax.all_gather(across[2], "dp", axis=1, tiled=True),
        lax.all_gather(across[3], "dp", axis=1, tiled=True),
    )


def attention_scores(queries_b, keys_b, allowed):
    scores = jnp.einsum(
        "qhd,khd->hqk",
        split_heads(queries_b),
        split_heads(keys_b),
        preferred_element_type=jnp.float32,
    )
    return jnp.where(allowed[None], scores * HEAD ** (-0.5), masked_score)


def forward_pass(tokens_b, lengths, weights):
    qkv_b, out_b, ffn_b, vec_b = weights
    vec = vec_b.astype(jnp.float32)
    rows = tokens_b.shape[0]
    valid, allowed = segments(lengths, rows)
    projected = jnp.einsum("rd,kde->kre", tokens_b, qkv_b, preferred_element_type=jnp.float32)
    queries_b = (projected[0] + vec[0]).astype(jnp.bfloat16)
    keys_b = projected[1].astype(jnp.bfloat16)
    values_b = (projected[2] + vec[1]).astype(jnp.bfloat16)
    scores = attention_scores(queries_b, keys_b, allowed)
    largest = jnp.max(scores, axis=-1, keepdims=True)
    exponent = jnp.exp(scores - largest)
    totals = jnp.sum(exponent, axis=-1, keepdims=True)
    logsum = largest + jnp.log(totals)
    probs_b = (exponent / totals).astype(jnp.bfloat16)
    mixed = jnp.einsum(
        "hqk,khd->qhd", probs_b, split_heads(values_b), preferred_element_type=jnp.float32
    )
    mixed_b = mixed.reshape(rows, -1).astype(jnp.bfloat16)
    attended = jnp.dot(mixed_b, out_b, preferred_element_type=jnp.float32) + vec[2]
    first_in = tokens_b.astype(jnp.float32) + attended
    first = layer_norm(first_in, vec[3], vec[4])
    first_b = first.astype(jnp.bfloat16)
    inner = jnp.dot(first_b, ffn_b[0], preferred_element_type=jnp.float32) + vec[8:].reshape(-1)
    activ_b = gelu_exact(inner).astype(jnp.bfloat16)
    branch = jnp.einsum("rf,df->rd", activ_b, ffn_b[1], preferred_element_type=jnp.float32) + vec[5]
    second_in = first + branch
    result = layer_norm(second_in, vec[6], vec[7]) * valid[:, None].astype(jnp.float32)
    kept = (
        queries_b,
        keys_b,
        values_b,
        logsum,
        mixed_b,
        first_in,
        first_b,
        inner,
        activ_b,
        second_in,
    )
    return (result.astype(jnp.bfloat16), kept)


def backward_pass(cot_b, tokens_b, lengths, weights, kept):
    qkv_b, out_b, ffn_b, vec_b = weights
    vec = vec_b.astype(jnp.float32)
    queries_b, keys_b, values_b, logsum, mixed_b, first_in, first_b, inner, activ_b, second_in = (
        kept
    )
    rows = tokens_b.shape[0]
    valid, allowed = segments(lengths, rows)
    grad_out = cot_b.astype(jnp.float32) * valid[:, None].astype(jnp.float32)
    unused, pull_two = jax.vjp(layer_norm, second_in, vec[6], vec[7])
    d_second, d_gain_two, d_shift_two = pull_two(grad_out)
    d_branch_b = d_second.astype(jnp.bfloat16)
    d_bias_down = jnp.sum(d_branch_b.astype(jnp.float32), axis=0)
    d_activ = jnp.dot(d_branch_b, ffn_b[1], preferred_element_type=jnp.float32)
    unused, pull_gelu = jax.vjp(gelu_exact, inner)
    (d_inner,) = pull_gelu(d_activ)
    d_inner_b = d_inner.astype(jnp.bfloat16)
    d_bias_up = jnp.sum(d_inner_b.astype(jnp.float32), axis=0)
    d_first = d_second + jnp.einsum(
        "rf,df->rd", d_inner_b, ffn_b[0], preferred_element_type=jnp.float32
    )
    unused, pull_one = jax.vjp(layer_norm, first_in, vec[3], vec[4])
    d_first_in, d_gain_one, d_shift_one = pull_one(d_first)
    d_attended_b = d_first_in.astype(jnp.bfloat16)
    d_bias_out = jnp.sum(d_attended_b.astype(jnp.float32), axis=0)
    d_mixed_b = jnp.einsum(
        "re,de->rd", d_attended_b, out_b, preferred_element_type=jnp.float32
    ).astype(jnp.bfloat16)
    scores = attention_scores(queries_b, keys_b, allowed)
    probs = jnp.exp(scores - logsum)
    mixed_heads = split_heads(d_mixed_b)
    d_probs = jnp.einsum(
        "qhd,khd->hqk", mixed_heads, split_heads(values_b), preferred_element_type=jnp.float32
    )
    d_values = jnp.einsum(
        "hqk,qhd->khd", probs.astype(jnp.bfloat16), mixed_heads, preferred_element_type=jnp.float32
    )
    d_scores_b = (probs * (d_probs - jnp.sum(probs * d_probs, axis=-1, keepdims=True))).astype(
        jnp.bfloat16
    )
    d_queries = jnp.einsum(
        "hqk,khd->qhd", d_scores_b, split_heads(keys_b), preferred_element_type=jnp.float32
    ) * HEAD ** (-0.5)
    d_keys = jnp.einsum(
        "hqk,qhd->khd", d_scores_b, split_heads(queries_b), preferred_element_type=jnp.float32
    ) * HEAD ** (-0.5)
    d_proj_b = jnp.stack([d_queries, d_keys, d_values]).reshape(3, rows, -1).astype(jnp.bfloat16)
    d_tokens = d_first_in + jnp.einsum(
        "kre,kde->rd", d_proj_b, qkv_b, preferred_element_type=jnp.float32
    )
    proj_sums = jnp.sum(d_proj_b.astype(jnp.float32), axis=1)
    grad_vec = jnp.concatenate(
        [
            jnp.stack(
                [
                    proj_sums[0],
                    proj_sums[2],
                    d_bias_out,
                    d_gain_one,
                    d_shift_one,
                    d_bias_down,
                    d_gain_two,
                    d_shift_two,
                ]
            ),
            d_bias_up.reshape(-1, vec.shape[1]),
        ],
        axis=0,
    )
    factors = (d_branch_b, activ_b, first_b, d_inner_b, mixed_b, d_attended_b, d_proj_b)
    return (d_tokens, factors, grad_vec)


def orthogonalize_pair(square, wide):
    matrices = (square, wide)
    present = tuple((matrix.astype(jnp.bfloat16) for matrix in matrices))
    states = matrices
    for step in range(NS_STEPS):
        partial_value = tuple(
            (
                jnp.einsum("iw,jw->ij", block, block, preferred_element_type=jnp.float32)
                for block in present
            )
        )
        gram_part = (
            lax.psum_scatter(
                partial_value[0].astype(jnp.bfloat16), "shard", scatter_dimension=0, tiled=True
            ).astype(jnp.float32),
            lax.psum_scatter(
                partial_value[1].astype(jnp.bfloat16), "shard", scatter_dimension=0, tiled=True
            ).astype(jnp.float32),
        )
        grams = (
            lax.all_gather(gram_part[0].astype(jnp.bfloat16), "shard", axis=0, tiled=True).astype(
                jnp.float32
            ),
            lax.all_gather(gram_part[1].astype(jnp.bfloat16), "shard", axis=0, tiled=True).astype(
                jnp.float32
            ),
        )
        if step == 0:
            scales = tuple((jnp.sqrt(jnp.trace(gram)) + ortho_eps for gram in grams))
            grams = tuple((gram / (scale * scale) for gram, scale in zip(grams, scales)))
            present = tuple(
                ((matrix / scale).astype(jnp.bfloat16) for matrix, scale in zip(matrices, scales))
            )
        renewed = []
        for gram, current in zip(grams, present):
            gram_b = gram.astype(jnp.bfloat16)
            once = jnp.dot(gram_b, current, preferred_element_type=jnp.float32)
            twice = jnp.dot(gram_b, once.astype(jnp.bfloat16), preferred_element_type=jnp.float32)
            renewed.append(
                coef_first * current.astype(jnp.float32) + coef_second * once + coef_third * twice
            )
        states = tuple(renewed)
        present = tuple((state.astype(jnp.bfloat16) for state in states))
    return states


def per_device(
    tokens, cotangent, doc_lengths, qkv_w, out_w, ffn_w, vecs, qkv_mom, out_mom, ffn_mom, vec_mom
):
    micro = tokens.shape[0]
    shared = gather_weights(qkv_w, out_w, ffn_w, vecs)
    outputs = []
    stored = []
    for index in range(micro):
        weights = shared
        result_b, kept = forward_pass(tokens[index], doc_lengths[index], weights)
        outputs.append(result_b)
        stored.append(kept)
    grad_rows = [None] * micro
    factor_list = [None] * micro
    vec_total = None
    for index in reversed(range(micro)):
        weights = shared
        d_tokens, factors, vec_part = backward_pass(
            cotangent[index], tokens[index], doc_lengths[index], weights, stored[index]
        )
        grad_rows[index] = d_tokens
        factor_list[index] = factors
        vec_total = vec_part if vec_total is None else vec_total + vec_part
    (
        branch_gradient_rows,
        activation_rows,
        first_norm_rows,
        inner_gradient_rows,
        mixed_all,
        d_attended_all,
        d_proj_all,
    ) = [jnp.stack([factors[place] for factors in factor_list]) for place in range(7)]
    grad_down = jnp.einsum(
        "hzo,hzx->ox", branch_gradient_rows, activation_rows, preferred_element_type=jnp.float32
    )
    up_weight_gradient = jnp.einsum(
        "hzo,hzx->ox", first_norm_rows, inner_gradient_rows, preferred_element_type=jnp.float32
    )
    grad_wout_sum = jnp.einsum(
        "mrd,mre->de", mixed_all, d_attended_all, preferred_element_type=jnp.float32
    )
    grad_qkv_sum = jnp.einsum(
        "mrd,mkre->kde", tokens, d_proj_all, preferred_element_type=jnp.float32
    )
    summed = (grad_qkv_sum, grad_wout_sum, jnp.stack([up_weight_gradient, grad_down]), vec_total)
    reduced = (
        lax.psum_scatter(
            summed[0].astype(jnp.bfloat16), "dp", scatter_dimension=1, tiled=True
        ).astype(jnp.float32),
        lax.psum_scatter(
            summed[1].astype(jnp.bfloat16), "dp", scatter_dimension=0, tiled=True
        ).astype(jnp.float32),
        lax.psum_scatter(
            summed[2].astype(jnp.bfloat16), "dp", scatter_dimension=1, tiled=True
        ).astype(jnp.float32),
        lax.psum_scatter(
            summed[3].astype(jnp.bfloat16), "dp", scatter_dimension=1, tiled=True
        ).astype(jnp.float32),
    )
    grad_qkv, grad_wout, grad_ffn, grad_vec = (
        lax.psum_scatter(
            reduced[0].astype(jnp.bfloat16), "shard", scatter_dimension=2, tiled=True
        ).astype(jnp.float32),
        lax.psum_scatter(
            reduced[1].astype(jnp.bfloat16), "shard", scatter_dimension=1, tiled=True
        ).astype(jnp.float32),
        lax.psum_scatter(
            reduced[2].astype(jnp.bfloat16), "shard", scatter_dimension=2, tiled=True
        ).astype(jnp.float32),
        lax.psum_scatter(
            reduced[3].astype(jnp.bfloat16), "shard", scatter_dimension=1, tiled=True
        ).astype(jnp.float32),
    )
    new_qkv_mom = momentum_decay * qkv_mom + grad_qkv
    new_out_mom = momentum_decay * out_mom + grad_wout
    new_ffn_mom = momentum_decay * ffn_mom + grad_ffn
    square_local = jnp.concatenate([new_qkv_mom, new_out_mom[None]], axis=0)
    square_cols, wide_cols = (
        lax.all_gather(square_local.astype(jnp.bfloat16), "dp", axis=1, tiled=True).astype(
            square_local.dtype
        ),
        lax.all_gather(new_ffn_mom.astype(jnp.bfloat16), "dp", axis=1, tiled=True).astype(
            new_ffn_mom.dtype
        ),
    )
    row = lax.axis_index("dp")
    rows_count = lax.axis_size("dp")
    owners = [place * rows_count // 6 for place in range(6)]
    square_pick = sum(((row == owners[place]).astype(jnp.int32) * place for place in range(4)))
    wide_pick = (row == owners[5]).astype(jnp.int32)
    square_state, wide_state = orthogonalize_pair(
        lax.dynamic_index_in_dim(square_cols, square_pick, 0, keepdims=False),
        lax.dynamic_index_in_dim(wide_cols, wide_pick, 0, keepdims=False),
    )
    depth = qkv_w.shape[1]
    square_rows = []
    for place in range(4):
        whole = spread_2(square_state.astype(jnp.bfloat16), "dp", owners[place]).astype(
            square_state.dtype
        )
        square_rows.append(lax.dynamic_slice_in_dim(whole, row * depth, depth, 0))
    wide_rows = []
    for place in range(4, 6):
        whole = spread_2(wide_state.astype(jnp.bfloat16), "dp", owners[place]).astype(
            wide_state.dtype
        )
        wide_rows.append(lax.dynamic_slice_in_dim(whole, row * depth, depth, 0))
    qkv_new = qkv_w - muon_rate * jnp.stack(square_rows[:3])
    out_new = out_w - muon_rate * square_rows[3]
    ffn_new = ffn_w - muon_rate * (FF / D) ** 0.5 * jnp.stack(wide_rows)
    token_count = tokens.shape[0] * tokens.shape[1] * lax.axis_size("dp") * lax.axis_size("shard")
    new_vec_mom = momentum_decay * vec_mom + grad_vec
    vec_new = vecs - vec_rate * token_count ** (-0.5) * new_vec_mom
    return (
        jnp.stack(outputs),
        jnp.stack(grad_rows),
        grad_qkv,
        grad_wout,
        grad_ffn,
        grad_vec,
        new_qkv_mom,
        new_out_mom,
        new_ffn_mom,
        new_vec_mom,
        qkv_new,
        out_new,
        ffn_new,
        vec_new,
    )


def gather_direct(block, axis):
    count = lax.axis_size(axis)
    me = lax.axis_index(axis)
    whole = jnp.zeros((count,) + block.shape, block.dtype)
    whole = lax.dynamic_update_index_in_dim(whole, block, me, 0)
    for step in range(1, count):
        got = lax.ppermute(block, axis, [(i, (i + step) % count) for i in range(count)])
        whole = lax.dynamic_update_index_in_dim(whole, got, lax.rem(me - step + count, count), 0)
    return whole


def pieces_of(block, axis):
    count = lax.axis_size(axis)
    return [block] + [
        lax.ppermute(block, axis, [(i, (i + step) % count) for i in range(count)])
        for step in range(1, count)
    ]


def send_parts(parts, axis):
    count = lax.axis_size(axis)
    return [parts[0]] + [
        lax.ppermute(parts[step], axis, [(i, (i + step) % count) for i in range(count)])
        for step in range(1, count)
    ]


def swap(block, axis, bit):
    return lax.ppermute(block, axis, [(i, i ^ bit) for i in range(lax.axis_size(axis))])


def gather_double(block, axis):
    me = lax.axis_index(axis)
    bit = 1
    whole = block[None]
    while bit < lax.axis_size(axis):
        other = swap(whole, axis, bit)
        high = (me & bit) != 0
        whole = jnp.concatenate(
            [jnp.where(high, other, whole), jnp.where(high, whole, other)], axis=0
        )
        bit *= 2
    return whole


def dot(left, right, dims):
    return lax.dot_general(left, right, (dims, ((), ())), preferred_element_type=jnp.float32)


def norm_parts(inputs):
    center = inputs - jnp.mean(inputs, axis=-1, keepdims=True)
    spread = jnp.mean(center * center, axis=-1, keepdims=True)
    scale = lax.rsqrt(spread + norm_eps)
    return center * scale, scale


def norm_back(grad, unit, scale, gain):
    scaled = grad * gain
    mean_grad = jnp.mean(scaled, axis=-1, keepdims=True)
    mean_unit = jnp.mean(scaled * unit, axis=-1, keepdims=True)
    return scale * (scaled - mean_grad - unit * mean_unit)


BLOCK = 256
SPLIT = 4


def source_of(column, step):
    return lax.rem(column - step + SPLIT, SPLIT)


def put_pieces(pieces, column, whole):
    count = pieces[0].shape[0]
    for step, piece in enumerate(pieces):
        at = pl.multiple_of(source_of(column, step) * count, count)
        whole[pl.ds(at, count), :] = piece[...]


def take_parts(whole, column, parts):
    count = parts[0].shape[0]
    for step, part in enumerate(parts):
        at = pl.multiple_of(lax.rem(column + step, SPLIT) * count, count)
        part[...] = whole[pl.ds(at, count), :].astype(part.dtype)


def sum_pieces(pieces):
    total = pieces[0][...]
    for piece in pieces[1:]:
        total = total + piece[...].astype(jnp.float32)
    return total


def row_sums(values):
    return jnp.sum(values, axis=0, keepdims=True)


def layer_middle(place, *refs):
    pieces, refs = refs[:SPLIT], refs[SPLIT:]
    out_weight, tokens, vec, weights, bias_up, first_b, activ_b, slope, first_in, *refs = refs
    parts, (moving,) = refs[:SPLIT], refs[SPLIT:]
    column = place[0]
    own = pieces[0].shape[1]
    attended = vec[2:3, :] + tokens[...].astype(jnp.float32)
    for step, piece in enumerate(pieces):
        at = pl.multiple_of(source_of(column, step) * own, own)
        attended = attended + dot(piece[...], out_weight[pl.ds(at, own), :], ((1,), (0,)))
    moving[...] = attended
    take_parts(moving, column, [first_in])
    unit, scale = norm_parts(attended)
    first_b[...] = (unit * vec[3:4, :] + vec[4:5, :]).astype(jnp.bfloat16)
    hidden = slope.shape[1]
    inner = dot(first_b[...], weights[:, :hidden], ((1,), (0,))) + bias_up[...]
    cdf = 0.5 * (1.0 + lax.erf(inner * 2.0 ** (-0.5)))
    activ_b[...] = (inner * cdf).astype(jnp.bfloat16)
    slope[...] = cdf + inner * jnp.exp(-0.5 * inner * inner) * (2.0 * math.pi) ** (-0.5)
    moving[...] = dot(activ_b[...], weights[:, hidden : 2 * hidden], ((1,), (1,)))
    take_parts(moving, column, parts)


def second_norm(*refs):
    pieces, refs = refs[:SPLIT], refs[SPLIT:]
    first_in, vec, cotangent, valid, layer_out, d_branch, d_second, sums = refs
    unit, scale = norm_parts(first_in[...])
    first = unit * vec[3:4, :] + vec[4:5, :]
    unit, scale = norm_parts(first + (sum_pieces(pieces) + vec[5:6, :]))
    layer_out[...] = ((unit * vec[6:7, :] + vec[7:8, :]) * valid[...]).astype(jnp.bfloat16)
    grad = cotangent[...].astype(jnp.float32) * valid[...]
    d_rows = norm_back(grad, unit, scale, vec[6:7, :])
    d_second[...] = d_rows
    d_branch[...] = d_rows.astype(jnp.bfloat16)
    sums[0:1, :] = row_sums(d_branch[...].astype(jnp.float32))
    sums[1:2, :] = row_sums(grad * unit)
    sums[2:3, :] = row_sums(grad)


def inner_backward(place, *refs):
    pieces, refs = refs[:SPLIT], refs[SPLIT:]
    slope, weights, d_branch, d_inner, sums, *refs = refs
    parts, (moving,) = refs[:SPLIT], refs[SPLIT:]
    column = place[0]
    put_pieces(pieces, column, d_branch)
    hidden = slope.shape[1]
    d_activ = dot(d_branch[...], weights[:, hidden : 2 * hidden], ((1,), (0,)))
    d_inner[...] = (d_activ * slope[...]).astype(jnp.bfloat16)
    sums[...] = row_sums(d_inner[...].astype(jnp.float32))
    moving[...] = dot(d_inner[...], weights[:, :hidden], ((1,), (1,)))
    take_parts(moving, column, parts)


def inner_gradients(first_b, activ_b, d_inner, d_branch, grads):
    grads[0] = dot(first_b[...], d_inner[...], ((0,), (0,))).astype(jnp.bfloat16)
    grads[1] = dot(d_branch[...], activ_b[...], ((0,), (0,))).astype(jnp.bfloat16)


def wide_momenta(place, summed, moments, grads, moments_new, mine, far):
    low = place[0] < SPLIT // 2
    for part in range(2):
        grads[part] = summed[part].astype(jnp.float32)
        moments_new[part] = momentum_decay * moments[part] + grads[part]
    first, second = moments_new[0].astype(jnp.bfloat16), moments_new[1].astype(jnp.bfloat16)
    mine[...] = jnp.where(low, first, second)
    far[...] = jnp.where(low, second, first)


def wide_gram(rows, wide, gram):
    gram[...] = dot(rows[...], wide[...], ((1,), (1,))).astype(jnp.bfloat16)


def first_norm(*refs):
    pieces, refs = refs[:SPLIT], refs[SPLIT:]
    d_second, first_in, vec, d_first_in, d_attended, sums = refs
    unit, scale = norm_parts(first_in[...])
    grad = sum_pieces(pieces) + d_second[...]
    d_rows = norm_back(grad, unit, scale, vec[3:4, :])
    d_first_in[...] = d_rows
    d_attended[...] = d_rows.astype(jnp.bfloat16)
    sums[0:1, :] = row_sums(d_attended[...].astype(jnp.float32))
    sums[1:2, :] = row_sums(grad * unit)
    sums[2:3, :] = row_sums(grad)


def split_state(place, kept, other, *refs):
    blocks, (mine, far) = refs[:SPLIT], refs[SPLIT:]
    column, even = place[0], place[1] == 0
    own, hidden = blocks[0].shape[1], mine.shape[1]
    for step, block in enumerate(blocks):
        there = lax.rem(column + step, SPLIT)
        for at in range(SPLIT):
            lanes = slice(at * own, (at + 1) * own)

            @pl.when(there == at)
            def _():
                block[...] = jnp.where(even, kept[:, lanes], other[:, lanes])

    mine[...] = jnp.where(even, other[:, :hidden], kept[:, :hidden])
    far[...] = jnp.where(even, other[:, hidden:], kept[:, hidden:])


def new_weights(place, *refs):
    pieces, refs = refs[:SPLIT], refs[SPLIT:]
    mine, far, qkv_w, out_w, ffn_w, qkv_new, out_new, ffn_new, state = refs
    low = place[0] < SPLIT // 2
    for step, piece in enumerate(pieces):
        state[source_of(place[0], step)] = piece[...].astype(jnp.float32)
    for at in range(SPLIT - 1):
        qkv_new[at] = qkv_w[at] - muon_rate * state[at]
    out_new[...] = out_w[...] - muon_rate * state[SPLIT - 1]
    rate = muon_rate * (FF / D) ** 0.5
    ffn_new[0] = ffn_w[0] - rate * jnp.where(low, mine[...], far[...]).astype(jnp.float32)
    ffn_new[1] = ffn_w[1] - rate * jnp.where(low, far[...], mine[...]).astype(jnp.float32)


def probabilities(qkv, rows_at, head, own, id_column, id_row):
    queries = qkv[rows_at, head * HEAD : (head + 1) * HEAD]
    keys = qkv[rows_at, own + head * HEAD : own + (head + 1) * HEAD]
    values = qkv[rows_at, 2 * own + head * HEAD : 2 * own + (head + 1) * HEAD]
    scores = dot(queries, keys, ((1,), (1,))) * HEAD ** (-0.5)
    scores = jnp.where(id_column[rows_at, :] == id_row[:, rows_at], scores, masked_score)
    exponent = jnp.exp(scores - jnp.max(scores, axis=-1, keepdims=True))
    probs = exponent / jnp.sum(exponent, axis=-1, keepdims=True)
    return queries, keys, values, probs


def attention_forward(tokens, weight, bias, id_column, id_row, qkv, mixed):
    own = mixed.shape[1]
    proj = weight[:, weight.shape[1] - 3 * own :]
    qkv[...] = (dot(tokens[...], proj, ((1,), (0,))) + bias[...]).astype(jnp.bfloat16)
    for start in range(0, tokens.shape[0], BLOCK):
        rows_at = slice(start, start + BLOCK)
        for head in range(own // HEAD):
            queries, keys, values, probs = probabilities(qkv, rows_at, head, own, id_column, id_row)
            part = dot(probs.astype(jnp.bfloat16), values, ((1,), (0,)))
            mixed[rows_at, head * HEAD : (head + 1) * HEAD] = part.astype(jnp.bfloat16)


def attention_backward(
    place, *refs
):
    pieces, mixed, refs = refs[:SPLIT], refs[SPLIT : 2 * SPLIT], refs[2 * SPLIT :]
    out_weight, qkv, id_column, id_row, tokens, sums_one, sums_two, sums_up, *refs = refs
    kept, sent, d_proj, d_attended, sums = refs
    rows, width = tokens.shape
    own = qkv.shape[1] // 3
    column, core = place[0], place[1]
    put_pieces(pieces, column, d_attended)
    out_rows = out_weight[pl.ds(pl.multiple_of(column * own, own), own), :]
    d_mixed = dot(d_attended[...], out_rows, ((1,), (1,))).astype(jnp.bfloat16)
    for start in range(0, rows, BLOCK):
        rows_at = slice(start, start + BLOCK)
        for head in range(own // HEAD):
            queries, keys, values, probs = probabilities(qkv, rows_at, head, own, id_column, id_row)
            d_out = d_mixed[rows_at, head * HEAD : (head + 1) * HEAD]
            d_probs = dot(d_out, values, ((1,), (1,)))
            d_scores = probs * (d_probs - jnp.sum(probs * d_probs, axis=-1, keepdims=True))
            d_scores = d_scores.astype(jnp.bfloat16)
            d_values = dot(probs.astype(jnp.bfloat16), d_out, ((0,), (0,)))
            d_queries = dot(d_scores, keys, ((1,), (0,))) * HEAD ** (-0.5)
            d_keys = dot(d_scores, queries, ((0,), (0,))) * HEAD ** (-0.5)
            for part, value in enumerate((d_queries, d_keys, d_values)):
                at = part * own + head * HEAD
                d_proj[rows_at, at : at + HEAD] = value.astype(jnp.bfloat16)
    d_proj_all = d_proj[...]
    d_columns = d_attended[:, :own]
    for place_at in range(1, width // own):
        other = d_attended[:, place_at * own : (place_at + 1) * own]
        d_columns = jnp.where(column == place_at, other, d_columns)
    grad_proj = dot(tokens[...], d_proj_all, ((0,), (0,)))
    proj_sums = row_sums(d_proj_all.astype(jnp.float32))
    sums[...] = jnp.zeros_like(sums)
    for at in range(SPLIT):
        lanes = slice(at * own, (at + 1) * own)
        mine = (column == at).astype(jnp.float32)
        sums[0:1, lanes] = proj_sums[:, :own] * mine
        sums[1:2, lanes] = proj_sums[:, 2 * own :] * mine
        sums[8 + at : 9 + at, :] = sums_up[...] * mine
    sums[2:5, :] = sums_one[0:3, :]
    sums[5:8, :] = sums_two[0:3, :]
    depth = kept.shape[1] - sums.shape[0]
    for group in range(width // depth):
        at = slice(group * depth, (group + 1) * depth)

        def put(target, kind):
            target[group // 2, :depth, : 3 * own] = grad_proj[at].astype(kind)
            target[group // 2, depth:, :] = jnp.zeros((sums.shape[0], width), kind)
            target[group // 2, depth:, :depth] = sums[:, at].astype(kind)

        pl.when(core == group % 2)(lambda: put(kept, jnp.float32))
        pl.when(core != group % 2)(lambda: put(sent, jnp.bfloat16))
    for step, piece in enumerate(mixed):
        grad_out = dot(piece[...], d_columns, ((0,), (0,)))
        source = source_of(column, step)
        for half in range(2):
            block = grad_out[half * depth : (half + 1) * depth]

            def put_out(target, kind):
                target[source, :depth, 3 * own :] = block.astype(kind)

            pl.when(core == half)(lambda: put_out(kept, jnp.float32))
            pl.when(core != half)(lambda: put_out(sent, jnp.bfloat16))


def token_parts(place, d_proj, weight, *refs):
    parts, (moving,) = refs[:SPLIT], refs[SPLIT:]
    proj = weight[:, weight.shape[1] - d_proj.shape[1] :]
    moving[...] = dot(d_proj[...], proj, ((1,), (1,)))
    take_parts(moving, place[0], parts)


def pair_sum(place, kept, other, total, *blocks):
    chip = place[2]
    total[...] = kept[chip] + other[chip].astype(jnp.float32)
    for step, block in enumerate(blocks):
        at = chip ^ (step + 1)
        block[...] = (kept[at] + other[at].astype(jnp.float32)).astype(jnp.bfloat16)


def square_momenta(place, total, *refs):
    pieces, refs = refs[: SPLIT - 1], refs[SPLIT - 1 :]
    qkv_mom, out_mom, qkv_grad, out_grad, qkv_new, out_new, *refs = refs
    blocks, state = refs[:SPLIT], refs[SPLIT]
    depth, own = out_mom.shape
    whole = sum_pieces([total, *pieces])
    vec_own = depth // SPLIT
    for at in range(SPLIT):
        grad = whole[:depth, at * own : (at + 1) * own]
        if at < SPLIT - 1:
            qkv_grad[at] = grad
            moment = momentum_decay * qkv_mom[at] + grad
            qkv_new[at] = moment
        else:
            out_grad[...] = grad
            moment = momentum_decay * out_mom[...] + grad
            out_new[...] = moment
        state[at, :depth, :] = moment
        state[at, depth:, :] = jnp.zeros((whole.shape[0] - depth, own), jnp.float32)
        state[at, depth:, :vec_own] = whole[depth:, at * vec_own : (at + 1) * vec_own]
    for step, block in enumerate(blocks):
        block[...] = state[lax.rem(place[0] + step, SPLIT)].astype(jnp.bfloat16)


def join_squares(place, *refs):
    pieces, (gram, gram_other, mine, other, sums, rows) = refs[:SPLIT], refs[SPLIT:]
    depth, own = mine.shape[0], pieces[0].shape[1]
    total = jnp.zeros(sums.shape, jnp.float32)
    for step, piece in enumerate(pieces):
        total = total + piece[depth:, :].astype(jnp.float32)
        for at in range(SPLIT):

            @pl.when(source_of(place[0], step) == at)
            def _():
                rows[:, at * own : (at + 1) * own] = piece[:depth, :]

    sums[...] = total
    even = place[1] == 0
    gram_sum = (gram[...].astype(jnp.float32) + gram_other[...].astype(jnp.float32)).astype(jnp.bfloat16)
    mine[...] = jnp.where(even, rows[...], gram_sum)
    other[...] = jnp.where(even, gram_sum, rows[...])


def run_kernel(body, outputs, scalars=0, scratch=(), ties=()):
    def call(*operands):
        count = len(operands)

        def whole(*refs):
            body(*refs[:count], *refs[count + len(ties) :])

        spaces = [pltpu.SMEM] * scalars + [pltpu.VMEM] * (count - scalars) + [pl.ANY] * len(ties)
        return pl.pallas_call(
            whole,
            out_shape=outputs,
            in_specs=[pl.BlockSpec(memory_space=space) for space in spaces],
            out_specs=[pl.BlockSpec(memory_space=pltpu.VMEM)] * len(outputs),
            scratch_shapes=scratch,
            compiler_params=pltpu.CompilerParams(vmem_limit_bytes=16 * 2**20),
        )(*operands, *ties)

    return call


def newton_schulz(place, *refs):
    pieces, refs = refs[:SPLIT], refs[SPLIT:]
    wide, kept, sent, heard, gram, *factors = refs
    chip, core = place[2], place[1]
    width = heard.shape[0]
    for step, piece in enumerate(pieces):
        at = pl.multiple_of((chip ^ step) * piece.shape[0], piece.shape[0])
        heard[pl.ds(at, piece.shape[0]), :] = piece[...]
    depth = kept.shape[0]
    even = core == 0

    @pl.when(even)
    def _():
        gram[...] = dot(heard[...], heard[...], ((1,), (1,)))

    @pl.when(jnp.logical_not(even))
    def _():
        gram[...] = heard[...].astype(jnp.float32)

    at_row = lax.broadcasted_iota(jnp.int32, (width, width), 0)
    at_lane = lax.broadcasted_iota(jnp.int32, (width, width), 1)
    trace = jnp.sum(jnp.where(at_row == at_lane, gram[...], 0.0), keepdims=True)
    scale = jnp.sqrt(trace) + ortho_eps
    gram[...] = gram[...] / (scale * scale)
    for step, factor in enumerate(factors):
        gram_b = gram[...].astype(jnp.bfloat16)
        square = dot(gram_b, gram_b, ((1,), (0,)))
        factor[...] = (coef_second * gram[...] + coef_third * square).astype(jnp.bfloat16)
        if step < NS_STEPS - 1:
            moved = dot(factor[...], gram_b, ((1,), (0,)))
            twice = dot(factor[...], moved.astype(jnp.bfloat16), ((1,), (0,)))
            gram[...] = coef_first * coef_first * gram[...] + 2.0 * coef_first * moved + twice
    count = 2 * depth
    start = pl.multiple_of(chip * count, count)
    eye = lax.broadcasted_iota(jnp.int32, (count, width), 0) + start
    eye = (eye == lax.broadcasted_iota(jnp.int32, (count, width), 1)).astype(jnp.float32)
    rows = coef_first * eye + factors[-1][pl.ds(start, count), :].astype(jnp.float32)
    for factor in factors[-2::-1]:
        rows = coef_first * rows + dot(rows.astype(jnp.bfloat16), factor[...], ((1,), (0,)))
    rows = (rows / scale).astype(jnp.bfloat16)

    @pl.when(even)
    def _():
        state = dot(rows, heard[...], ((1,), (0,))).astype(jnp.bfloat16)
        kept[:, :width] = state[:depth]
        sent[:, :width] = state[depth:]
        kept[:, width:] = jnp.zeros_like(kept[:, width:])
        sent[:, width:] = jnp.zeros_like(sent[:, width:])

    @pl.when(jnp.logical_not(even))
    def _():
        state = dot(rows, wide[...], ((1,), (0,))).astype(jnp.bfloat16)
        kept[...] = state[depth:]
        sent[...] = state[:depth]


def split_device(
    tokens, cotangent, doc_lengths, qkv_w, out_w, ffn_w, vecs, qkv_mom, out_mom, ffn_mom, vec_mom
):
    micro, rows, width = tokens.shape
    shards = lax.axis_size("shard")
    groups = lax.axis_size("dp")
    column = lax.axis_index("shard")
    row = lax.axis_index("dp")
    slots = micro * shards
    own = qkv_w.shape[2]
    hidden = ffn_w.shape[2]
    bf16 = jnp.bfloat16

    packed = jnp.concatenate(
        [ffn_w[0], ffn_w[1], qkv_w[0], qkv_w[1], qkv_w[2]], axis=1
    ).astype(bf16)
    weights = lax.all_gather(packed, "dp", axis=0, tiled=True)

    flat = tokens.reshape(micro * rows, width)
    vec_rows, vec_own = vecs.shape
    small = jnp.concatenate(
        [vecs.astype(bf16).reshape(-1), doc_lengths.astype(bf16).reshape(-1)]
    )
    small = jnp.pad(small, (0, 8 * width - small.shape[0])).reshape(8, width)
    out_flat = out_w.astype(bf16).reshape(-1, width)
    out_count = out_flat.shape[0]
    heard = gather_direct(jnp.concatenate([flat, out_flat, small], axis=0), "shard")
    tokens_b = heard[:, : micro * rows].reshape(slots * rows, width)
    out_part = heard[:, micro * rows : micro * rows + out_count].reshape(shards, -1, own)
    out_part = out_part.transpose(1, 0, 2).reshape(-1, width)
    small = heard[:, micro * rows + out_count :].reshape(shards, -1)
    lengths = small[:, vecs.size : vecs.size + doc_lengths.size].astype(jnp.int32).reshape(slots, -1)
    small = small[:, : vecs.size].reshape(shards, vec_rows, vec_own).transpose(1, 0, 2).reshape(vec_rows, -1)
    vec = gather_double(small, "dp").transpose(1, 0, 2).reshape(vec_rows, -1).astype(jnp.float32)
    out_b = lax.all_gather(out_part, "dp", axis=0, tiled=True)
    position = jnp.arange(rows, dtype=jnp.int32)[None]
    ends = jnp.cumsum(lengths, axis=1)
    segment = jnp.sum((position[:, :, None] >= ends[:, None, :]).astype(jnp.int32), axis=2)
    valid = position < ends[:, -1:]
    slot = jnp.arange(slots, dtype=jnp.int32)[:, None]
    marks = jnp.where(valid, segment, ends.shape[1] + position) + slot * (ends.shape[1] + rows)
    id_column, id_row = marks.reshape(-1, 1), marks.reshape(1, -1)
    valid_own = lax.dynamic_slice_in_dim(valid, column * micro, micro, 0)
    valid_own = valid_own.reshape(-1, 1).astype(jnp.float32)
    bias_q = lax.dynamic_slice_in_dim(vec[0], column * own, own, 0)
    bias_v = lax.dynamic_slice_in_dim(vec[1], column * own, own, 0)
    bias_proj = jnp.concatenate([bias_q, jnp.zeros_like(bias_q), bias_v])[None]
    bias_up = lax.dynamic_slice_in_dim(vec[8:].reshape(-1), column * hidden, hidden, 0)

    qkv, mixed_own = run_kernel(
        attention_forward,
        [
            jax.ShapeDtypeStruct((slots * rows, 3 * own), bf16),
            jax.ShapeDtypeStruct((slots * rows, own), bf16),
        ],
    )(tokens_b, weights, bias_proj, id_column, id_row)

    depth = width // groups
    count = micro * rows
    whole_b = jax.ShapeDtypeStruct((slots * rows, width), bf16)
    own_f = jax.ShapeDtypeStruct((count, width), jnp.float32)
    own_b = jax.ShapeDtypeStruct((count, width), bf16)
    part_kinds = [own_f] + [own_b] * (shards - 1)
    sums_kind = jax.ShapeDtypeStruct((8, width), jnp.float32)
    moving = pltpu.VMEM((slots * rows, width), jnp.float32)
    place = jnp.stack([column, lax.rem(row, 2), row // 2]).astype(jnp.int32)

    mixed_pieces = pieces_of(mixed_own, "shard")
    first_b, activ_b, slope, first_in, *parts = run_kernel(
        layer_middle,
        [whole_b, whole_b, jax.ShapeDtypeStruct((slots * rows, hidden), jnp.float32), own_f] + part_kinds,
        scalars=1,
        scratch=[moving],
    )(place, *mixed_pieces, out_b, tokens_b, vec, weights, bias_up[None])
    layer_out, d_branch_own, d_second, sums_two = run_kernel(
        second_norm, [own_b, own_b, own_f, sums_kind]
    )(*send_parts(parts, "shard"), first_in, vec, cotangent.reshape(count, width), valid_own)
    layer_out = layer_out.reshape(tokens.shape)
    d_branch_b, d_inner_b, d_bias_up, *parts = run_kernel(
        inner_backward,
        [whole_b, whole_b, jax.ShapeDtypeStruct((1, hidden), jnp.float32)] + part_kinds,
        scalars=1,
        scratch=[moving],
    )(place, *pieces_of(d_branch_own, "shard"), slope, weights)
    (grads,) = run_kernel(inner_gradients, [jax.ShapeDtypeStruct((2, width, hidden), bf16)], ties=parts)(
        first_b, activ_b, d_inner_b, d_branch_b
    )
    summed = lax.psum_scatter(grads, "dp", scatter_dimension=1, tiled=True)
    d_first_in, d_attended_own, sums_one = run_kernel(
        first_norm, [own_f, own_b, sums_kind]
    )(*send_parts(parts, "shard"), d_second, first_in, vec)
    d_attended_pieces = pieces_of(d_attended_own, "shard")
    moment_kind = jax.ShapeDtypeStruct(ffn_mom.shape, ffn_mom.dtype)
    wide_kind = jax.ShapeDtypeStruct((depth, hidden), bf16)
    grad_ffn, new_ffn_mom, mine, far = run_kernel(
        wide_momenta,
        [moment_kind, moment_kind, wide_kind, wide_kind],
        scalars=1,
        ties=d_attended_pieces,
    )(place, summed, ffn_mom)
    even = lax.rem(row, 2) == 0
    far_rows = swap(far, "shard", shards // 2)
    wide_rows = jnp.concatenate([mine, far_rows], axis=1)
    wide = lax.all_gather(wide_rows, "dp", axis=0, tiled=True)

    packed_rows = depth + 16
    kept, sent, d_proj = run_kernel(
        attention_backward,
        [
            jax.ShapeDtypeStruct((groups // 2, packed_rows, width), jnp.float32),
            jax.ShapeDtypeStruct((groups // 2, packed_rows, width), bf16),
            jax.ShapeDtypeStruct((slots * rows, 3 * own), bf16),
        ],
        scalars=1,
        scratch=[pltpu.VMEM((slots * rows, width), bf16), pltpu.VMEM((16, width), jnp.float32)],
        ties=[far_rows],
    )(
        place, *d_attended_pieces, *mixed_pieces, out_b, qkv, id_column, id_row, tokens_b,
        sums_one, sums_two, d_bias_up,
    )
    block_kind = jax.ShapeDtypeStruct((packed_rows, width), bf16)
    total, *blocks = run_kernel(
        pair_sum, [jax.ShapeDtypeStruct((packed_rows, width), jnp.float32)] + [block_kind] * 3, scalars=1
    )(place, kept, swap(sent, "dp", 1))
    parts = run_kernel(token_parts, part_kinds, scalars=1, scratch=[moving], ties=[total])(
        place, d_proj, weights
    )
    d_tokens = d_first_in + sum(part.astype(jnp.float32) for part in send_parts(parts, "shard"))
    block_kind = jax.ShapeDtypeStruct((packed_rows, own), bf16)
    like = [jax.ShapeDtypeStruct(each.shape, each.dtype) for each in (qkv_mom, out_mom)]
    grad_qkv, grad_wout, new_qkv_mom, new_out_mom, *blocks = run_kernel(
        square_momenta,
        like + like + [block_kind] * shards,
        scalars=1,
        scratch=[pltpu.VMEM((shards, packed_rows, own), jnp.float32)],
    )(place, total, *[swap(block, "dp", 2 * at + 2) for at, block in enumerate(blocks)], qkv_mom, out_mom)
    (gram_rows,) = run_kernel(wide_gram, [jax.ShapeDtypeStruct((depth, width), bf16)], ties=blocks)(
        wide_rows, wide
    )
    row_kind = jax.ShapeDtypeStruct((depth, width), bf16)
    mine, other, grad_vec = run_kernel(
        join_squares,
        [row_kind, row_kind, jax.ShapeDtypeStruct((packed_rows - depth, own), jnp.float32)],
        scalars=1,
        scratch=[pltpu.VMEM((depth, width), bf16)],
        ties=[d_tokens],
    )(place, *send_parts(blocks, "shard"), gram_rows, swap(gram_rows, "shard", 1))
    grad_vec = grad_vec[:vec_rows, :vec_own]
    d_tokens = d_tokens.reshape(tokens.shape)
    other = swap(other, "dp", 1)
    pair_rows = jnp.concatenate([jnp.where(even, mine, other), jnp.where(even, other, mine)], axis=0)
    pair_pieces = [pair_rows] + [swap(pair_rows, "dp", bit) for bit in (2, 4, 6)]
    state_kind = jax.ShapeDtypeStruct((depth, 2 * hidden), bf16)
    kept, sent = run_kernel(
        newton_schulz,
        [state_kind, state_kind],
        scalars=1,
        scratch=[pltpu.VMEM((width, width), bf16), pltpu.VMEM((width, width), jnp.float32)]
        + [pltpu.VMEM((width, width), bf16)] * NS_STEPS,
    )(place, *pair_pieces, wide)
    block_kind = jax.ShapeDtypeStruct((depth, own), bf16)
    wide_kind = jax.ShapeDtypeStruct((depth, hidden), bf16)
    *blocks, mine, far = run_kernel(
        split_state, [block_kind] * shards + [wide_kind, wide_kind], scalars=1
    )(place, kept, swap(sent, "dp", 1))
    qkv_new, out_new, ffn_new = run_kernel(
        new_weights,
        [jax.ShapeDtypeStruct(each.shape, each.dtype) for each in (qkv_w, out_w, ffn_w)],
        scalars=1,
        scratch=[pltpu.VMEM((shards, depth, own), jnp.float32)],
    )(
        place, *send_parts(blocks, "shard"), mine, swap(far, "shard", shards // 2), qkv_w, out_w, ffn_w
    )

    token_count = micro * rows * groups * shards
    new_vec_mom = momentum_decay * vec_mom + grad_vec
    vec_new = vecs - vec_rate * token_count ** (-0.5) * new_vec_mom
    return (
        layer_out,
        d_tokens,
        grad_qkv,
        grad_wout,
        grad_ffn,
        grad_vec,
        new_qkv_mom,
        new_out_mom,
        new_ffn_mom,
        new_vec_mom,
        qkv_new,
        out_new,
        ffn_new,
        vec_new,
    )


def solution(mesh):
    fits = (mesh.shape["dp"], mesh.shape["shard"]) == (8, 4)
    in_specs = (
        P(("dp", "shard"), None, None),
        P(("dp", "shard"), None, None),
        P(("dp", "shard"), None),
        P(None, "dp", "shard"),
        P("dp", "shard"),
        P(None, "dp", "shard"),
        P(None, ("dp", "shard")),
        P(None, "dp", "shard"),
        P("dp", "shard"),
        P(None, "dp", "shard"),
        P(None, ("dp", "shard")),
    )
    out_specs = (
        P(("dp", "shard"), None, None),
        P(("dp", "shard"), None, None),
        P(None, "dp", "shard"),
        P("dp", "shard"),
        P(None, "dp", "shard"),
        P(None, ("dp", "shard")),
        P(None, "dp", "shard"),
        P("dp", "shard"),
        P(None, "dp", "shard"),
        P(None, ("dp", "shard")),
        P(None, "dp", "shard"),
        P("dp", "shard"),
        P(None, "dp", "shard"),
        P(None, ("dp", "shard")),
    )
    return jax.shard_map(
        split_device if fits else per_device, mesh=mesh, in_specs=in_specs, out_specs=out_specs, check_vma=False
    )
```

```python
import math
import jax
import jax.numpy as jnp
from jax import lax
from jax.experimental import pallas as pl
from jax.experimental.pallas import tpu as pltpu
from jax.sharding import PartitionSpec as P

D = 768
HEADS = 12
HEAD = 64
FF = 3072
NS_STEPS = 3


masked_score = -1e30
norm_eps = 1e-12
momentum_decay = 0.9
muon_rate = 0.8
vec_rate = 0.5
coef_first = 3.4445
coef_second = -4.775
coef_third = 2.0315
ortho_eps = 1e-07


def spread_2(block, axis, owner):
    block = jnp.where(lax.axis_index(axis) == owner, block, jnp.zeros_like(block))
    return lax.psum(block, axis)


def segments(lengths, rows):
    position = jnp.arange(rows, dtype=jnp.int32)
    ends = jnp.cumsum(lengths)
    segment = jnp.sum((position[:, None] >= ends[None, :]).astype(jnp.int32), axis=1)
    valid = position < ends[-1]
    same = segment[:, None] == segment[None, :]
    allowed = same & valid[:, None] | (position[:, None] == position[None, :])
    return (valid, allowed)


def layer_norm(inputs, gain, bias):
    center = inputs - jnp.mean(inputs, axis=-1, keepdims=True)
    spread = jnp.mean(center * center, axis=-1, keepdims=True)
    return center * lax.rsqrt(spread + norm_eps) * gain + bias


def gelu_exact(inputs):
    return jax.nn.gelu(inputs, approximate=False)


def split_heads(matrix):
    return matrix.reshape(matrix.shape[0], HEADS, HEAD)


def gather_weights(qkv_w, out_w, ffn_w, vecs):
    pieces = (
        qkv_w.astype(jnp.bfloat16),
        out_w.astype(jnp.bfloat16),
        ffn_w.astype(jnp.bfloat16),
        vecs.astype(jnp.bfloat16),
    )
    across = (
        lax.all_gather(pieces[0], "shard", axis=2, tiled=True),
        lax.all_gather(pieces[1], "shard", axis=1, tiled=True),
        lax.all_gather(pieces[2], "shard", axis=2, tiled=True),
        lax.all_gather(pieces[3], "shard", axis=1, tiled=True),
    )
    return (
        lax.all_gather(across[0], "dp", axis=1, tiled=True),
        lax.all_gather(across[1], "dp", axis=0, tiled=True),
        lax.all_gather(across[2], "dp", axis=1, tiled=True),
        lax.all_gather(across[3], "dp", axis=1, tiled=True),
    )


def attention_scores(queries_b, keys_b, allowed):
    scores = jnp.einsum(
        "qhd,khd->hqk",
        split_heads(queries_b),
        split_heads(keys_b),
        preferred_element_type=jnp.float32,
    )
    return jnp.where(allowed[None], scores * HEAD ** (-0.5), masked_score)


def forward_pass(tokens_b, lengths, weights):
    qkv_b, out_b, ffn_b, vec_b = weights
    vec = vec_b.astype(jnp.float32)
    rows = tokens_b.shape[0]
    valid, allowed = segments(lengths, rows)
    projected = jnp.einsum("rd,kde->kre", tokens_b, qkv_b, preferred_element_type=jnp.float32)
    queries_b = (projected[0] + vec[0]).astype(jnp.bfloat16)
    keys_b = projected[1].astype(jnp.bfloat16)
    values_b = (projected[2] + vec[1]).astype(jnp.bfloat16)
    scores = attention_scores(queries_b, keys_b, allowed)
    largest = jnp.max(scores, axis=-1, keepdims=True)
    exponent = jnp.exp(scores - largest)
    totals = jnp.sum(exponent, axis=-1, keepdims=True)
    logsum = largest + jnp.log(totals)
    probs_b = (exponent / totals).astype(jnp.bfloat16)
    mixed = jnp.einsum(
        "hqk,khd->qhd", probs_b, split_heads(values_b), preferred_element_type=jnp.float32
    )
    mixed_b = mixed.reshape(rows, -1).astype(jnp.bfloat16)
    attended = jnp.dot(mixed_b, out_b, preferred_element_type=jnp.float32) + vec[2]
    first_in = tokens_b.astype(jnp.float32) + attended
    first = layer_norm(first_in, vec[3], vec[4])
    first_b = first.astype(jnp.bfloat16)
    inner = jnp.dot(first_b, ffn_b[0], preferred_element_type=jnp.float32) + vec[8:].reshape(-1)
    activ_b = gelu_exact(inner).astype(jnp.bfloat16)
    branch = jnp.einsum("rf,df->rd", activ_b, ffn_b[1], preferred_element_type=jnp.float32) + vec[5]
    second_in = first + branch
    result = layer_norm(second_in, vec[6], vec[7]) * valid[:, None].astype(jnp.float32)
    kept = (
        queries_b,
        keys_b,
        values_b,
        logsum,
        mixed_b,
        first_in,
        first_b,
        inner,
        activ_b,
        second_in,
    )
    return (result.astype(jnp.bfloat16), kept)


def backward_pass(cot_b, tokens_b, lengths, weights, kept):
    qkv_b, out_b, ffn_b, vec_b = weights
    vec = vec_b.astype(jnp.float32)
    queries_b, keys_b, values_b, logsum, mixed_b, first_in, first_b, inner, activ_b, second_in = (
        kept
    )
    rows = tokens_b.shape[0]
    valid, allowed = segments(lengths, rows)
    grad_out = cot_b.astype(jnp.float32) * valid[:, None].astype(jnp.float32)
    unused, pull_two = jax.vjp(layer_norm, second_in, vec[6], vec[7])
    d_second, d_gain_two, d_shift_two = pull_two(grad_out)
    d_branch_b = d_second.astype(jnp.bfloat16)
    d_bias_down = jnp.sum(d_branch_b.astype(jnp.float32), axis=0)
    d_activ = jnp.dot(d_branch_b, ffn_b[1], preferred_element_type=jnp.float32)
    unused, pull_gelu = jax.vjp(gelu_exact, inner)
    (d_inner,) = pull_gelu(d_activ)
    d_inner_b = d_inner.astype(jnp.bfloat16)
    d_bias_up = jnp.sum(d_inner_b.astype(jnp.float32), axis=0)
    d_first = d_second + jnp.einsum(
        "rf,df->rd", d_inner_b, ffn_b[0], preferred_element_type=jnp.float32
    )
    unused, pull_one = jax.vjp(layer_norm, first_in, vec[3], vec[4])
    d_first_in, d_gain_one, d_shift_one = pull_one(d_first)
    d_attended_b = d_first_in.astype(jnp.bfloat16)
    d_bias_out = jnp.sum(d_attended_b.astype(jnp.float32), axis=0)
    d_mixed_b = jnp.einsum(
        "re,de->rd", d_attended_b, out_b, preferred_element_type=jnp.float32
    ).astype(jnp.bfloat16)
    scores = attention_scores(queries_b, keys_b, allowed)
    probs = jnp.exp(scores - logsum)
    mixed_heads = split_heads(d_mixed_b)
    d_probs = jnp.einsum(
        "qhd,khd->hqk", mixed_heads, split_heads(values_b), preferred_element_type=jnp.float32
    )
    d_values = jnp.einsum(
        "hqk,qhd->khd", probs.astype(jnp.bfloat16), mixed_heads, preferred_element_type=jnp.float32
    )
    d_scores_b = (probs * (d_probs - jnp.sum(probs * d_probs, axis=-1, keepdims=True))).astype(
        jnp.bfloat16
    )
    d_queries = jnp.einsum(
        "hqk,khd->qhd", d_scores_b, split_heads(keys_b), preferred_element_type=jnp.float32
    ) * HEAD ** (-0.5)
    d_keys = jnp.einsum(
        "hqk,qhd->khd", d_scores_b, split_heads(queries_b), preferred_element_type=jnp.float32
    ) * HEAD ** (-0.5)
    d_proj_b = jnp.stack([d_queries, d_keys, d_values]).reshape(3, rows, -1).astype(jnp.bfloat16)
    d_tokens = d_first_in + jnp.einsum(
        "kre,kde->rd", d_proj_b, qkv_b, preferred_element_type=jnp.float32
    )
    proj_sums = jnp.sum(d_proj_b.astype(jnp.float32), axis=1)
    grad_vec = jnp.concatenate(
        [
            jnp.stack(
                [
                    proj_sums[0],
                    proj_sums[2],
                    d_bias_out,
                    d_gain_one,
                    d_shift_one,
                    d_bias_down,
                    d_gain_two,
                    d_shift_two,
                ]
            ),
            d_bias_up.reshape(-1, vec.shape[1]),
        ],
        axis=0,
    )
    factors = (d_branch_b, activ_b, first_b, d_inner_b, mixed_b, d_attended_b, d_proj_b)
    return (d_tokens, factors, grad_vec)


def orthogonalize_pair(square, wide):
    matrices = (square, wide)
    present = tuple((matrix.astype(jnp.bfloat16) for matrix in matrices))
    states = matrices
    for step in range(NS_STEPS):
        partial_value = tuple(
            (
                jnp.einsum("iw,jw->ij", block, block, preferred_element_type=jnp.float32)
                for block in present
            )
        )
        gram_part = (
            lax.psum_scatter(
                partial_value[0].astype(jnp.bfloat16), "shard", scatter_dimension=0, tiled=True
            ).astype(jnp.float32),
            lax.psum_scatter(
                partial_value[1].astype(jnp.bfloat16), "shard", scatter_dimension=0, tiled=True
            ).astype(jnp.float32),
        )
        grams = (
            lax.all_gather(gram_part[0].astype(jnp.bfloat16), "shard", axis=0, tiled=True).astype(
                jnp.float32
            ),
            lax.all_gather(gram_part[1].astype(jnp.bfloat16), "shard", axis=0, tiled=True).astype(
                jnp.float32
            ),
        )
        if step == 0:
            scales = tuple((jnp.sqrt(jnp.trace(gram)) + ortho_eps for gram in grams))
            grams = tuple((gram / (scale * scale) for gram, scale in zip(grams, scales)))
            present = tuple(
                ((matrix / scale).astype(jnp.bfloat16) for matrix, scale in zip(matrices, scales))
            )
        renewed = []
        for gram, current in zip(grams, present):
            gram_b = gram.astype(jnp.bfloat16)
            once = jnp.dot(gram_b, current, preferred_element_type=jnp.float32)
            twice = jnp.dot(gram_b, once.astype(jnp.bfloat16), preferred_element_type=jnp.float32)
            renewed.append(
                coef_first * current.astype(jnp.float32) + coef_second * once + coef_third * twice
            )
        states = tuple(renewed)
        present = tuple((state.astype(jnp.bfloat16) for state in states))
    return states


def per_device(
    tokens, cotangent, doc_lengths, qkv_w, out_w, ffn_w, vecs, qkv_mom, out_mom, ffn_mom, vec_mom
):
    micro = tokens.shape[0]
    shared = gather_weights(qkv_w, out_w, ffn_w, vecs)
    outputs = []
    stored = []
    for index in range(micro):
        weights = shared
        result_b, kept = forward_pass(tokens[index], doc_lengths[index], weights)
        outputs.append(result_b)
        stored.append(kept)
    grad_rows = [None] * micro
    factor_list = [None] * micro
    vec_total = None
    for index in reversed(range(micro)):
        weights = shared
        d_tokens, factors, vec_part = backward_pass(
            cotangent[index], tokens[index], doc_lengths[index], weights, stored[index]
        )
        grad_rows[index] = d_tokens
        factor_list[index] = factors
        vec_total = vec_part if vec_total is None else vec_total + vec_part
    (
        branch_gradient_rows,
        activation_rows,
        first_norm_rows,
        inner_gradient_rows,
        mixed_all,
        d_attended_all,
        d_proj_all,
    ) = [jnp.stack([factors[place] for factors in factor_list]) for place in range(7)]
    grad_down = jnp.einsum(
        "hzo,hzx->ox", branch_gradient_rows, activation_rows, preferred_element_type=jnp.float32
    )
    up_weight_gradient = jnp.einsum(
        "hzo,hzx->ox", first_norm_rows, inner_gradient_rows, preferred_element_type=jnp.float32
    )
    grad_wout_sum = jnp.einsum(
        "mrd,mre->de", mixed_all, d_attended_all, preferred_element_type=jnp.float32
    )
    grad_qkv_sum = jnp.einsum(
        "mrd,mkre->kde", tokens, d_proj_all, preferred_element_type=jnp.float32
    )
    summed = (grad_qkv_sum, grad_wout_sum, jnp.stack([up_weight_gradient, grad_down]), vec_total)
    reduced = (
        lax.psum_scatter(
            summed[0].astype(jnp.bfloat16), "dp", scatter_dimension=1, tiled=True
        ).astype(jnp.float32),
        lax.psum_scatter(
            summed[1].astype(jnp.bfloat16), "dp", scatter_dimension=0, tiled=True
        ).astype(jnp.float32),
        lax.psum_scatter(
            summed[2].astype(jnp.bfloat16), "dp", scatter_dimension=1, tiled=True
        ).astype(jnp.float32),
        lax.psum_scatter(
            summed[3].astype(jnp.bfloat16), "dp", scatter_dimension=1, tiled=True
        ).astype(jnp.float32),
    )
    grad_qkv, grad_wout, grad_ffn, grad_vec = (
        lax.psum_scatter(
            reduced[0].astype(jnp.bfloat16), "shard", scatter_dimension=2, tiled=True
        ).astype(jnp.float32),
        lax.psum_scatter(
            reduced[1].astype(jnp.bfloat16), "shard", scatter_dimension=1, tiled=True
        ).astype(jnp.float32),
        lax.psum_scatter(
            reduced[2].astype(jnp.bfloat16), "shard", scatter_dimension=2, tiled=True
        ).astype(jnp.float32),
        lax.psum_scatter(
            reduced[3].astype(jnp.bfloat16), "shard", scatter_dimension=1, tiled=True
        ).astype(jnp.float32),
    )
    new_qkv_mom = momentum_decay * qkv_mom + grad_qkv
    new_out_mom = momentum_decay * out_mom + grad_wout
    new_ffn_mom = momentum_decay * ffn_mom + grad_ffn
    square_local = jnp.concatenate([new_qkv_mom, new_out_mom[None]], axis=0)
    square_cols, wide_cols = (
        lax.all_gather(square_local.astype(jnp.bfloat16), "dp", axis=1, tiled=True).astype(
            square_local.dtype
        ),
        lax.all_gather(new_ffn_mom.astype(jnp.bfloat16), "dp", axis=1, tiled=True).astype(
            new_ffn_mom.dtype
        ),
    )
    row = lax.axis_index("dp")
    rows_count = lax.axis_size("dp")
    owners = [place * rows_count // 6 for place in range(6)]
    square_pick = sum(((row == owners[place]).astype(jnp.int32) * place for place in range(4)))
    wide_pick = (row == owners[5]).astype(jnp.int32)
    square_state, wide_state = orthogonalize_pair(
        lax.dynamic_index_in_dim(square_cols, square_pick, 0, keepdims=False),
        lax.dynamic_index_in_dim(wide_cols, wide_pick, 0, keepdims=False),
    )
    depth = qkv_w.shape[1]
    square_rows = []
    for place in range(4):
        whole = spread_2(square_state.astype(jnp.bfloat16), "dp", owners[place]).astype(
            square_state.dtype
        )
        square_rows.append(lax.dynamic_slice_in_dim(whole, row * depth, depth, 0))
    wide_rows = []
    for place in range(4, 6):
        whole = spread_2(wide_state.astype(jnp.bfloat16), "dp", owners[place]).astype(
            wide_state.dtype
        )
        wide_rows.append(lax.dynamic_slice_in_dim(whole, row * depth, depth, 0))
    qkv_new = qkv_w - muon_rate * jnp.stack(square_rows[:3])
    out_new = out_w - muon_rate * square_rows[3]
    ffn_new = ffn_w - muon_rate * (FF / D) ** 0.5 * jnp.stack(wide_rows)
    token_count = tokens.shape[0] * tokens.shape[1] * lax.axis_size("dp") * lax.axis_size("shard")
    new_vec_mom = momentum_decay * vec_mom + grad_vec
    vec_new = vecs - vec_rate * token_count ** (-0.5) * new_vec_mom
    return (
        jnp.stack(outputs),
        jnp.stack(grad_rows),
        grad_qkv,
        grad_wout,
        grad_ffn,
        grad_vec,
        new_qkv_mom,
        new_out_mom,
        new_ffn_mom,
        new_vec_mom,
        qkv_new,
        out_new,
        ffn_new,
        vec_new,
    )


def gather_direct(block, axis):
    count = lax.axis_size(axis)
    me = lax.axis_index(axis)
    whole = jnp.zeros((count,) + block.shape, block.dtype)
    whole = lax.dynamic_update_index_in_dim(whole, block, me, 0)
    for step in range(1, count):
        got = lax.ppermute(block, axis, [(i, (i + step) % count) for i in range(count)])
        whole = lax.dynamic_update_index_in_dim(whole, got, lax.rem(me - step + count, count), 0)
    return whole


def pieces_of(block, axis):
    count = lax.axis_size(axis)
    return [block] + [
        lax.ppermute(block, axis, [(i, (i + step) % count) for i in range(count)])
        for step in range(1, count)
    ]


def send_parts(parts, axis):
    count = lax.axis_size(axis)
    return [parts[0]] + [
        lax.ppermute(parts[step], axis, [(i, (i + step) % count) for i in range(count)])
        for step in range(1, count)
    ]


def swap(block, axis, bit):
    return lax.ppermute(block, axis, [(i, i ^ bit) for i in range(lax.axis_size(axis))])


def gather_double(block, axis):
    me = lax.axis_index(axis)
    bit = 1
    whole = block[None]
    while bit < lax.axis_size(axis):
        other = swap(whole, axis, bit)
        high = (me & bit) != 0
        whole = jnp.concatenate(
            [jnp.where(high, other, whole), jnp.where(high, whole, other)], axis=0
        )
        bit *= 2
    return whole


def dot(left, right, dims):
    return lax.dot_general(left, right, (dims, ((), ())), preferred_element_type=jnp.float32)


def norm_parts(inputs):
    center = inputs - jnp.mean(inputs, axis=-1, keepdims=True)
    spread = jnp.mean(center * center, axis=-1, keepdims=True)
    scale = lax.rsqrt(spread + norm_eps)
    return center * scale, scale


def norm_back(grad, unit, scale, gain):
    scaled = grad * gain
    mean_grad = jnp.mean(scaled, axis=-1, keepdims=True)
    mean_unit = jnp.mean(scaled * unit, axis=-1, keepdims=True)
    return scale * (scaled - mean_grad - unit * mean_unit)


BLOCK = 256
SPLIT = 4


def source_of(column, step):
    return lax.rem(column - step + SPLIT, SPLIT)


def put_pieces(pieces, column, whole):
    count = pieces[0].shape[0]
    for step, piece in enumerate(pieces):
        at = pl.multiple_of(source_of(column, step) * count, count)
        whole[pl.ds(at, count), :] = piece[...]


def take_parts(whole, column, parts):
    count = parts[0].shape[0]
    for step, part in enumerate(parts):
        at = pl.multiple_of(lax.rem(column + step, SPLIT) * count, count)
        part[...] = whole[pl.ds(at, count), :].astype(part.dtype)


def sum_pieces(pieces):
    total = pieces[0][...]
    for piece in pieces[1:]:
        total = total + piece[...].astype(jnp.float32)
    return total


def row_sums(values):
    return jnp.sum(values, axis=0, keepdims=True)


def unpack_rows(piece, rows):
    count = rows // piece.shape[0]
    own = piece.shape[1] // count
    return jnp.concatenate([piece[:, at * own : (at + 1) * own] for at in range(count)], axis=0)


def layer_middle(place, *refs):
    pieces, refs = refs[:SPLIT], refs[SPLIT:]
    out_weight, tokens, vec, weights, bias_up, first_b, activ_b, slope, first_in, *refs = refs
    parts, (moving,) = refs[:SPLIT], refs[SPLIT:]
    column = place[0]
    attended = vec[2:3, :] + tokens[...].astype(jnp.float32)
    for step, piece in enumerate(pieces):
        rows = unpack_rows(piece, tokens.shape[0])
        own = rows.shape[1]
        at = pl.multiple_of(source_of(column, step) * own, own)
        attended = attended + dot(rows, out_weight[pl.ds(at, own), :], ((1,), (0,)))
    moving[...] = attended
    take_parts(moving, column, [first_in])
    unit, scale = norm_parts(attended)
    first_b[...] = (unit * vec[3:4, :] + vec[4:5, :]).astype(jnp.bfloat16)
    hidden = slope.shape[1]
    inner = dot(first_b[...], weights[:, :hidden], ((1,), (0,))) + bias_up[...]
    cdf = 0.5 * (1.0 + lax.erf(inner * 2.0 ** (-0.5)))
    activ_b[...] = (inner * cdf).astype(jnp.bfloat16)
    slope[...] = cdf + inner * jnp.exp(-0.5 * inner * inner) * (2.0 * math.pi) ** (-0.5)
    moving[...] = dot(activ_b[...], weights[:, hidden : 2 * hidden], ((1,), (1,)))
    take_parts(moving, column, parts)


def second_norm(place, *refs):
    pieces, refs = refs[:SPLIT], refs[SPLIT:]
    first_in, vec, cotangent, ids, layer_out, d_branch, d_second, sums = refs
    count = first_in.shape[0]
    at = pl.multiple_of(place[0] * count, count)
    valid = (ids[pl.ds(at, count), :] >= 0).astype(jnp.float32)
    unit, scale = norm_parts(first_in[...])
    first = unit * vec[3:4, :] + vec[4:5, :]
    unit, scale = norm_parts(first + (sum_pieces(pieces) + vec[5:6, :]))
    layer_out[...] = ((unit * vec[6:7, :] + vec[7:8, :]) * valid).astype(jnp.bfloat16)
    grad = cotangent[...].astype(jnp.float32) * valid
    d_rows = norm_back(grad, unit, scale, vec[6:7, :])
    d_second[...] = d_rows
    d_branch[...] = d_rows.astype(jnp.bfloat16)
    sums[0:1, :] = row_sums(d_branch[...].astype(jnp.float32))
    sums[1:2, :] = row_sums(grad * unit)
    sums[2:3, :] = row_sums(grad)


def inner_backward(place, *refs):
    pieces, refs = refs[:SPLIT], refs[SPLIT:]
    slope, weights, d_branch, d_inner, sums, *refs = refs
    parts, (moving,) = refs[:SPLIT], refs[SPLIT:]
    column = place[0]
    put_pieces(pieces, column, d_branch)
    hidden = slope.shape[1]
    d_activ = dot(d_branch[...], weights[:, hidden : 2 * hidden], ((1,), (0,)))
    d_inner[...] = (d_activ * slope[...]).astype(jnp.bfloat16)
    sums[...] = row_sums(d_inner[...].astype(jnp.float32))
    moving[...] = dot(d_inner[...], weights[:, :hidden], ((1,), (1,)))
    take_parts(moving, column, parts)


def inner_gradients(first_b, activ_b, d_inner, d_branch, grads):
    grads[0] = dot(first_b[...], d_inner[...], ((0,), (0,))).astype(jnp.bfloat16)
    grads[1] = dot(d_branch[...], activ_b[...], ((0,), (0,))).astype(jnp.bfloat16)


def wide_momenta(place, summed, moments, grads, moments_new, mine, far):
    low = place[0] < SPLIT // 2
    for part in range(2):
        grads[part] = summed[part].astype(jnp.float32)
        moments_new[part] = momentum_decay * moments[part] + grads[part]
    first, second = moments_new[0].astype(jnp.bfloat16), moments_new[1].astype(jnp.bfloat16)
    mine[...] = jnp.where(low, first, second)
    far[...] = jnp.where(low, second, first)


def wide_gram(rows, wide, gram):
    gram[...] = dot(rows[...], wide[...], ((1,), (1,))).astype(jnp.bfloat16)


def first_norm(*refs):
    pieces, refs = refs[:SPLIT], refs[SPLIT:]
    d_second, first_in, vec, d_first_in, d_attended, sums = refs
    unit, scale = norm_parts(first_in[...])
    grad = sum_pieces(pieces) + d_second[...]
    d_rows = norm_back(grad, unit, scale, vec[3:4, :])
    d_first_in[...] = d_rows
    d_attended[...] = d_rows.astype(jnp.bfloat16)
    sums[0:1, :] = row_sums(d_attended[...].astype(jnp.float32))
    sums[1:2, :] = row_sums(grad * unit)
    sums[2:3, :] = row_sums(grad)


def split_state(place, kept, other, *refs):
    blocks, (mine, far) = refs[:SPLIT], refs[SPLIT:]
    column, even = place[0], place[1] == 0
    own, hidden = blocks[0].shape[1], mine.shape[1]
    for step, block in enumerate(blocks):
        there = lax.rem(column + step, SPLIT)
        for at in range(SPLIT):
            lanes = slice(at * own, (at + 1) * own)

            @pl.when(there == at)
            def _():
                block[...] = jnp.where(even, kept[:, lanes], other[:, lanes])

    mine[...] = jnp.where(even, other[:, :hidden], kept[:, :hidden])
    far[...] = jnp.where(even, other[:, hidden:], kept[:, hidden:])


def new_weights(place, *refs):
    pieces, refs = refs[:SPLIT], refs[SPLIT:]
    mine, far, qkv_w, out_w, ffn_w, qkv_new, out_new, ffn_new, state = refs
    low = place[0] < SPLIT // 2
    for step, piece in enumerate(pieces):
        state[source_of(place[0], step)] = piece[...].astype(jnp.float32)
    for at in range(SPLIT - 1):
        qkv_new[at] = qkv_w[at] - muon_rate * state[at]
    out_new[...] = out_w[...] - muon_rate * state[SPLIT - 1]
    rate = muon_rate * (FF / D) ** 0.5
    ffn_new[0] = ffn_w[0] - rate * jnp.where(low, mine[...], far[...]).astype(jnp.float32)
    ffn_new[1] = ffn_w[1] - rate * jnp.where(low, far[...], mine[...]).astype(jnp.float32)


def probabilities(qkv, rows_at, head, own, id_column, id_row):
    queries = qkv[rows_at, head * HEAD : (head + 1) * HEAD]
    keys = qkv[rows_at, own + head * HEAD : own + (head + 1) * HEAD]
    values = qkv[rows_at, 2 * own + head * HEAD : 2 * own + (head + 1) * HEAD]
    scores = dot(queries, keys, ((1,), (1,))) * HEAD ** (-0.5)
    scores = jnp.where(id_column[rows_at, :] == id_row[:, rows_at], scores, masked_score)
    exponent = jnp.exp(scores - jnp.max(scores, axis=-1, keepdims=True))
    probs = exponent / jnp.sum(exponent, axis=-1, keepdims=True)
    return queries, keys, values, probs


def attention_forward(place, tokens, weight, bias, id_column, id_row, qkv, mixed):
    own = qkv.shape[1] // 3
    proj = weight[:, weight.shape[1] - 3 * own :]
    qkv[...] = (dot(tokens[...], proj, ((1,), (0,))) + bias[...]).astype(jnp.bfloat16)
    for start in range(0, tokens.shape[0], BLOCK):
        rows_at = slice(start, start + BLOCK)
        for head in range(own // HEAD):
            queries, keys, values, probs = probabilities(qkv, rows_at, head, own, id_column, id_row)
            part = dot(probs.astype(jnp.bfloat16), values, ((1,), (0,)))
            at = start // BLOCK * own + head * HEAD
            mixed[:, at : at + HEAD] = part.astype(jnp.bfloat16)


def attention_backward(
    place, *refs
):
    pieces, mixed, refs = refs[:SPLIT], refs[SPLIT : 2 * SPLIT], refs[2 * SPLIT :]
    out_weight, qkv, id_column, id_row, tokens, sums_one, sums_two, sums_up, *refs = refs
    kept, sent, d_proj, d_attended, sums = refs
    rows, width = tokens.shape
    own = qkv.shape[1] // 3
    column, core = place[0], place[1]
    put_pieces(pieces, column, d_attended)
    out_rows = out_weight[pl.ds(pl.multiple_of(column * own, own), own), :]
    d_mixed = dot(d_attended[...], out_rows, ((1,), (1,))).astype(jnp.bfloat16)
    for start in range(0, rows, BLOCK):
        rows_at = slice(start, start + BLOCK)
        for head in range(own // HEAD):
            queries, keys, values, probs = probabilities(qkv, rows_at, head, own, id_column, id_row)
            d_out = d_mixed[rows_at, head * HEAD : (head + 1) * HEAD]
            d_probs = dot(d_out, values, ((1,), (1,)))
            d_scores = probs * (d_probs - jnp.sum(probs * d_probs, axis=-1, keepdims=True))
            d_scores = d_scores.astype(jnp.bfloat16)
            d_values = dot(probs.astype(jnp.bfloat16), d_out, ((0,), (0,)))
            d_queries = dot(d_scores, keys, ((1,), (0,))) * HEAD ** (-0.5)
            d_keys = dot(d_scores, queries, ((0,), (0,))) * HEAD ** (-0.5)
            for part, value in enumerate((d_queries, d_keys, d_values)):
                at = part * own + head * HEAD
                d_proj[rows_at, at : at + HEAD] = value.astype(jnp.bfloat16)
    d_proj_all = d_proj[...]
    d_columns = d_attended[:, :own]
    for place_at in range(1, width // own):
        other = d_attended[:, place_at * own : (place_at + 1) * own]
        d_columns = jnp.where(column == place_at, other, d_columns)
    grad_proj = dot(tokens[...], d_proj_all, ((0,), (0,)))
    proj_sums = row_sums(d_proj_all.astype(jnp.float32))
    sums[...] = jnp.zeros_like(sums)
    for at in range(SPLIT):
        lanes = slice(at * own, (at + 1) * own)
        mine = (column == at).astype(jnp.float32)
        sums[0:1, lanes] = proj_sums[:, :own] * mine
        sums[1:2, lanes] = proj_sums[:, 2 * own :] * mine
        sums[8 + at : 9 + at, :] = sums_up[...] * mine
    sums[2:5, :] = sums_one[0:3, :]
    sums[5:8, :] = sums_two[0:3, :]
    depth = kept.shape[1] - sums.shape[0]
    for group in range(width // depth):
        at = slice(group * depth, (group + 1) * depth)

        def put(target, kind):
            target[group // 2, :depth, : 3 * own] = grad_proj[at].astype(kind)
            target[group // 2, depth:, :] = jnp.zeros((sums.shape[0], width), kind)
            target[group // 2, depth:, :depth] = sums[:, at].astype(kind)

        pl.when(core == group % 2)(lambda: put(kept, jnp.float32))
        pl.when(core != group % 2)(lambda: put(sent, jnp.bfloat16))
    for step, piece in enumerate(mixed):
        grad_out = dot(unpack_rows(piece, rows), d_columns, ((0,), (0,)))
        source = source_of(column, step)
        for half in range(2):
            block = grad_out[half * depth : (half + 1) * depth]

            def put_out(target, kind):
                target[source, :depth, 3 * own :] = block.astype(kind)

            pl.when(core == half)(lambda: put_out(kept, jnp.float32))
            pl.when(core != half)(lambda: put_out(sent, jnp.bfloat16))


def token_parts(place, d_proj, weight, *refs):
    parts, (moving,) = refs[:SPLIT], refs[SPLIT:]
    proj = weight[:, weight.shape[1] - d_proj.shape[1] :]
    moving[...] = dot(d_proj[...], proj, ((1,), (1,)))
    take_parts(moving, place[0], parts)


def pair_sum(place, kept, other, total, *blocks):
    chip = place[2]
    total[...] = kept[chip] + other[chip].astype(jnp.float32)
    for step, block in enumerate(blocks):
        at = chip ^ (step + 1)
        block[...] = (kept[at] + other[at].astype(jnp.float32)).astype(jnp.bfloat16)


def square_momenta(place, total, *refs):
    pieces, refs = refs[: SPLIT - 1], refs[SPLIT - 1 :]
    qkv_mom, out_mom, qkv_grad, out_grad, qkv_new, out_new, *refs = refs
    blocks, state = refs[:SPLIT], refs[SPLIT]
    depth, own = out_mom.shape
    whole = sum_pieces([total, *pieces])
    vec_own = depth // SPLIT
    for at in range(SPLIT):
        grad = whole[:depth, at * own : (at + 1) * own]
        if at < SPLIT - 1:
            qkv_grad[at] = grad
            moment = momentum_decay * qkv_mom[at] + grad
            qkv_new[at] = moment
        else:
            out_grad[...] = grad
            moment = momentum_decay * out_mom[...] + grad
            out_new[...] = moment
        state[at, :depth, :] = moment
        state[at, depth:, :] = jnp.zeros((whole.shape[0] - depth, own), jnp.float32)
        state[at, depth:, :vec_own] = whole[depth:, at * vec_own : (at + 1) * vec_own]
    for step, block in enumerate(blocks):
        block[...] = state[lax.rem(place[0] + step, SPLIT)].astype(jnp.bfloat16)


def join_squares(place, *refs):
    pieces, (gram, gram_other, mine, other, sums, rows) = refs[:SPLIT], refs[SPLIT:]
    depth, own = mine.shape[0], pieces[0].shape[1]
    total = jnp.zeros(sums.shape, jnp.float32)
    for step, piece in enumerate(pieces):
        total = total + piece[depth:, :].astype(jnp.float32)
        for at in range(SPLIT):

            @pl.when(source_of(place[0], step) == at)
            def _():
                rows[:, at * own : (at + 1) * own] = piece[:depth, :]

    sums[...] = total
    even = place[1] == 0
    gram_sum = (gram[...].astype(jnp.float32) + gram_other[...].astype(jnp.float32)).astype(jnp.bfloat16)
    mine[...] = jnp.where(even, rows[...], gram_sum)
    other[...] = jnp.where(even, gram_sum, rows[...])


def join_pair(place, mine, other, rows):
    depth = mine.shape[0]
    even = place[1] == 0
    rows[:depth, :] = jnp.where(even, mine[...], other[...])
    rows[depth:, :] = jnp.where(even, other[...], mine[...])


def run_kernel(body, outputs, scalars=0, scratch=(), ties=(), far=(), far_out=()):
    def call(*operands):
        count, made = len(operands), len(outputs)

        def whole(*refs):
            inputs, refs = list(refs[:count]), refs[count + len(ties) :]
            results, refs = list(refs[:made]), refs[made:]
            mine, refs = refs[: len(scratch)], refs[len(scratch) :]
            rooms, refs = refs[: len(far)], refs[len(far) :]
            rooms_out, refs = refs[: len(far_out)], refs[len(far_out) :]
            copies = []
            for at, room in zip(far, rooms):
                copies.append(pltpu.make_async_copy(inputs[at], room, refs[len(copies)]))
                copies[-1].start()
                inputs[at] = room
            for copy in copies:
                copy.wait()
            targets = [results[at] for at in far_out]
            for at, room in zip(far_out, rooms_out):
                results[at] = room
            body(*inputs, *results, *mine)
            copies_out = []
            for room, target in zip(rooms_out, targets):
                at = len(far) + len(copies_out)
                copies_out.append(pltpu.make_async_copy(room, target, refs[at]))
                copies_out[-1].start()
            for copy in copies_out:
                copy.wait()

        operands = list(operands)
        for at in far:
            operands[at] = pltpu.with_memory_space_constraint(operands[at], pltpu.HBM)
        kinds = list(outputs)
        for at in far_out:
            kinds[at] = pltpu.HBM(kinds[at].shape, kinds[at].dtype)
        spaces = [pltpu.SMEM] * scalars + [pltpu.VMEM] * (count - scalars) + [pl.ANY] * len(ties)
        for at in far:
            spaces[at] = pltpu.HBM
        spaces_out = [pltpu.HBM if at in far_out else pltpu.VMEM for at in range(made)]
        rooms = [pltpu.VMEM(operands[at].shape, operands[at].dtype) for at in far]
        rooms_out = [pltpu.VMEM(outputs[at].shape, outputs[at].dtype) for at in far_out]
        signals = [pltpu.SemaphoreType.DMA] * (len(far) + len(far_out))
        return pl.pallas_call(
            whole,
            out_shape=kinds,
            in_specs=[pl.BlockSpec(memory_space=space) for space in spaces],
            out_specs=[pl.BlockSpec(memory_space=space) for space in spaces_out],
            scratch_shapes=[*scratch, *rooms, *rooms_out, *signals],
            compiler_params=pltpu.CompilerParams(vmem_limit_bytes=24 * 2**20),
        )(*operands, *ties)

    return call


def newton_schulz(place, *refs):
    pieces, refs = refs[:SPLIT], refs[SPLIT:]
    wide, kept, sent, heard, gram, *factors = refs
    chip, core = place[2], place[1]
    width = heard.shape[0]
    for step, piece in enumerate(pieces):
        at = pl.multiple_of((chip ^ step) * piece.shape[0], piece.shape[0])
        heard[pl.ds(at, piece.shape[0]), :] = piece[...]
    depth = kept.shape[0]
    even = core == 0

    @pl.when(even)
    def _():
        gram[...] = dot(heard[...], heard[...], ((1,), (1,)))

    @pl.when(jnp.logical_not(even))
    def _():
        gram[...] = heard[...].astype(jnp.float32)

    at_row = lax.broadcasted_iota(jnp.int32, (width, width), 0)
    at_lane = lax.broadcasted_iota(jnp.int32, (width, width), 1)
    trace = jnp.sum(jnp.where(at_row == at_lane, gram[...], 0.0), keepdims=True)
    scale = jnp.sqrt(trace) + ortho_eps
    gram[...] = gram[...] / (scale * scale)
    for step, factor in enumerate(factors):
        gram_b = gram[...].astype(jnp.bfloat16)
        square = dot(gram_b, gram_b, ((1,), (0,)))
        factor[...] = (coef_second * gram[...] + coef_third * square).astype(jnp.bfloat16)
        if step < NS_STEPS - 1:
            moved = dot(factor[...], gram_b, ((1,), (0,)))
            twice = dot(factor[...], moved.astype(jnp.bfloat16), ((1,), (0,)))
            gram[...] = coef_first * coef_first * gram[...] + 2.0 * coef_first * moved + twice
    count = 2 * depth
    start = pl.multiple_of(chip * count, count)
    eye = lax.broadcasted_iota(jnp.int32, (count, width), 0) + start
    eye = (eye == lax.broadcasted_iota(jnp.int32, (count, width), 1)).astype(jnp.float32)
    rows = coef_first * eye + factors[-1][pl.ds(start, count), :].astype(jnp.float32)
    for factor in factors[-2::-1]:
        rows = coef_first * rows + dot(rows.astype(jnp.bfloat16), factor[...], ((1,), (0,)))
    rows = (rows / scale).astype(jnp.bfloat16)

    @pl.when(even)
    def _():
        state = dot(rows, heard[...], ((1,), (0,))).astype(jnp.bfloat16)
        kept[:, :width] = state[:depth]
        sent[:, :width] = state[depth:]
        kept[:, width:] = jnp.zeros_like(kept[:, width:])
        sent[:, width:] = jnp.zeros_like(sent[:, width:])

    @pl.when(jnp.logical_not(even))
    def _():
        state = dot(rows, wide[...], ((1,), (0,))).astype(jnp.bfloat16)
        kept[...] = state[depth:]
        sent[...] = state[:depth]


def split_device(
    tokens, cotangent, doc_lengths, qkv_w, out_w, ffn_w, vecs, qkv_mom, out_mom, ffn_mom, vec_mom
):
    micro, rows, width = tokens.shape
    shards = lax.axis_size("shard")
    groups = lax.axis_size("dp")
    column = lax.axis_index("shard")
    row = lax.axis_index("dp")
    place = jnp.stack([column, row & 1, row >> 1]).astype(jnp.int32)
    slots = micro * shards
    own = qkv_w.shape[2]
    hidden = ffn_w.shape[2]
    bf16 = jnp.bfloat16

    packed = jnp.concatenate(
        [ffn_w[0], ffn_w[1], qkv_w[0], qkv_w[1], qkv_w[2]], axis=1
    ).astype(bf16)
    weights = lax.all_gather(packed, "dp", axis=0, tiled=True)

    flat = tokens.reshape(micro * rows, width)
    vec_rows, vec_own = vecs.shape
    small = jnp.concatenate(
        [vecs.astype(bf16).reshape(-1), doc_lengths.astype(bf16).reshape(-1)]
    )
    small = jnp.pad(small, (0, 8 * width - small.shape[0])).reshape(8, width)
    out_flat = out_w.astype(bf16).reshape(-1, width)
    out_count = out_flat.shape[0]
    heard = gather_direct(jnp.concatenate([flat, out_flat, small], axis=0), "shard")
    tokens_b = heard[:, : micro * rows].reshape(slots * rows, width)
    out_part = heard[:, micro * rows : micro * rows + out_count].reshape(shards, -1, own)
    out_part = out_part.transpose(1, 0, 2).reshape(-1, width)
    small = heard[:, micro * rows + out_count :].reshape(shards, -1)
    lengths = small[:, vecs.size : vecs.size + doc_lengths.size].astype(jnp.int32).reshape(slots, -1)
    small = small[:, : vecs.size].reshape(shards, vec_rows, vec_own).transpose(1, 0, 2).reshape(vec_rows, -1)
    vec = gather_double(small, "dp").transpose(1, 0, 2).reshape(vec_rows, -1).astype(jnp.float32)
    out_b = lax.all_gather(out_part, "dp", axis=0, tiled=True)
    position = jnp.arange(rows, dtype=jnp.int32)[None]
    ends = jnp.cumsum(lengths, axis=1)
    segment = jnp.sum((position[:, :, None] >= ends[:, None, :]).astype(jnp.int32), axis=2)
    valid = position < ends[:, -1:]
    slot = jnp.arange(slots, dtype=jnp.int32)[:, None]
    marks = jnp.where(valid, segment + slot * ends.shape[1], -1 - position - slot * rows)
    id_column, id_row = marks.reshape(-1, 1), marks.reshape(1, -1)
    bias_q = lax.dynamic_slice_in_dim(vec[0], column * own, own, 0)
    bias_v = lax.dynamic_slice_in_dim(vec[1], column * own, own, 0)
    bias_proj = jnp.concatenate([bias_q, jnp.zeros_like(bias_q), bias_v])[None]
    bias_up = lax.dynamic_slice_in_dim(vec[8:].reshape(-1), column * hidden, hidden, 0)[None]

    qkv, mixed_own = run_kernel(
        attention_forward,
        [
            jax.ShapeDtypeStruct((slots * rows, 3 * own), bf16),
            jax.ShapeDtypeStruct((BLOCK, slots * rows // BLOCK * own), bf16),
        ],
        scalars=1,
        ties=[vec, bias_up],
        far=(1, 2, 4),
        far_out=(0,),
    )(place, tokens_b, weights, bias_proj, id_column, id_row)

    depth = width // groups
    count = micro * rows
    whole_b = jax.ShapeDtypeStruct((slots * rows, width), bf16)
    own_f = jax.ShapeDtypeStruct((count, width), jnp.float32)
    own_b = jax.ShapeDtypeStruct((count, width), bf16)
    part_kinds = [own_f] + [own_b] * (shards - 1)
    sums_kind = jax.ShapeDtypeStruct((8, width), jnp.float32)
    moving = pltpu.VMEM((slots * rows, width), jnp.float32)

    mixed_pieces = pieces_of(mixed_own, "shard")
    first_b, activ_b, slope, first_in, *parts = run_kernel(
        layer_middle,
        [whole_b, whole_b, jax.ShapeDtypeStruct((slots * rows, hidden), jnp.float32), own_f] + part_kinds,
        scalars=1,
        scratch=[moving],
        far=(5, 6, 8),
    )(place, *mixed_pieces, out_b, tokens_b, vec, weights, bias_up)
    layer_out, d_branch_own, d_second, sums_two = run_kernel(
        second_norm, [own_b, own_b, own_f, sums_kind], scalars=1, far=(7, 8), far_out=(0, 2, 3)
    )(place, *send_parts(parts, "shard"), first_in, vec, cotangent.reshape(count, width), id_column)
    layer_out = layer_out.reshape(tokens.shape)
    d_branch_b, d_inner_b, d_bias_up, *parts = run_kernel(
        inner_backward,
        [whole_b, whole_b, jax.ShapeDtypeStruct((1, hidden), jnp.float32)] + part_kinds,
        scalars=1,
        scratch=[moving],
        far=(6,),
        far_out=(2, 3, 4, 5, 6),
    )(place, *pieces_of(d_branch_own, "shard"), slope, weights)
    (grads,) = run_kernel(inner_gradients, [jax.ShapeDtypeStruct((2, width, hidden), bf16)], far_out=(0,))(
        first_b, activ_b, d_inner_b, d_branch_b
    )
    summed = lax.psum_scatter(grads, "dp", scatter_dimension=1, tiled=True)
    d_first_in, d_attended_own, sums_one = run_kernel(
        first_norm, [own_f, own_b, sums_kind], far=(0, 4, 5), far_out=(0, 2)
    )(*send_parts(parts, "shard"), d_second, first_in, vec)
    d_attended_pieces = pieces_of(d_attended_own, "shard")
    packed_rows = depth + 16
    kept, sent, d_proj = run_kernel(
        attention_backward,
        [
            jax.ShapeDtypeStruct((groups // 2, packed_rows, width), jnp.float32),
            jax.ShapeDtypeStruct((groups // 2, packed_rows, width), bf16),
            jax.ShapeDtypeStruct((slots * rows, 3 * own), bf16),
        ],
        scalars=1,
        scratch=[pltpu.VMEM((slots * rows, width), bf16), pltpu.VMEM((16, width), jnp.float32)],
        far=(5, 6, 7, 8, 9, 10, 11, 13, 14, 15),
        far_out=(0, 2),
    )(
        place, *d_attended_pieces, *mixed_pieces, out_b, qkv, id_column, id_row, tokens_b,
        sums_one, sums_two, d_bias_up,
    )
    moment_kind = jax.ShapeDtypeStruct(ffn_mom.shape, ffn_mom.dtype)
    wide_kind = jax.ShapeDtypeStruct((depth, hidden), bf16)
    grad_ffn, new_ffn_mom, mine, far = run_kernel(
        wide_momenta,
        [moment_kind, moment_kind, wide_kind, wide_kind],
        scalars=1,
        ties=[kept],
        far=(1, 2),
        far_out=(0, 1),
    )(place, summed, ffn_mom)
    far_rows = swap(far, "shard", shards // 2)
    wide_rows = jnp.concatenate([mine, far_rows], axis=1)
    wide = lax.all_gather(wide_rows, "dp", axis=0, tiled=True)

    block_kind = jax.ShapeDtypeStruct((packed_rows, width), bf16)
    total, *blocks = run_kernel(
        pair_sum, [jax.ShapeDtypeStruct((packed_rows, width), jnp.float32)] + [block_kind] * 3, scalars=1, far=(1,)
    )(place, kept, swap(sent, "dp", 1))
    parts = run_kernel(token_parts, part_kinds, scalars=1, scratch=[moving], ties=[total], far=(1, 2))(
        place, d_proj, weights
    )
    d_tokens = d_first_in + sum(part.astype(jnp.float32) for part in send_parts(parts, "shard"))
    block_kind = jax.ShapeDtypeStruct((packed_rows, own), bf16)
    like = [jax.ShapeDtypeStruct(each.shape, each.dtype) for each in (qkv_mom, out_mom)]
    grad_qkv, grad_wout, new_qkv_mom, new_out_mom, *blocks = run_kernel(
        square_momenta,
        like + like + [block_kind] * shards,
        scalars=1,
        scratch=[pltpu.VMEM((shards, packed_rows, own), jnp.float32)],
        far=(5, 6),
        far_out=(0, 1, 2, 3),
    )(place, total, *[swap(block, "dp", 2 * at + 2) for at, block in enumerate(blocks)], qkv_mom, out_mom)
    (gram_rows,) = run_kernel(wide_gram, [jax.ShapeDtypeStruct((depth, width), bf16)], ties=blocks, far=(0, 1))(
        wide_rows, wide
    )
    row_kind = jax.ShapeDtypeStruct((depth, width), bf16)
    mine, other, grad_vec = run_kernel(
        join_squares,
        [row_kind, row_kind, jax.ShapeDtypeStruct((packed_rows - depth, own), jnp.float32)],
        scalars=1,
        scratch=[pltpu.VMEM((depth, width), bf16)],
        ties=[d_tokens],
    )(place, *send_parts(blocks, "shard"), gram_rows, swap(gram_rows, "shard", 1))
    grad_vec = grad_vec[:vec_rows, :vec_own]
    d_tokens = d_tokens.reshape(tokens.shape)
    (pair_rows,) = run_kernel(
        join_pair, [jax.ShapeDtypeStruct((2 * depth, width), bf16)], scalars=1
    )(place, mine, swap(other, "dp", 1))
    pair_pieces = [pair_rows] + [swap(pair_rows, "dp", bit) for bit in (2, 4, 6)]
    state_kind = jax.ShapeDtypeStruct((depth, 2 * hidden), bf16)
    kept, sent = run_kernel(
        newton_schulz,
        [state_kind, state_kind],
        scalars=1,
        scratch=[pltpu.VMEM((width, width), bf16), pltpu.VMEM((width, width), jnp.float32)]
        + [pltpu.VMEM((width, width), bf16)] * NS_STEPS,
        far=(5,),
    )(place, *pair_pieces, wide)
    block_kind = jax.ShapeDtypeStruct((depth, own), bf16)
    wide_kind = jax.ShapeDtypeStruct((depth, hidden), bf16)
    *blocks, mine, far = run_kernel(
        split_state, [block_kind] * shards + [wide_kind, wide_kind], scalars=1
    )(place, kept, swap(sent, "dp", 1))
    qkv_new, out_new, ffn_new = run_kernel(
        new_weights,
        [jax.ShapeDtypeStruct(each.shape, each.dtype) for each in (qkv_w, out_w, ffn_w)],
        scalars=1,
        scratch=[pltpu.VMEM((shards, depth, own), jnp.float32)],
        far=(7, 8, 9),
        far_out=(0, 1, 2),
    )(
        place, *send_parts(blocks, "shard"), mine, swap(far, "shard", shards // 2), qkv_w, out_w, ffn_w
    )

    token_count = micro * rows * groups * shards
    new_vec_mom = momentum_decay * vec_mom + grad_vec
    vec_new = vecs - vec_rate * token_count ** (-0.5) * new_vec_mom
    return (
        layer_out,
        d_tokens,
        grad_qkv,
        grad_wout,
        grad_ffn,
        grad_vec,
        new_qkv_mom,
        new_out_mom,
        new_ffn_mom,
        new_vec_mom,
        qkv_new,
        out_new,
        ffn_new,
        vec_new,
    )


def solution(mesh):
    fits = (mesh.shape["dp"], mesh.shape["shard"]) == (8, 4)
    in_specs = (
        P(("dp", "shard"), None, None),
        P(("dp", "shard"), None, None),
        P(("dp", "shard"), None),
        P(None, "dp", "shard"),
        P("dp", "shard"),
        P(None, "dp", "shard"),
        P(None, ("dp", "shard")),
        P(None, "dp", "shard"),
        P("dp", "shard"),
        P(None, "dp", "shard"),
        P(None, ("dp", "shard")),
    )
    out_specs = (
        P(("dp", "shard"), None, None),
        P(("dp", "shard"), None, None),
        P(None, "dp", "shard"),
        P("dp", "shard"),
        P(None, "dp", "shard"),
        P(None, ("dp", "shard")),
        P(None, "dp", "shard"),
        P("dp", "shard"),
        P(None, "dp", "shard"),
        P(None, ("dp", "shard")),
        P(None, "dp", "shard"),
        P("dp", "shard"),
        P(None, "dp", "shard"),
        P(None, ("dp", "shard")),
    )
    return jax.shard_map(
        split_device if fits else per_device, mesh=mesh, in_specs=in_specs, out_specs=out_specs, check_vma=False
    )
```

```python
import math
import jax
import jax.numpy as jnp
from jax import lax
from jax.experimental import pallas as pl
from jax.experimental.pallas import tpu as pltpu
from jax.sharding import PartitionSpec as P

D = 768
HEADS = 12
HEAD = 64
FF = 3072
NS_STEPS = 3


masked_score = -1e30
norm_eps = 1e-12
momentum_decay = 0.9
muon_rate = 0.8
vec_rate = 0.5
coef_first = 3.4445
coef_second = -4.775
coef_third = 2.0315
ortho_eps = 1e-07


def spread_2(block, axis, owner):
    block = jnp.where(lax.axis_index(axis) == owner, block, jnp.zeros_like(block))
    return lax.psum(block, axis)


def segments(lengths, rows):
    position = jnp.arange(rows, dtype=jnp.int32)
    ends = jnp.cumsum(lengths)
    segment = jnp.sum((position[:, None] >= ends[None, :]).astype(jnp.int32), axis=1)
    valid = position < ends[-1]
    same = segment[:, None] == segment[None, :]
    allowed = same & valid[:, None] | (position[:, None] == position[None, :])
    return (valid, allowed)


def layer_norm(inputs, gain, bias):
    center = inputs - jnp.mean(inputs, axis=-1, keepdims=True)
    spread = jnp.mean(center * center, axis=-1, keepdims=True)
    return center * lax.rsqrt(spread + norm_eps) * gain + bias


def gelu_exact(inputs):
    return jax.nn.gelu(inputs, approximate=False)


def split_heads(matrix):
    return matrix.reshape(matrix.shape[0], HEADS, HEAD)


def gather_weights(qkv_w, out_w, ffn_w, vecs):
    pieces = (
        qkv_w.astype(jnp.bfloat16),
        out_w.astype(jnp.bfloat16),
        ffn_w.astype(jnp.bfloat16),
        vecs.astype(jnp.bfloat16),
    )
    across = (
        lax.all_gather(pieces[0], "shard", axis=2, tiled=True),
        lax.all_gather(pieces[1], "shard", axis=1, tiled=True),
        lax.all_gather(pieces[2], "shard", axis=2, tiled=True),
        lax.all_gather(pieces[3], "shard", axis=1, tiled=True),
    )
    return (
        lax.all_gather(across[0], "dp", axis=1, tiled=True),
        lax.all_gather(across[1], "dp", axis=0, tiled=True),
        lax.all_gather(across[2], "dp", axis=1, tiled=True),
        lax.all_gather(across[3], "dp", axis=1, tiled=True),
    )


def attention_scores(queries_b, keys_b, allowed):
    scores = jnp.einsum(
        "qhd,khd->hqk",
        split_heads(queries_b),
        split_heads(keys_b),
        preferred_element_type=jnp.float32,
    )
    return jnp.where(allowed[None], scores * HEAD ** (-0.5), masked_score)


def forward_pass(tokens_b, lengths, weights):
    qkv_b, out_b, ffn_b, vec_b = weights
    vec = vec_b.astype(jnp.float32)
    rows = tokens_b.shape[0]
    valid, allowed = segments(lengths, rows)
    projected = jnp.einsum("rd,kde->kre", tokens_b, qkv_b, preferred_element_type=jnp.float32)
    queries_b = (projected[0] + vec[0]).astype(jnp.bfloat16)
    keys_b = projected[1].astype(jnp.bfloat16)
    values_b = (projected[2] + vec[1]).astype(jnp.bfloat16)
    scores = attention_scores(queries_b, keys_b, allowed)
    largest = jnp.max(scores, axis=-1, keepdims=True)
    exponent = jnp.exp(scores - largest)
    totals = jnp.sum(exponent, axis=-1, keepdims=True)
    logsum = largest + jnp.log(totals)
    probs_b = (exponent / totals).astype(jnp.bfloat16)
    mixed = jnp.einsum(
        "hqk,khd->qhd", probs_b, split_heads(values_b), preferred_element_type=jnp.float32
    )
    mixed_b = mixed.reshape(rows, -1).astype(jnp.bfloat16)
    attended = jnp.dot(mixed_b, out_b, preferred_element_type=jnp.float32) + vec[2]
    first_in = tokens_b.astype(jnp.float32) + attended
    first = layer_norm(first_in, vec[3], vec[4])
    first_b = first.astype(jnp.bfloat16)
    inner = jnp.dot(first_b, ffn_b[0], preferred_element_type=jnp.float32) + vec[8:].reshape(-1)
    activ_b = gelu_exact(inner).astype(jnp.bfloat16)
    branch = jnp.einsum("rf,df->rd", activ_b, ffn_b[1], preferred_element_type=jnp.float32) + vec[5]
    second_in = first + branch
    result = layer_norm(second_in, vec[6], vec[7]) * valid[:, None].astype(jnp.float32)
    kept = (
        queries_b,
        keys_b,
        values_b,
        logsum,
        mixed_b,
        first_in,
        first_b,
        inner,
        activ_b,
        second_in,
    )
    return (result.astype(jnp.bfloat16), kept)


def backward_pass(cot_b, tokens_b, lengths, weights, kept):
    qkv_b, out_b, ffn_b, vec_b = weights
    vec = vec_b.astype(jnp.float32)
    queries_b, keys_b, values_b, logsum, mixed_b, first_in, first_b, inner, activ_b, second_in = (
        kept
    )
    rows = tokens_b.shape[0]
    valid, allowed = segments(lengths, rows)
    grad_out = cot_b.astype(jnp.float32) * valid[:, None].astype(jnp.float32)
    unused, pull_two = jax.vjp(layer_norm, second_in, vec[6], vec[7])
    d_second, d_gain_two, d_shift_two = pull_two(grad_out)
    d_branch_b = d_second.astype(jnp.bfloat16)
    d_bias_down = jnp.sum(d_branch_b.astype(jnp.float32), axis=0)
    d_activ = jnp.dot(d_branch_b, ffn_b[1], preferred_element_type=jnp.float32)
    unused, pull_gelu = jax.vjp(gelu_exact, inner)
    (d_inner,) = pull_gelu(d_activ)
    d_inner_b = d_inner.astype(jnp.bfloat16)
    d_bias_up = jnp.sum(d_inner_b.astype(jnp.float32), axis=0)
    d_first = d_second + jnp.einsum(
        "rf,df->rd", d_inner_b, ffn_b[0], preferred_element_type=jnp.float32
    )
    unused, pull_one = jax.vjp(layer_norm, first_in, vec[3], vec[4])
    d_first_in, d_gain_one, d_shift_one = pull_one(d_first)
    d_attended_b = d_first_in.astype(jnp.bfloat16)
    d_bias_out = jnp.sum(d_attended_b.astype(jnp.float32), axis=0)
    d_mixed_b = jnp.einsum(
        "re,de->rd", d_attended_b, out_b, preferred_element_type=jnp.float32
    ).astype(jnp.bfloat16)
    scores = attention_scores(queries_b, keys_b, allowed)
    probs = jnp.exp(scores - logsum)
    mixed_heads = split_heads(d_mixed_b)
    d_probs = jnp.einsum(
        "qhd,khd->hqk", mixed_heads, split_heads(values_b), preferred_element_type=jnp.float32
    )
    d_values = jnp.einsum(
        "hqk,qhd->khd", probs.astype(jnp.bfloat16), mixed_heads, preferred_element_type=jnp.float32
    )
    d_scores_b = (probs * (d_probs - jnp.sum(probs * d_probs, axis=-1, keepdims=True))).astype(
        jnp.bfloat16
    )
    d_queries = jnp.einsum(
        "hqk,khd->qhd", d_scores_b, split_heads(keys_b), preferred_element_type=jnp.float32
    ) * HEAD ** (-0.5)
    d_keys = jnp.einsum(
        "hqk,qhd->khd", d_scores_b, split_heads(queries_b), preferred_element_type=jnp.float32
    ) * HEAD ** (-0.5)
    d_proj_b = jnp.stack([d_queries, d_keys, d_values]).reshape(3, rows, -1).astype(jnp.bfloat16)
    d_tokens = d_first_in + jnp.einsum(
        "kre,kde->rd", d_proj_b, qkv_b, preferred_element_type=jnp.float32
    )
    proj_sums = jnp.sum(d_proj_b.astype(jnp.float32), axis=1)
    grad_vec = jnp.concatenate(
        [
            jnp.stack(
                [
                    proj_sums[0],
                    proj_sums[2],
                    d_bias_out,
                    d_gain_one,
                    d_shift_one,
                    d_bias_down,
                    d_gain_two,
                    d_shift_two,
                ]
            ),
            d_bias_up.reshape(-1, vec.shape[1]),
        ],
        axis=0,
    )
    factors = (d_branch_b, activ_b, first_b, d_inner_b, mixed_b, d_attended_b, d_proj_b)
    return (d_tokens, factors, grad_vec)


def orthogonalize_pair(square, wide):
    matrices = (square, wide)
    present = tuple((matrix.astype(jnp.bfloat16) for matrix in matrices))
    states = matrices
    for step in range(NS_STEPS):
        partial_value = tuple(
            (
                jnp.einsum("iw,jw->ij", block, block, preferred_element_type=jnp.float32)
                for block in present
            )
        )
        gram_part = (
            lax.psum_scatter(
                partial_value[0].astype(jnp.bfloat16), "shard", scatter_dimension=0, tiled=True
            ).astype(jnp.float32),
            lax.psum_scatter(
                partial_value[1].astype(jnp.bfloat16), "shard", scatter_dimension=0, tiled=True
            ).astype(jnp.float32),
        )
        grams = (
            lax.all_gather(gram_part[0].astype(jnp.bfloat16), "shard", axis=0, tiled=True).astype(
                jnp.float32
            ),
            lax.all_gather(gram_part[1].astype(jnp.bfloat16), "shard", axis=0, tiled=True).astype(
                jnp.float32
            ),
        )
        if step == 0:
            scales = tuple((jnp.sqrt(jnp.trace(gram)) + ortho_eps for gram in grams))
            grams = tuple((gram / (scale * scale) for gram, scale in zip(grams, scales)))
            present = tuple(
                ((matrix / scale).astype(jnp.bfloat16) for matrix, scale in zip(matrices, scales))
            )
        renewed = []
        for gram, current in zip(grams, present):
            gram_b = gram.astype(jnp.bfloat16)
            once = jnp.dot(gram_b, current, preferred_element_type=jnp.float32)
            twice = jnp.dot(gram_b, once.astype(jnp.bfloat16), preferred_element_type=jnp.float32)
            renewed.append(
                coef_first * current.astype(jnp.float32) + coef_second * once + coef_third * twice
            )
        states = tuple(renewed)
        present = tuple((state.astype(jnp.bfloat16) for state in states))
    return states


def per_device(
    tokens, cotangent, doc_lengths, qkv_w, out_w, ffn_w, vecs, qkv_mom, out_mom, ffn_mom, vec_mom
):
    micro = tokens.shape[0]
    shared = gather_weights(qkv_w, out_w, ffn_w, vecs)
    outputs = []
    stored = []
    for index in range(micro):
        weights = shared
        result_b, kept = forward_pass(tokens[index], doc_lengths[index], weights)
        outputs.append(result_b)
        stored.append(kept)
    grad_rows = [None] * micro
    factor_list = [None] * micro
    vec_total = None
    for index in reversed(range(micro)):
        weights = shared
        d_tokens, factors, vec_part = backward_pass(
            cotangent[index], tokens[index], doc_lengths[index], weights, stored[index]
        )
        grad_rows[index] = d_tokens
        factor_list[index] = factors
        vec_total = vec_part if vec_total is None else vec_total + vec_part
    (
        branch_gradient_rows,
        activation_rows,
        first_norm_rows,
        inner_gradient_rows,
        mixed_all,
        d_attended_all,
        d_proj_all,
    ) = [jnp.stack([factors[place] for factors in factor_list]) for place in range(7)]
    grad_down = jnp.einsum(
        "hzo,hzx->ox", branch_gradient_rows, activation_rows, preferred_element_type=jnp.float32
    )
    up_weight_gradient = jnp.einsum(
        "hzo,hzx->ox", first_norm_rows, inner_gradient_rows, preferred_element_type=jnp.float32
    )
    grad_wout_sum = jnp.einsum(
        "mrd,mre->de", mixed_all, d_attended_all, preferred_element_type=jnp.float32
    )
    grad_qkv_sum = jnp.einsum(
        "mrd,mkre->kde", tokens, d_proj_all, preferred_element_type=jnp.float32
    )
    summed = (grad_qkv_sum, grad_wout_sum, jnp.stack([up_weight_gradient, grad_down]), vec_total)
    reduced = (
        lax.psum_scatter(
            summed[0].astype(jnp.bfloat16), "dp", scatter_dimension=1, tiled=True
        ).astype(jnp.float32),
        lax.psum_scatter(
            summed[1].astype(jnp.bfloat16), "dp", scatter_dimension=0, tiled=True
        ).astype(jnp.float32),
        lax.psum_scatter(
            summed[2].astype(jnp.bfloat16), "dp", scatter_dimension=1, tiled=True
        ).astype(jnp.float32),
        lax.psum_scatter(
            summed[3].astype(jnp.bfloat16), "dp", scatter_dimension=1, tiled=True
        ).astype(jnp.float32),
    )
    grad_qkv, grad_wout, grad_ffn, grad_vec = (
        lax.psum_scatter(
            reduced[0].astype(jnp.bfloat16), "shard", scatter_dimension=2, tiled=True
        ).astype(jnp.float32),
        lax.psum_scatter(
            reduced[1].astype(jnp.bfloat16), "shard", scatter_dimension=1, tiled=True
        ).astype(jnp.float32),
        lax.psum_scatter(
            reduced[2].astype(jnp.bfloat16), "shard", scatter_dimension=2, tiled=True
        ).astype(jnp.float32),
        lax.psum_scatter(
            reduced[3].astype(jnp.bfloat16), "shard", scatter_dimension=1, tiled=True
        ).astype(jnp.float32),
    )
    new_qkv_mom = momentum_decay * qkv_mom + grad_qkv
    new_out_mom = momentum_decay * out_mom + grad_wout
    new_ffn_mom = momentum_decay * ffn_mom + grad_ffn
    square_local = jnp.concatenate([new_qkv_mom, new_out_mom[None]], axis=0)
    square_cols, wide_cols = (
        lax.all_gather(square_local.astype(jnp.bfloat16), "dp", axis=1, tiled=True).astype(
            square_local.dtype
        ),
        lax.all_gather(new_ffn_mom.astype(jnp.bfloat16), "dp", axis=1, tiled=True).astype(
            new_ffn_mom.dtype
        ),
    )
    row = lax.axis_index("dp")
    rows_count = lax.axis_size("dp")
    owners = [place * rows_count // 6 for place in range(6)]
    square_pick = sum(((row == owners[place]).astype(jnp.int32) * place for place in range(4)))
    wide_pick = (row == owners[5]).astype(jnp.int32)
    square_state, wide_state = orthogonalize_pair(
        lax.dynamic_index_in_dim(square_cols, square_pick, 0, keepdims=False),
        lax.dynamic_index_in_dim(wide_cols, wide_pick, 0, keepdims=False),
    )
    depth = qkv_w.shape[1]
    square_rows = []
    for place in range(4):
        whole = spread_2(square_state.astype(jnp.bfloat16), "dp", owners[place]).astype(
            square_state.dtype
        )
        square_rows.append(lax.dynamic_slice_in_dim(whole, row * depth, depth, 0))
    wide_rows = []
    for place in range(4, 6):
        whole = spread_2(wide_state.astype(jnp.bfloat16), "dp", owners[place]).astype(
            wide_state.dtype
        )
        wide_rows.append(lax.dynamic_slice_in_dim(whole, row * depth, depth, 0))
    qkv_new = qkv_w - muon_rate * jnp.stack(square_rows[:3])
    out_new = out_w - muon_rate * square_rows[3]
    ffn_new = ffn_w - muon_rate * (FF / D) ** 0.5 * jnp.stack(wide_rows)
    token_count = tokens.shape[0] * tokens.shape[1] * lax.axis_size("dp") * lax.axis_size("shard")
    new_vec_mom = momentum_decay * vec_mom + grad_vec
    vec_new = vecs - vec_rate * token_count ** (-0.5) * new_vec_mom
    return (
        jnp.stack(outputs),
        jnp.stack(grad_rows),
        grad_qkv,
        grad_wout,
        grad_ffn,
        grad_vec,
        new_qkv_mom,
        new_out_mom,
        new_ffn_mom,
        new_vec_mom,
        qkv_new,
        out_new,
        ffn_new,
        vec_new,
    )


def gather_direct(block, axis):
    count = lax.axis_size(axis)
    me = lax.axis_index(axis)
    whole = jnp.zeros((count,) + block.shape, block.dtype)
    whole = lax.dynamic_update_index_in_dim(whole, block, me, 0)
    for step in range(1, count):
        got = lax.ppermute(block, axis, [(i, (i + step) % count) for i in range(count)])
        whole = lax.dynamic_update_index_in_dim(whole, got, lax.rem(me - step + count, count), 0)
    return whole


def pieces_of(block, axis):
    count = lax.axis_size(axis)
    return [block] + [
        lax.ppermute(block, axis, [(i, (i + step) % count) for i in range(count)])
        for step in range(1, count)
    ]


def send_parts(parts, axis):
    count = lax.axis_size(axis)
    return [parts[0]] + [
        lax.ppermute(parts[step], axis, [(i, (i + step) % count) for i in range(count)])
        for step in range(1, count)
    ]


def swap(block, axis, bit):
    return lax.ppermute(block, axis, [(i, i ^ bit) for i in range(lax.axis_size(axis))])


def gather_double(block, axis):
    me = lax.axis_index(axis)
    bit = 1
    whole = block[None]
    while bit < lax.axis_size(axis):
        other = swap(whole, axis, bit)
        high = (me & bit) != 0
        whole = jnp.concatenate(
            [jnp.where(high, other, whole), jnp.where(high, whole, other)], axis=0
        )
        bit *= 2
    return whole


def dot(left, right, dims):
    return lax.dot_general(left, right, (dims, ((), ())), preferred_element_type=jnp.float32)


def norm_parts(inputs):
    center = inputs - jnp.mean(inputs, axis=-1, keepdims=True)
    spread = jnp.mean(center * center, axis=-1, keepdims=True)
    scale = lax.rsqrt(spread + norm_eps)
    return center * scale, scale


def norm_back(grad, unit, scale, gain):
    scaled = grad * gain
    mean_grad = jnp.mean(scaled, axis=-1, keepdims=True)
    mean_unit = jnp.mean(scaled * unit, axis=-1, keepdims=True)
    return scale * (scaled - mean_grad - unit * mean_unit)


BLOCK = 256
PAD = 64
SPLIT = 4


def source_of(column, step):
    return lax.rem(column - step + SPLIT, SPLIT)


def put_pieces(pieces, column, whole):
    count = pieces[0].shape[0]
    for step, piece in enumerate(pieces):
        at = pl.multiple_of(source_of(column, step) * count, count)
        whole[pl.ds(at, count), :] = piece[...]


def take_parts(whole, column, parts):
    count = parts[0].shape[0]
    for step, part in enumerate(parts):
        at = pl.multiple_of(lax.rem(column + step, SPLIT) * count, count)
        part[...] = whole[pl.ds(at, count), :].astype(part.dtype)


def sum_pieces(pieces):
    total = pieces[0][...]
    for piece in pieces[1:]:
        total = total + piece[...].astype(jnp.float32)
    return total


def row_sums(values):
    return jnp.sum(values, axis=0, keepdims=True)


def unpack_rows(piece, rows):
    count = rows // piece.shape[0]
    own = piece.shape[1] // count
    return jnp.concatenate([piece[:, at * own : (at + 1) * own] for at in range(count)], axis=0)


def layer_middle(waits, place, *refs):
    pieces, refs = refs[:SPLIT], refs[SPLIT:]
    out_weight, tokens, vec, weights, bias_up, first_b, activ_b, slope, first_in, *refs = refs
    parts, (moving,) = refs[:SPLIT], refs[SPLIT:]
    column = place[0]
    attended = vec[2:3, :] + tokens[...].astype(jnp.float32)
    for step, piece in enumerate(pieces):
        rows = unpack_rows(piece, tokens.shape[0])
        own = rows.shape[1]
        at = pl.multiple_of(source_of(column, step) * own, own)
        attended = attended + dot(rows, out_weight[pl.ds(at, own), :], ((1,), (0,)))
    moving[...] = attended
    take_parts(moving, column, [first_in])
    unit, scale = norm_parts(attended)
    first_b[...] = (unit * vec[3:4, :] + vec[4:5, :]).astype(jnp.bfloat16)
    hidden = slope.shape[1]
    waits[0]()
    inner = dot(first_b[...], weights[:, :hidden], ((1,), (0,))) + bias_up[...]
    cdf = 0.5 * (1.0 + lax.erf(inner * 2.0 ** (-0.5)))
    activ_b[...] = (inner * cdf).astype(jnp.bfloat16)
    slope[...] = cdf + inner * jnp.exp(-0.5 * inner * inner) * (2.0 * math.pi) ** (-0.5)
    moving[...] = dot(activ_b[...], weights[:, hidden : 2 * hidden], ((1,), (1,)))
    take_parts(moving, column, parts)


def second_norm(place, *refs):
    pieces, refs = refs[:SPLIT], refs[SPLIT:]
    first_in, vec, cotangent, ids, layer_out, d_branch, d_second, sums = refs
    count = first_in.shape[0]
    at = pl.multiple_of(place[0] * count, count)
    valid = (ids[pl.ds(at, count), :] >= 0).astype(jnp.float32)
    unit, scale = norm_parts(first_in[...])
    first = unit * vec[3:4, :] + vec[4:5, :]
    unit, scale = norm_parts(first + (sum_pieces(pieces) + vec[5:6, :]))
    layer_out[...] = ((unit * vec[6:7, :] + vec[7:8, :]) * valid).astype(jnp.bfloat16)
    grad = cotangent[...].astype(jnp.float32) * valid
    d_rows = norm_back(grad, unit, scale, vec[6:7, :])
    d_second[...] = d_rows
    d_branch[...] = d_rows.astype(jnp.bfloat16)
    sums[0:1, :] = row_sums(d_branch[...].astype(jnp.float32))
    sums[1:2, :] = row_sums(grad * unit)
    sums[2:3, :] = row_sums(grad)


def inner_backward(place, *refs):
    pieces, refs = refs[:SPLIT], refs[SPLIT:]
    slope, weights, d_branch, d_inner, sums, *refs = refs
    parts, (moving,) = refs[:SPLIT], refs[SPLIT:]
    column = place[0]
    put_pieces(pieces, column, d_branch)
    hidden = slope.shape[1]
    d_activ = dot(d_branch[...], weights[:, hidden : 2 * hidden], ((1,), (0,)))
    d_inner[...] = (d_activ * slope[...]).astype(jnp.bfloat16)
    sums[...] = row_sums(d_inner[...].astype(jnp.float32))
    moving[...] = dot(d_inner[...], weights[:, :hidden], ((1,), (1,)))
    take_parts(moving, column, parts)


def inner_gradients(first_b, activ_b, d_inner, d_branch, grads):
    grads[0] = dot(first_b[...], d_inner[...], ((0,), (0,))).astype(jnp.bfloat16)
    grads[1] = dot(d_branch[...], activ_b[...], ((0,), (0,))).astype(jnp.bfloat16)


def wide_momenta(place, summed, moments, grads, moments_new, mine, far):
    low = place[0] < SPLIT // 2
    for part in range(2):
        grads[part] = summed[part].astype(jnp.float32)
        moments_new[part] = momentum_decay * moments[part] + grads[part]
    first, second = moments_new[0].astype(jnp.bfloat16), moments_new[1].astype(jnp.bfloat16)
    mine[...] = jnp.where(low, first, second)
    far[...] = jnp.where(low, second, first)


def join_wide(mine, far, rows):
    hidden = mine.shape[1]
    rows[:, :hidden] = mine[...]
    rows[:, hidden:] = far[...]


def wide_gram(rows, wide, gram):
    gram[...] = dot(rows[...], wide[...], ((1,), (1,))).astype(jnp.bfloat16)


def first_norm(*refs):
    pieces, refs = refs[:SPLIT], refs[SPLIT:]
    d_second, first_in, vec, d_first_in, d_attended, sums = refs
    unit, scale = norm_parts(first_in[...])
    grad = sum_pieces(pieces) + d_second[...]
    d_rows = norm_back(grad, unit, scale, vec[3:4, :])
    d_first_in[...] = d_rows
    d_attended[...] = d_rows.astype(jnp.bfloat16)
    sums[0:1, :] = row_sums(d_attended[...].astype(jnp.float32))
    sums[1:2, :] = row_sums(grad * unit)
    sums[2:3, :] = row_sums(grad)


def split_state(place, kept, other, *refs):
    blocks, (mine,) = refs[:SPLIT], refs[SPLIT:]
    column, even = place[0], place[1] == 0
    own, hidden = blocks[0].shape[1], mine.shape[1]
    far = blocks[SPLIT // 2]
    for step, block in enumerate(blocks):
        there = lax.rem(column + step, SPLIT)
        for at in range(SPLIT):
            lanes = slice(at * own, (at + 1) * own)

            @pl.when(there == at)
            def _():
                block[:, block.shape[1] - own :] = jnp.where(even, kept[:, lanes], other[:, lanes])

    mine[...] = jnp.where(even, other[:, :hidden], kept[:, :hidden])
    far[:, :hidden] = jnp.where(even, other[:, hidden:], kept[:, hidden:])


def new_weights(place, *refs):
    pieces, refs = refs[:SPLIT], refs[SPLIT:]
    mine, qkv_w, out_w, ffn_w, qkv_new, out_new, ffn_new, state = refs
    low = place[0] < SPLIT // 2
    own, hidden = out_w.shape[1], mine.shape[1]
    far = pieces[SPLIT // 2][:, :hidden]
    for step, piece in enumerate(pieces):
        state[source_of(place[0], step)] = piece[:, piece.shape[1] - own :].astype(jnp.float32)
    for at in range(SPLIT - 1):
        qkv_new[at] = qkv_w[at] - muon_rate * state[at]
    out_new[...] = out_w[...] - muon_rate * state[SPLIT - 1]
    rate = muon_rate * (FF / D) ** 0.5
    ffn_new[0] = ffn_w[0] - rate * jnp.where(low, mine[...], far).astype(jnp.float32)
    ffn_new[1] = ffn_w[1] - rate * jnp.where(low, far, mine[...]).astype(jnp.float32)


def probabilities(qkv, rows_at, head, own, id_column, id_row):
    queries = qkv[rows_at, head * HEAD : (head + 1) * HEAD]
    keys = qkv[rows_at, own + head * HEAD : own + (head + 1) * HEAD]
    values = qkv[rows_at, 2 * own + head * HEAD : 2 * own + (head + 1) * HEAD]
    scores = dot(queries, keys, ((1,), (1,))) * HEAD ** (-0.5)
    scores = jnp.where(id_column[rows_at, :] == id_row[:, rows_at], scores, masked_score)
    exponent = jnp.exp(scores - jnp.max(scores, axis=-1, keepdims=True))
    probs = exponent / jnp.sum(exponent, axis=-1, keepdims=True)
    return queries, keys, values, probs


def attention_forward(place, tokens, weight, bias, id_column, id_row, qkv, mixed):
    own = qkv.shape[1] // 3
    proj = weight[:, : 3 * own]
    qkv[...] = (dot(tokens[...], proj, ((1,), (0,))) + bias[...]).astype(jnp.bfloat16)
    for start in range(0, tokens.shape[0], BLOCK):
        rows_at = slice(start, start + BLOCK)
        for head in range(own // HEAD):
            queries, keys, values, probs = probabilities(qkv, rows_at, head, own, id_column, id_row)
            part = dot(probs.astype(jnp.bfloat16), values, ((1,), (0,)))
            at = start // BLOCK * own + head * HEAD
            mixed[:, at : at + HEAD] = part.astype(jnp.bfloat16)


def attention_backward(waits, place, *refs):
    pieces, mixed, refs = refs[:SPLIT], refs[SPLIT : 2 * SPLIT], refs[2 * SPLIT :]
    out_weight, qkv, id_column, id_row, tokens, sums_one, sums_two, sums_up, *refs = refs
    kept, sent, d_proj, d_attended, sums = refs
    rows, width = tokens.shape
    own = qkv.shape[1] // 3
    column, core = place[0], place[1]
    put_pieces(pieces, column, d_attended)
    out_rows = out_weight[pl.ds(pl.multiple_of(column * own, own), own), :]
    d_mixed = dot(d_attended[...], out_rows, ((1,), (1,))).astype(jnp.bfloat16)
    for start in range(0, rows, BLOCK):
        rows_at = slice(start, start + BLOCK)
        for head in range(own // HEAD):
            queries, keys, values, probs = probabilities(qkv, rows_at, head, own, id_column, id_row)
            d_out = d_mixed[rows_at, head * HEAD : (head + 1) * HEAD]
            d_probs = dot(d_out, values, ((1,), (1,)))
            d_scores = probs * (d_probs - jnp.sum(probs * d_probs, axis=-1, keepdims=True))
            d_scores = d_scores.astype(jnp.bfloat16)
            d_values = dot(probs.astype(jnp.bfloat16), d_out, ((0,), (0,)))
            d_queries = dot(d_scores, keys, ((1,), (0,))) * HEAD ** (-0.5)
            d_keys = dot(d_scores, queries, ((0,), (0,))) * HEAD ** (-0.5)
            for part, value in enumerate((d_queries, d_keys, d_values)):
                at = part * own + head * HEAD
                d_proj[rows_at, at : at + HEAD] = value.astype(jnp.bfloat16)
    d_proj_all = d_proj[...]
    d_columns = d_attended[:, :own]
    for place_at in range(1, width // own):
        other = d_attended[:, place_at * own : (place_at + 1) * own]
        d_columns = jnp.where(column == place_at, other, d_columns)
    for wait in waits:
        wait()
    grad_proj = dot(tokens[...], d_proj_all, ((0,), (0,)))
    proj_sums = row_sums(d_proj_all.astype(jnp.float32))
    sums[...] = jnp.zeros_like(sums)
    for at in range(SPLIT):
        lanes = slice(at * own, (at + 1) * own)
        mine = (column == at).astype(jnp.float32)
        sums[0:1, lanes] = proj_sums[:, :own] * mine
        sums[1:2, lanes] = proj_sums[:, 2 * own :] * mine
        sums[8 + at : 9 + at, :] = sums_up[...] * mine
    sums[2:5, :] = sums_one[0:3, :]
    sums[5:8, :] = sums_two[0:3, :]
    depth = kept.shape[1] - sums.shape[0]
    for group in range(width // depth):
        at = slice(group * depth, (group + 1) * depth)

        def put(target, kind):
            target[group // 2, :depth, : 3 * own] = grad_proj[at].astype(kind)
            target[group // 2, depth:, :] = jnp.zeros((sums.shape[0], width), kind)
            target[group // 2, depth:, :depth] = sums[:, at].astype(kind)

        pl.when(core == group % 2)(lambda: put(kept, jnp.float32))
        pl.when(core != group % 2)(lambda: put(sent, jnp.bfloat16))
    for step, piece in enumerate(mixed):
        grad_out = dot(unpack_rows(piece, rows), d_columns, ((0,), (0,)))
        source = source_of(column, step)
        for half in range(2):
            block = grad_out[half * depth : (half + 1) * depth]

            def put_out(target, kind):
                target[source, :depth, 3 * own :] = block.astype(kind)

            pl.when(core == half)(lambda: put_out(kept, jnp.float32))
            pl.when(core != half)(lambda: put_out(sent, jnp.bfloat16))


def token_part(d_proj, weight, part):
    proj = weight[:, : d_proj.shape[1]]
    part[...] = dot(d_proj[...], proj, ((1,), (1,))).astype(jnp.bfloat16)


def pair_sum(place, kept, other, total, *blocks):
    chip = place[2]
    total[...] = kept[chip] + other[chip].astype(jnp.float32)
    for step, block in enumerate(blocks):
        at = chip ^ (step + 1)
        block[...] = (kept[at] + other[at].astype(jnp.float32)).astype(jnp.bfloat16)


def square_momenta(place, total, *refs):
    pieces, refs = refs[: SPLIT - 1], refs[SPLIT - 1 :]
    qkv_mom, out_mom, qkv_grad, out_grad, qkv_new, out_new, *refs = refs
    blocks, state = refs[:SPLIT], refs[SPLIT]
    depth, own = out_mom.shape
    whole = sum_pieces([total, *pieces])
    vec_own = depth // SPLIT
    for at in range(SPLIT):
        grad = whole[:depth, at * own : (at + 1) * own]
        if at < SPLIT - 1:
            qkv_grad[at] = grad
            moment = momentum_decay * qkv_mom[at] + grad
            qkv_new[at] = moment
        else:
            out_grad[...] = grad
            moment = momentum_decay * out_mom[...] + grad
            out_new[...] = moment
        state[at, :depth, :] = moment
        state[at, depth:, :] = jnp.zeros((whole.shape[0] - depth, own), jnp.float32)
        state[at, depth:, :vec_own] = whole[depth:, at * vec_own : (at + 1) * vec_own]
    for step, block in enumerate(blocks):
        block[...] = state[lax.rem(place[0] + step, SPLIT)].astype(jnp.bfloat16)


def join_squares(place, *refs):
    pieces, (gram, gram_other, mine, other, sums, rows) = refs[:SPLIT], refs[SPLIT:]
    depth, own = mine.shape[0], pieces[0].shape[1]
    total = jnp.zeros(sums.shape, jnp.float32)
    for step, piece in enumerate(pieces):
        total = total + piece[depth:, :].astype(jnp.float32)
        for at in range(SPLIT):

            @pl.when(source_of(place[0], step) == at)
            def _():
                rows[:, at * own : (at + 1) * own] = piece[:depth, :]

    sums[...] = total
    even = place[1] == 0
    gram_sum = (gram[...].astype(jnp.float32) + gram_other[...].astype(jnp.float32)).astype(jnp.bfloat16)
    mine[...] = jnp.where(even, rows[...], gram_sum)
    other[...] = jnp.where(even, gram_sum, rows[...])


def join_pair(place, mine, other, rows):
    depth = mine.shape[0]
    even = place[1] == 0
    rows[:depth, :] = jnp.where(even, mine[...], other[...])
    rows[depth:, :] = jnp.where(even, other[...], mine[...])


def run_kernel(body, outputs, scalars=0, scratch=(), ties=(), far=(), far_out=(), late=(), lanes={}):
    def call(*operands):
        operands = list(operands)
        count, made = len(operands), len(outputs)

        def whole(*refs):
            inputs, refs = list(refs[:count]), refs[count + len(ties) :]
            results, refs = list(refs[:made]), refs[made:]
            mine, refs = refs[: len(scratch)], refs[len(scratch) :]
            rooms, refs = refs[: len(far)], refs[len(far) :]
            rooms_out, signals = refs[: len(far_out)], refs[len(far_out) :]
            copies = []
            for at, room, signal in zip(far, rooms, signals):
                source = inputs[at].at[:, lanes[at]] if at in lanes else inputs[at]
                copies.append(pltpu.make_async_copy(source, room, signal))
                copies[-1].start()
                inputs[at] = room
            waits = [copy.wait for at, copy in zip(far, copies) if at in late]
            for at, copy in zip(far, copies):
                if at not in late:
                    copy.wait()
            targets = [results[at] for at in far_out]
            for at, room in zip(far_out, rooms_out):
                results[at] = room
            if late:
                body(waits, *inputs, *results, *mine)
            else:
                body(*inputs, *results, *mine)
            copies_out = []
            for room, target, signal in zip(rooms_out, targets, signals[len(far) :]):
                copies_out.append(pltpu.make_async_copy(room, target, signal))
                copies_out[-1].start()
            for copy in copies_out:
                copy.wait()

        rooms = []
        for at in far:
            shape = operands[at].shape
            if at in lanes:
                shape = (shape[0], lanes[at].size)
            rooms.append(pltpu.VMEM(shape, operands[at].dtype))
            operands[at] = pltpu.with_memory_space_constraint(operands[at], pltpu.HBM)
        kinds = list(outputs)
        for at in far_out:
            kinds[at] = pltpu.HBM(kinds[at].shape, kinds[at].dtype)
        spaces = [pltpu.SMEM] * scalars + [pltpu.VMEM] * (count - scalars) + [pl.ANY] * len(ties)
        for at in far:
            spaces[at] = pltpu.HBM
        spaces_out = [pltpu.HBM if at in far_out else pltpu.VMEM for at in range(made)]
        rooms_out = [pltpu.VMEM(outputs[at].shape, outputs[at].dtype) for at in far_out]
        signals = [pltpu.SemaphoreType.DMA] * (len(far) + len(far_out))
        return pl.pallas_call(
            whole,
            out_shape=kinds,
            in_specs=[pl.BlockSpec(memory_space=space) for space in spaces],
            out_specs=[pl.BlockSpec(memory_space=space) for space in spaces_out],
            scratch_shapes=[*scratch, *rooms, *rooms_out, *signals],
            compiler_params=pltpu.CompilerParams(vmem_limit_bytes=24 * 2**20),
        )(*operands, *ties)

    return call


def newton_schulz(waits, place, *refs):
    pieces, refs = refs[:SPLIT], refs[SPLIT:]
    wide, kept, sent, heard, gram, *factors = refs
    chip, core = place[2], place[1]
    width = heard.shape[0]
    for step, piece in enumerate(pieces):
        at = pl.multiple_of((chip ^ step) * piece.shape[0], piece.shape[0])
        heard[pl.ds(at, piece.shape[0]), :] = piece[...]
    depth = kept.shape[0]
    even = core == 0

    @pl.when(even)
    def _():
        gram[...] = dot(heard[...], heard[...], ((1,), (1,)))

    @pl.when(jnp.logical_not(even))
    def _():
        gram[...] = heard[...].astype(jnp.float32)

    at_row = lax.broadcasted_iota(jnp.int32, (width, width), 0)
    at_lane = lax.broadcasted_iota(jnp.int32, (width, width), 1)
    trace = jnp.sum(jnp.where(at_row == at_lane, gram[...], 0.0), keepdims=True)
    scale = jnp.sqrt(trace) + ortho_eps
    gram[...] = gram[...] / (scale * scale)
    count = 2 * depth
    start = pl.multiple_of(chip * count, count)
    for factor in factors:
        gram_b = gram[...].astype(jnp.bfloat16)
        square = dot(gram_b, gram_b, ((1,), (0,)))
        factor[...] = (coef_second * gram[...] + coef_third * square).astype(jnp.bfloat16)
        moved = dot(factor[...], gram_b, ((1,), (0,)))
        twice = dot(factor[...], moved.astype(jnp.bfloat16), ((1,), (0,)))
        gram[...] = coef_first * coef_first * gram[...] + 2.0 * coef_first * moved + twice
    eye = lax.broadcasted_iota(jnp.int32, (count, width), 0) + start
    eye = (eye == lax.broadcasted_iota(jnp.int32, (count, width), 1)).astype(jnp.float32)
    rows = gram[pl.ds(start, count), :]
    square = dot(rows.astype(jnp.bfloat16), gram[...].astype(jnp.bfloat16), ((1,), (0,)))
    rows = coef_first * eye + (coef_second * rows + coef_third * square)
    for factor in factors[::-1]:
        rows = coef_first * rows + dot(rows.astype(jnp.bfloat16), factor[...], ((1,), (0,)))
    waits[0]()
    rows = (rows / scale).astype(jnp.bfloat16)

    @pl.when(even)
    def _():
        state = dot(rows, heard[...], ((1,), (0,))).astype(jnp.bfloat16)
        kept[:, :width] = state[:depth]
        sent[:, :width] = state[depth:]
        kept[:, width:] = jnp.zeros_like(kept[:, width:])
        sent[:, width:] = jnp.zeros_like(sent[:, width:])

    @pl.when(jnp.logical_not(even))
    def _():
        state = dot(rows, wide[...], ((1,), (0,))).astype(jnp.bfloat16)
        kept[...] = state[depth:]
        sent[...] = state[:depth]


def split_device(
    tokens, cotangent, doc_lengths, qkv_w, out_w, ffn_w, vecs, qkv_mom, out_mom, ffn_mom, vec_mom
):
    micro, rows, width = tokens.shape
    shards = lax.axis_size("shard")
    groups = lax.axis_size("dp")
    column = lax.axis_index("shard")
    row = lax.axis_index("dp")
    place = jnp.stack([column, row & 1, row >> 1]).astype(jnp.int32)
    slots = micro * shards
    own = qkv_w.shape[2]
    hidden = ffn_w.shape[2]
    bf16 = jnp.bfloat16

    packed = jnp.concatenate(
        [ffn_w[0], ffn_w[1], qkv_w[0], qkv_w[1], qkv_w[2], jnp.zeros((ffn_w.shape[1], PAD))], axis=1
    ).astype(bf16)
    weights = lax.all_gather(packed, "dp", axis=0, tiled=True)

    flat = tokens.reshape(micro * rows, width)
    vec_rows, vec_own = vecs.shape
    small = jnp.concatenate(
        [vecs.astype(bf16).reshape(-1), doc_lengths.astype(bf16).reshape(-1)]
    )
    small = jnp.pad(small, (0, 8 * width - small.shape[0])).reshape(8, width)
    out_flat = out_w.astype(bf16).reshape(-1, width)
    out_count = out_flat.shape[0]
    heard = gather_direct(jnp.concatenate([flat, out_flat, small], axis=0), "shard")
    tokens_b = heard[:, : micro * rows].reshape(slots * rows, width)
    out_part = heard[:, micro * rows : micro * rows + out_count].reshape(shards, -1, own)
    out_part = out_part.transpose(1, 0, 2).reshape(-1, width)
    small = heard[:, micro * rows + out_count :].reshape(shards, -1)
    lengths = small[:, vecs.size : vecs.size + doc_lengths.size].astype(jnp.int32).reshape(slots, -1)
    small = small[:, : vecs.size].reshape(shards, vec_rows, vec_own).transpose(1, 0, 2).reshape(vec_rows, -1)
    vec = gather_double(small, "dp").transpose(1, 0, 2).reshape(vec_rows, -1).astype(jnp.float32)
    out_b = lax.all_gather(out_part, "dp", axis=0, tiled=True)
    position = jnp.arange(rows, dtype=jnp.int32)[None]
    ends = jnp.cumsum(lengths, axis=1)
    segment = jnp.sum((position[:, :, None] >= ends[:, None, :]).astype(jnp.int32), axis=2)
    valid = position < ends[:, -1:]
    slot = jnp.arange(slots, dtype=jnp.int32)[:, None]
    marks = jnp.where(valid, segment + slot * ends.shape[1], -1 - position - slot * rows)
    id_column, id_row = marks.reshape(-1, 1), marks.reshape(1, -1)
    bias_q = lax.dynamic_slice_in_dim(vec[0], column * own, own, 0)
    bias_v = lax.dynamic_slice_in_dim(vec[1], column * own, own, 0)
    bias_proj = jnp.concatenate([bias_q, jnp.zeros_like(bias_q), bias_v])[None]
    bias_up = lax.dynamic_slice_in_dim(vec[8:].reshape(-1), column * hidden, hidden, 0)[None]

    proj_lanes = pl.ds(2 * hidden, weights.shape[1] - 2 * hidden)
    ffn_lanes = pl.ds(0, 2 * hidden)
    qkv, mixed_own = run_kernel(
        attention_forward,
        [
            jax.ShapeDtypeStruct((slots * rows, 3 * own), bf16),
            jax.ShapeDtypeStruct((BLOCK, slots * rows // BLOCK * own), bf16),
        ],
        scalars=1,
        ties=[vec, bias_up],
        far=(1, 2, 4),
        far_out=(0,),
        lanes={2: proj_lanes},
    )(place, tokens_b, weights, bias_proj, id_column, id_row)

    depth = width // groups
    count = micro * rows
    whole_b = jax.ShapeDtypeStruct((slots * rows, width), bf16)
    own_f = jax.ShapeDtypeStruct((count, width), jnp.float32)
    own_b = jax.ShapeDtypeStruct((count, width), bf16)
    part_kinds = [own_f] + [own_b] * (shards - 1)
    sums_kind = jax.ShapeDtypeStruct((8, width), jnp.float32)
    moving = pltpu.VMEM((slots * rows, width), jnp.float32)

    mixed_pieces = pieces_of(mixed_own, "shard")
    first_b, activ_b, slope, first_in, *parts = run_kernel(
        layer_middle,
        [whole_b, whole_b, jax.ShapeDtypeStruct((slots * rows, hidden), jnp.float32), own_f] + part_kinds,
        scalars=1,
        scratch=[moving],
        far=(5, 6, 8),
        late=(8,),
        lanes={8: ffn_lanes},
    )(place, *mixed_pieces, out_b, tokens_b, vec, weights, bias_up)
    layer_out, d_branch_own, d_second, sums_two = run_kernel(
        second_norm, [own_b, own_b, own_f, sums_kind], scalars=1, far=(7, 8), far_out=(0, 2, 3)
    )(place, *send_parts(parts, "shard"), first_in, vec, cotangent.reshape(count, width), id_column)
    layer_out = layer_out.reshape(tokens.shape)
    d_branch_b, d_inner_b, d_bias_up, *parts = run_kernel(
        inner_backward,
        [whole_b, whole_b, jax.ShapeDtypeStruct((1, hidden), jnp.float32)] + part_kinds,
        scalars=1,
        scratch=[moving],
        far=(6,),
        far_out=(2, 3, 4, 5, 6),
        lanes={6: ffn_lanes},
    )(place, *pieces_of(d_branch_own, "shard"), slope, weights)
    (grads,) = run_kernel(inner_gradients, [jax.ShapeDtypeStruct((2, width, hidden), bf16)], far_out=(0,))(
        first_b, activ_b, d_inner_b, d_branch_b
    )
    summed = lax.psum_scatter(grads, "dp", scatter_dimension=1, tiled=True)
    d_first_in, d_attended_own, sums_one = run_kernel(
        first_norm, [own_f, own_b, sums_kind], far=(0, 4, 5), far_out=(0, 1, 2)
    )(*send_parts(parts, "shard"), d_second, first_in, vec)
    d_attended_pieces = pieces_of(d_attended_own, "shard")
    moment_kind = jax.ShapeDtypeStruct(ffn_mom.shape, ffn_mom.dtype)
    wide_kind = jax.ShapeDtypeStruct((depth, hidden), bf16)
    grad_ffn, new_ffn_mom, mine, far_send = run_kernel(
        wide_momenta,
        [moment_kind, moment_kind, wide_kind, wide_kind],
        scalars=1,
        ties=d_attended_pieces[1:],
        far=(1, 2),
        far_out=(0, 1),
    )(place, summed, ffn_mom)
    far_rows = swap(far_send, "shard", shards // 2)

    packed_rows = depth + 16
    kept, sent, d_proj = run_kernel(
        attention_backward,
        [
            jax.ShapeDtypeStruct((groups // 2, packed_rows, width), jnp.float32),
            jax.ShapeDtypeStruct((groups // 2, packed_rows, width), bf16),
            jax.ShapeDtypeStruct((slots * rows, 3 * own), bf16),
        ],
        scalars=1,
        scratch=[pltpu.VMEM((slots * rows, width), bf16), pltpu.VMEM((16, width), jnp.float32)],
        far=(1, 2, 3, 4, 9, 10, 11, 5, 6, 7, 8, 13, 14, 15),
        far_out=(0, 2),
        late=(5, 6, 7, 8, 13, 14, 15),
        ties=[far_send],
    )(
        place, *d_attended_pieces, *mixed_pieces, out_b, qkv, id_column, id_row, tokens_b,
        sums_one, sums_two, d_bias_up,
    )
    (wide_rows,) = run_kernel(
        join_wide, [jax.ShapeDtypeStruct((depth, 2 * hidden), bf16)], ties=[kept], far_out=(0,)
    )(mine, far_rows)
    wide = lax.all_gather(wide_rows, "dp", axis=0, tiled=True)
    block_kind = jax.ShapeDtypeStruct((packed_rows, width), bf16)
    total, *blocks = run_kernel(
        pair_sum, [jax.ShapeDtypeStruct((packed_rows, width), jnp.float32)] + [block_kind] * 3, scalars=1, far=(1,)
    )(place, kept, swap(sent, "dp", 1))
    (part,) = run_kernel(
        token_part, [whole_b], ties=[total], far=(0, 1), far_out=(0,), lanes={1: proj_lanes}
    )(d_proj, weights)
    d_tokens = lax.psum_scatter(part, "shard", scatter_dimension=0, tiled=True)
    d_tokens = d_first_in + d_tokens.astype(jnp.float32)
    block_kind = jax.ShapeDtypeStruct((packed_rows, own), bf16)
    like = [jax.ShapeDtypeStruct(each.shape, each.dtype) for each in (qkv_mom, out_mom)]
    grad_qkv, grad_wout, new_qkv_mom, new_out_mom, *blocks = run_kernel(
        square_momenta,
        like + like + [block_kind] * shards,
        scalars=1,
        scratch=[pltpu.VMEM((shards, packed_rows, own), jnp.float32)],
        far=(5, 6),
        far_out=(0, 1, 2, 3),
    )(place, total, *[swap(block, "dp", 2 * at + 2) for at, block in enumerate(blocks)], qkv_mom, out_mom)
    (gram_rows,) = run_kernel(wide_gram, [jax.ShapeDtypeStruct((depth, width), bf16)], ties=blocks, far=(0, 1))(
        wide_rows, wide
    )
    row_kind = jax.ShapeDtypeStruct((depth, width), bf16)
    mine, other, grad_vec = run_kernel(
        join_squares,
        [row_kind, row_kind, jax.ShapeDtypeStruct((packed_rows - depth, own), jnp.float32)],
        scalars=1,
        scratch=[pltpu.VMEM((depth, width), bf16)],
    )(place, *send_parts(blocks, "shard"), gram_rows, swap(gram_rows, "shard", 1))
    grad_vec = grad_vec[:vec_rows, :vec_own]
    d_tokens = d_tokens.reshape(tokens.shape)
    (pair_rows,) = run_kernel(
        join_pair, [jax.ShapeDtypeStruct((2 * depth, width), bf16)], scalars=1
    )(place, mine, swap(other, "dp", 1))
    pair_pieces = [pair_rows] + [swap(pair_rows, "dp", bit) for bit in (2, 4, 6)]
    state_kind = jax.ShapeDtypeStruct((depth, 2 * hidden), bf16)
    kept, sent = run_kernel(
        newton_schulz,
        [state_kind, state_kind],
        scalars=1,
        scratch=[pltpu.VMEM((width, width), bf16), pltpu.VMEM((width, width), jnp.float32)]
        + [pltpu.VMEM((width, width), bf16)] * (NS_STEPS - 1),
        far=(5,),
        late=(5,),
    )(place, *pair_pieces, wide)
    block_kind = jax.ShapeDtypeStruct((depth, own), bf16)
    wide_kind = jax.ShapeDtypeStruct((depth, hidden), bf16)
    kinds = [block_kind] * shards + [wide_kind]
    kinds[shards // 2] = jax.ShapeDtypeStruct((depth, hidden + own), bf16)
    *blocks, mine = run_kernel(
        split_state, kinds, scalars=1
    )(place, kept, swap(sent, "dp", 1))
    qkv_new, out_new, ffn_new = run_kernel(
        new_weights,
        [jax.ShapeDtypeStruct(each.shape, each.dtype) for each in (qkv_w, out_w, ffn_w)],
        scalars=1,
        scratch=[pltpu.VMEM((shards, depth, own), jnp.float32)],
        far=(6, 7, 8),
        far_out=(0, 1, 2),
    )(
        place, *send_parts(blocks, "shard"), mine, qkv_w, out_w, ffn_w
    )

    token_count = micro * rows * groups * shards
    new_vec_mom = momentum_decay * vec_mom + grad_vec
    vec_new = vecs - vec_rate * token_count ** (-0.5) * new_vec_mom
    return (
        layer_out,
        d_tokens,
        grad_qkv,
        grad_wout,
        grad_ffn,
        grad_vec,
        new_qkv_mom,
        new_out_mom,
        new_ffn_mom,
        new_vec_mom,
        qkv_new,
        out_new,
        ffn_new,
        vec_new,
    )


def solution(mesh):
    fits = (mesh.shape["dp"], mesh.shape["shard"]) == (8, 4)
    in_specs = (
        P(("dp", "shard"), None, None),
        P(("dp", "shard"), None, None),
        P(("dp", "shard"), None),
        P(None, "dp", "shard"),
        P("dp", "shard"),
        P(None, "dp", "shard"),
        P(None, ("dp", "shard")),
        P(None, "dp", "shard"),
        P("dp", "shard"),
        P(None, "dp", "shard"),
        P(None, ("dp", "shard")),
    )
    out_specs = (
        P(("dp", "shard"), None, None),
        P(("dp", "shard"), None, None),
        P(None, "dp", "shard"),
        P("dp", "shard"),
        P(None, "dp", "shard"),
        P(None, ("dp", "shard")),
        P(None, "dp", "shard"),
        P("dp", "shard"),
        P(None, "dp", "shard"),
        P(None, ("dp", "shard")),
        P(None, "dp", "shard"),
        P("dp", "shard"),
        P(None, "dp", "shard"),
        P(None, ("dp", "shard")),
    )
    return jax.shard_map(
        split_device if fits else per_device, mesh=mesh, in_specs=in_specs, out_specs=out_specs, check_vma=False
    )
```

```python
import math
import jax
import jax.numpy as jnp
from jax import lax
from jax.experimental import pallas as pl
from jax.experimental.pallas import tpu as pltpu
from jax.sharding import PartitionSpec as P

D = 768
HEADS = 12
HEAD = 64
FF = 3072
NS_STEPS = 3


masked_score = -1e30
norm_eps = 1e-12
momentum_decay = 0.9
muon_rate = 0.8
vec_rate = 0.5
coef_first = 3.4445
coef_second = -4.775
coef_third = 2.0315
ortho_eps = 1e-07


def spread_2(block, axis, owner):
    block = jnp.where(lax.axis_index(axis) == owner, block, jnp.zeros_like(block))
    return lax.psum(block, axis)


def segments(lengths, rows):
    position = jnp.arange(rows, dtype=jnp.int32)
    ends = jnp.cumsum(lengths)
    segment = jnp.sum((position[:, None] >= ends[None, :]).astype(jnp.int32), axis=1)
    valid = position < ends[-1]
    same = segment[:, None] == segment[None, :]
    allowed = same & valid[:, None] | (position[:, None] == position[None, :])
    return (valid, allowed)


def layer_norm(inputs, gain, bias):
    center = inputs - jnp.mean(inputs, axis=-1, keepdims=True)
    spread = jnp.mean(center * center, axis=-1, keepdims=True)
    return center * lax.rsqrt(spread + norm_eps) * gain + bias


def gelu_exact(inputs):
    return jax.nn.gelu(inputs, approximate=False)


def split_heads(matrix):
    return matrix.reshape(matrix.shape[0], HEADS, HEAD)


def gather_weights(qkv_w, out_w, ffn_w, vecs):
    pieces = (
        qkv_w.astype(jnp.bfloat16),
        out_w.astype(jnp.bfloat16),
        ffn_w.astype(jnp.bfloat16),
        vecs.astype(jnp.bfloat16),
    )
    across = (
        lax.all_gather(pieces[0], "shard", axis=2, tiled=True),
        lax.all_gather(pieces[1], "shard", axis=1, tiled=True),
        lax.all_gather(pieces[2], "shard", axis=2, tiled=True),
        lax.all_gather(pieces[3], "shard", axis=1, tiled=True),
    )
    return (
        lax.all_gather(across[0], "dp", axis=1, tiled=True),
        lax.all_gather(across[1], "dp", axis=0, tiled=True),
        lax.all_gather(across[2], "dp", axis=1, tiled=True),
        lax.all_gather(across[3], "dp", axis=1, tiled=True),
    )


def attention_scores(queries_b, keys_b, allowed):
    scores = jnp.einsum(
        "qhd,khd->hqk",
        split_heads(queries_b),
        split_heads(keys_b),
        preferred_element_type=jnp.float32,
    )
    return jnp.where(allowed[None], scores * HEAD ** (-0.5), masked_score)


def forward_pass(tokens_b, lengths, weights):
    qkv_b, out_b, ffn_b, vec_b = weights
    vec = vec_b.astype(jnp.float32)
    rows = tokens_b.shape[0]
    valid, allowed = segments(lengths, rows)
    projected = jnp.einsum("rd,kde->kre", tokens_b, qkv_b, preferred_element_type=jnp.float32)
    queries_b = (projected[0] + vec[0]).astype(jnp.bfloat16)
    keys_b = projected[1].astype(jnp.bfloat16)
    values_b = (projected[2] + vec[1]).astype(jnp.bfloat16)
    scores = attention_scores(queries_b, keys_b, allowed)
    largest = jnp.max(scores, axis=-1, keepdims=True)
    exponent = jnp.exp(scores - largest)
    totals = jnp.sum(exponent, axis=-1, keepdims=True)
    logsum = largest + jnp.log(totals)
    probs_b = (exponent / totals).astype(jnp.bfloat16)
    mixed = jnp.einsum(
        "hqk,khd->qhd", probs_b, split_heads(values_b), preferred_element_type=jnp.float32
    )
    mixed_b = mixed.reshape(rows, -1).astype(jnp.bfloat16)
    attended = jnp.dot(mixed_b, out_b, preferred_element_type=jnp.float32) + vec[2]
    first_in = tokens_b.astype(jnp.float32) + attended
    first = layer_norm(first_in, vec[3], vec[4])
    first_b = first.astype(jnp.bfloat16)
    inner = jnp.dot(first_b, ffn_b[0], preferred_element_type=jnp.float32) + vec[8:].reshape(-1)
    activ_b = gelu_exact(inner).astype(jnp.bfloat16)
    branch = jnp.einsum("rf,df->rd", activ_b, ffn_b[1], preferred_element_type=jnp.float32) + vec[5]
    second_in = first + branch
    result = layer_norm(second_in, vec[6], vec[7]) * valid[:, None].astype(jnp.float32)
    kept = (
        queries_b,
        keys_b,
        values_b,
        logsum,
        mixed_b,
        first_in,
        first_b,
        inner,
        activ_b,
        second_in,
    )
    return (result.astype(jnp.bfloat16), kept)


def backward_pass(cot_b, tokens_b, lengths, weights, kept):
    qkv_b, out_b, ffn_b, vec_b = weights
    vec = vec_b.astype(jnp.float32)
    queries_b, keys_b, values_b, logsum, mixed_b, first_in, first_b, inner, activ_b, second_in = (
        kept
    )
    rows = tokens_b.shape[0]
    valid, allowed = segments(lengths, rows)
    grad_out = cot_b.astype(jnp.float32) * valid[:, None].astype(jnp.float32)
    unused, pull_two = jax.vjp(layer_norm, second_in, vec[6], vec[7])
    d_second, d_gain_two, d_shift_two = pull_two(grad_out)
    d_branch_b = d_second.astype(jnp.bfloat16)
    d_bias_down = jnp.sum(d_branch_b.astype(jnp.float32), axis=0)
    d_activ = jnp.dot(d_branch_b, ffn_b[1], preferred_element_type=jnp.float32)
    unused, pull_gelu = jax.vjp(gelu_exact, inner)
    (d_inner,) = pull_gelu(d_activ)
    d_inner_b = d_inner.astype(jnp.bfloat16)
    d_bias_up = jnp.sum(d_inner_b.astype(jnp.float32), axis=0)
    d_first = d_second + jnp.einsum(
        "rf,df->rd", d_inner_b, ffn_b[0], preferred_element_type=jnp.float32
    )
    unused, pull_one = jax.vjp(layer_norm, first_in, vec[3], vec[4])
    d_first_in, d_gain_one, d_shift_one = pull_one(d_first)
    d_attended_b = d_first_in.astype(jnp.bfloat16)
    d_bias_out = jnp.sum(d_attended_b.astype(jnp.float32), axis=0)
    d_mixed_b = jnp.einsum(
        "re,de->rd", d_attended_b, out_b, preferred_element_type=jnp.float32
    ).astype(jnp.bfloat16)
    scores = attention_scores(queries_b, keys_b, allowed)
    probs = jnp.exp(scores - logsum)
    mixed_heads = split_heads(d_mixed_b)
    d_probs = jnp.einsum(
        "qhd,khd->hqk", mixed_heads, split_heads(values_b), preferred_element_type=jnp.float32
    )
    d_values = jnp.einsum(
        "hqk,qhd->khd", probs.astype(jnp.bfloat16), mixed_heads, preferred_element_type=jnp.float32
    )
    d_scores_b = (probs * (d_probs - jnp.sum(probs * d_probs, axis=-1, keepdims=True))).astype(
        jnp.bfloat16
    )
    d_queries = jnp.einsum(
        "hqk,khd->qhd", d_scores_b, split_heads(keys_b), preferred_element_type=jnp.float32
    ) * HEAD ** (-0.5)
    d_keys = jnp.einsum(
        "hqk,qhd->khd", d_scores_b, split_heads(queries_b), preferred_element_type=jnp.float32
    ) * HEAD ** (-0.5)
    d_proj_b = jnp.stack([d_queries, d_keys, d_values]).reshape(3, rows, -1).astype(jnp.bfloat16)
    d_tokens = d_first_in + jnp.einsum(
        "kre,kde->rd", d_proj_b, qkv_b, preferred_element_type=jnp.float32
    )
    proj_sums = jnp.sum(d_proj_b.astype(jnp.float32), axis=1)
    grad_vec = jnp.concatenate(
        [
            jnp.stack(
                [
                    proj_sums[0],
                    proj_sums[2],
                    d_bias_out,
                    d_gain_one,
                    d_shift_one,
                    d_bias_down,
                    d_gain_two,
                    d_shift_two,
                ]
            ),
            d_bias_up.reshape(-1, vec.shape[1]),
        ],
        axis=0,
    )
    factors = (d_branch_b, activ_b, first_b, d_inner_b, mixed_b, d_attended_b, d_proj_b)
    return (d_tokens, factors, grad_vec)


def orthogonalize_pair(square, wide):
    matrices = (square, wide)
    present = tuple((matrix.astype(jnp.bfloat16) for matrix in matrices))
    states = matrices
    for step in range(NS_STEPS):
        partial_value = tuple(
            (
                jnp.einsum("iw,jw->ij", block, block, preferred_element_type=jnp.float32)
                for block in present
            )
        )
        gram_part = (
            lax.psum_scatter(
                partial_value[0].astype(jnp.bfloat16), "shard", scatter_dimension=0, tiled=True
            ).astype(jnp.float32),
            lax.psum_scatter(
                partial_value[1].astype(jnp.bfloat16), "shard", scatter_dimension=0, tiled=True
            ).astype(jnp.float32),
        )
        grams = (
            lax.all_gather(gram_part[0].astype(jnp.bfloat16), "shard", axis=0, tiled=True).astype(
                jnp.float32
            ),
            lax.all_gather(gram_part[1].astype(jnp.bfloat16), "shard", axis=0, tiled=True).astype(
                jnp.float32
            ),
        )
        if step == 0:
            scales = tuple((jnp.sqrt(jnp.trace(gram)) + ortho_eps for gram in grams))
            grams = tuple((gram / (scale * scale) for gram, scale in zip(grams, scales)))
            present = tuple(
                ((matrix / scale).astype(jnp.bfloat16) for matrix, scale in zip(matrices, scales))
            )
        renewed = []
        for gram, current in zip(grams, present):
            gram_b = gram.astype(jnp.bfloat16)
            once = jnp.dot(gram_b, current, preferred_element_type=jnp.float32)
            twice = jnp.dot(gram_b, once.astype(jnp.bfloat16), preferred_element_type=jnp.float32)
            renewed.append(
                coef_first * current.astype(jnp.float32) + coef_second * once + coef_third * twice
            )
        states = tuple(renewed)
        present = tuple((state.astype(jnp.bfloat16) for state in states))
    return states


def per_device(
    tokens, cotangent, doc_lengths, qkv_w, out_w, ffn_w, vecs, qkv_mom, out_mom, ffn_mom, vec_mom
):
    micro = tokens.shape[0]
    shared = gather_weights(qkv_w, out_w, ffn_w, vecs)
    outputs = []
    stored = []
    for index in range(micro):
        weights = shared
        result_b, kept = forward_pass(tokens[index], doc_lengths[index], weights)
        outputs.append(result_b)
        stored.append(kept)
    grad_rows = [None] * micro
    factor_list = [None] * micro
    vec_total = None
    for index in reversed(range(micro)):
        weights = shared
        d_tokens, factors, vec_part = backward_pass(
            cotangent[index], tokens[index], doc_lengths[index], weights, stored[index]
        )
        grad_rows[index] = d_tokens
        factor_list[index] = factors
        vec_total = vec_part if vec_total is None else vec_total + vec_part
    (
        branch_gradient_rows,
        activation_rows,
        first_norm_rows,
        inner_gradient_rows,
        mixed_all,
        d_attended_all,
        d_proj_all,
    ) = [jnp.stack([factors[place] for factors in factor_list]) for place in range(7)]
    grad_down = jnp.einsum(
        "hzo,hzx->ox", branch_gradient_rows, activation_rows, preferred_element_type=jnp.float32
    )
    up_weight_gradient = jnp.einsum(
        "hzo,hzx->ox", first_norm_rows, inner_gradient_rows, preferred_element_type=jnp.float32
    )
    grad_wout_sum = jnp.einsum(
        "mrd,mre->de", mixed_all, d_attended_all, preferred_element_type=jnp.float32
    )
    grad_qkv_sum = jnp.einsum(
        "mrd,mkre->kde", tokens, d_proj_all, preferred_element_type=jnp.float32
    )
    summed = (grad_qkv_sum, grad_wout_sum, jnp.stack([up_weight_gradient, grad_down]), vec_total)
    reduced = (
        lax.psum_scatter(
            summed[0].astype(jnp.bfloat16), "dp", scatter_dimension=1, tiled=True
        ).astype(jnp.float32),
        lax.psum_scatter(
            summed[1].astype(jnp.bfloat16), "dp", scatter_dimension=0, tiled=True
        ).astype(jnp.float32),
        lax.psum_scatter(
            summed[2].astype(jnp.bfloat16), "dp", scatter_dimension=1, tiled=True
        ).astype(jnp.float32),
        lax.psum_scatter(
            summed[3].astype(jnp.bfloat16), "dp", scatter_dimension=1, tiled=True
        ).astype(jnp.float32),
    )
    grad_qkv, grad_wout, grad_ffn, grad_vec = (
        lax.psum_scatter(
            reduced[0].astype(jnp.bfloat16), "shard", scatter_dimension=2, tiled=True
        ).astype(jnp.float32),
        lax.psum_scatter(
            reduced[1].astype(jnp.bfloat16), "shard", scatter_dimension=1, tiled=True
        ).astype(jnp.float32),
        lax.psum_scatter(
            reduced[2].astype(jnp.bfloat16), "shard", scatter_dimension=2, tiled=True
        ).astype(jnp.float32),
        lax.psum_scatter(
            reduced[3].astype(jnp.bfloat16), "shard", scatter_dimension=1, tiled=True
        ).astype(jnp.float32),
    )
    new_qkv_mom = momentum_decay * qkv_mom + grad_qkv
    new_out_mom = momentum_decay * out_mom + grad_wout
    new_ffn_mom = momentum_decay * ffn_mom + grad_ffn
    square_local = jnp.concatenate([new_qkv_mom, new_out_mom[None]], axis=0)
    square_cols, wide_cols = (
        lax.all_gather(square_local.astype(jnp.bfloat16), "dp", axis=1, tiled=True).astype(
            square_local.dtype
        ),
        lax.all_gather(new_ffn_mom.astype(jnp.bfloat16), "dp", axis=1, tiled=True).astype(
            new_ffn_mom.dtype
        ),
    )
    row = lax.axis_index("dp")
    rows_count = lax.axis_size("dp")
    owners = [place * rows_count // 6 for place in range(6)]
    square_pick = sum(((row == owners[place]).astype(jnp.int32) * place for place in range(4)))
    wide_pick = (row == owners[5]).astype(jnp.int32)
    square_state, wide_state = orthogonalize_pair(
        lax.dynamic_index_in_dim(square_cols, square_pick, 0, keepdims=False),
        lax.dynamic_index_in_dim(wide_cols, wide_pick, 0, keepdims=False),
    )
    depth = qkv_w.shape[1]
    square_rows = []
    for place in range(4):
        whole = spread_2(square_state.astype(jnp.bfloat16), "dp", owners[place]).astype(
            square_state.dtype
        )
        square_rows.append(lax.dynamic_slice_in_dim(whole, row * depth, depth, 0))
    wide_rows = []
    for place in range(4, 6):
        whole = spread_2(wide_state.astype(jnp.bfloat16), "dp", owners[place]).astype(
            wide_state.dtype
        )
        wide_rows.append(lax.dynamic_slice_in_dim(whole, row * depth, depth, 0))
    qkv_new = qkv_w - muon_rate * jnp.stack(square_rows[:3])
    out_new = out_w - muon_rate * square_rows[3]
    ffn_new = ffn_w - muon_rate * (FF / D) ** 0.5 * jnp.stack(wide_rows)
    token_count = tokens.shape[0] * tokens.shape[1] * lax.axis_size("dp") * lax.axis_size("shard")
    new_vec_mom = momentum_decay * vec_mom + grad_vec
    vec_new = vecs - vec_rate * token_count ** (-0.5) * new_vec_mom
    return (
        jnp.stack(outputs),
        jnp.stack(grad_rows),
        grad_qkv,
        grad_wout,
        grad_ffn,
        grad_vec,
        new_qkv_mom,
        new_out_mom,
        new_ffn_mom,
        new_vec_mom,
        qkv_new,
        out_new,
        ffn_new,
        vec_new,
    )


def gather_direct(block, axis):
    count = lax.axis_size(axis)
    me = lax.axis_index(axis)
    whole = jnp.zeros((count,) + block.shape, block.dtype)
    whole = lax.dynamic_update_index_in_dim(whole, block, me, 0)
    for step in range(1, count):
        got = lax.ppermute(block, axis, [(i, (i + step) % count) for i in range(count)])
        whole = lax.dynamic_update_index_in_dim(whole, got, lax.rem(me - step + count, count), 0)
    return whole


def pieces_of(block, axis):
    count = lax.axis_size(axis)
    return [block] + [
        lax.ppermute(block, axis, [(i, (i + step) % count) for i in range(count)])
        for step in range(1, count)
    ]


def send_parts(parts, axis):
    count = lax.axis_size(axis)
    return [parts[0]] + [
        lax.ppermute(parts[step], axis, [(i, (i + step) % count) for i in range(count)])
        for step in range(1, count)
    ]


def swap(block, axis, bit):
    return lax.ppermute(block, axis, [(i, i ^ bit) for i in range(lax.axis_size(axis))])


def gather_double(block, axis):
    me = lax.axis_index(axis)
    bit = 1
    whole = block[None]
    while bit < lax.axis_size(axis):
        other = swap(whole, axis, bit)
        high = (me & bit) != 0
        whole = jnp.concatenate(
            [jnp.where(high, other, whole), jnp.where(high, whole, other)], axis=0
        )
        bit *= 2
    return whole


def dot(left, right, dims):
    return lax.dot_general(left, right, (dims, ((), ())), preferred_element_type=jnp.float32)


def norm_parts(inputs):
    center = inputs - jnp.mean(inputs, axis=-1, keepdims=True)
    spread = jnp.mean(center * center, axis=-1, keepdims=True)
    scale = lax.rsqrt(spread + norm_eps)
    return center * scale, scale


def norm_back(grad, unit, scale, gain):
    scaled = grad * gain
    mean_grad = jnp.mean(scaled, axis=-1, keepdims=True)
    mean_unit = jnp.mean(scaled * unit, axis=-1, keepdims=True)
    return scale * (scaled - mean_grad - unit * mean_unit)


BLOCK = 256
PAD = 64
SPLIT = 4


def source_of(column, step):
    return lax.rem(column - step + SPLIT, SPLIT)


def put_pieces(pieces, column, whole):
    count = pieces[0].shape[0]
    for step, piece in enumerate(pieces):
        at = pl.multiple_of(source_of(column, step) * count, count)
        whole[pl.ds(at, count), :] = piece[...]


def take_parts(whole, column, parts):
    count = parts[0].shape[0]
    for step, part in enumerate(parts):
        at = pl.multiple_of(lax.rem(column + step, SPLIT) * count, count)
        part[...] = whole[pl.ds(at, count), :].astype(part.dtype)


def sum_pieces(pieces):
    total = pieces[0][...]
    for piece in pieces[1:]:
        total = total + piece[...].astype(jnp.float32)
    return total


def row_sums(values):
    return jnp.sum(values, axis=0, keepdims=True)


def unpack_rows(piece, rows):
    count = rows // piece.shape[0]
    own = piece.shape[1] // count
    return jnp.concatenate([piece[:, at * own : (at + 1) * own] for at in range(count)], axis=0)


def layer_middle(waits, place, *refs):
    pieces, refs = refs[:SPLIT], refs[SPLIT:]
    out_weight, tokens, vec, weights, bias_up, first_b, activ_b, slope, first_in, *refs = refs
    parts, (moving,) = refs[:SPLIT], refs[SPLIT:]
    column = place[0]
    attended = vec[2:3, :] + tokens[...].astype(jnp.float32)
    for step, piece in enumerate(pieces):
        rows = unpack_rows(piece, tokens.shape[0])
        own = rows.shape[1]
        at = pl.multiple_of(source_of(column, step) * own, own)
        attended = attended + dot(rows, out_weight[pl.ds(at, own), :], ((1,), (0,)))
    moving[...] = attended
    take_parts(moving, column, [first_in])
    unit, scale = norm_parts(attended)
    first_b[...] = (unit * vec[3:4, :] + vec[4:5, :]).astype(jnp.bfloat16)
    hidden = slope.shape[1]
    waits[0]()
    inner = dot(first_b[...], weights[:, :hidden], ((1,), (0,))) + bias_up[...]
    cdf = 0.5 * (1.0 + lax.erf(inner * 2.0 ** (-0.5)))
    activ_b[...] = (inner * cdf).astype(jnp.bfloat16)
    slope[...] = cdf + inner * jnp.exp(-0.5 * inner * inner) * (2.0 * math.pi) ** (-0.5)
    moving[...] = dot(activ_b[...], weights[:, hidden : 2 * hidden], ((1,), (1,)))
    take_parts(moving, column, parts)


def second_norm(place, *refs):
    pieces, refs = refs[:SPLIT], refs[SPLIT:]
    first_in, vec, cotangent, ids, layer_out, d_branch, d_second, sums = refs
    count = first_in.shape[0]
    at = pl.multiple_of(place[0] * count, count)
    valid = (ids[pl.ds(at, count), :] >= 0).astype(jnp.float32)
    unit, scale = norm_parts(first_in[...])
    first = unit * vec[3:4, :] + vec[4:5, :]
    unit, scale = norm_parts(first + (sum_pieces(pieces) + vec[5:6, :]))
    layer_out[...] = ((unit * vec[6:7, :] + vec[7:8, :]) * valid).astype(jnp.bfloat16)
    grad = cotangent[...].astype(jnp.float32) * valid
    d_rows = norm_back(grad, unit, scale, vec[6:7, :])
    d_second[...] = d_rows
    d_branch[...] = d_rows.astype(jnp.bfloat16)
    sums[0:1, :] = row_sums(d_branch[...].astype(jnp.float32))
    sums[1:2, :] = row_sums(grad * unit)
    sums[2:3, :] = row_sums(grad)


def inner_backward(place, *refs):
    pieces, refs = refs[:SPLIT], refs[SPLIT:]
    slope, weights, d_branch, d_inner, sums, *refs = refs
    parts, (moving,) = refs[:SPLIT], refs[SPLIT:]
    column = place[0]
    put_pieces(pieces, column, d_branch)
    hidden = slope.shape[1]
    d_activ = dot(d_branch[...], weights[:, hidden : 2 * hidden], ((1,), (0,)))
    d_inner[...] = (d_activ * slope[...]).astype(jnp.bfloat16)
    sums[...] = row_sums(d_inner[...].astype(jnp.float32))
    moving[...] = dot(d_inner[...], weights[:, :hidden], ((1,), (1,)))
    take_parts(moving, column, parts)


def inner_gradients(first_b, activ_b, d_inner, d_branch, grads):
    grads[0] = dot(first_b[...], d_inner[...], ((0,), (0,))).astype(jnp.bfloat16)
    grads[1] = dot(d_branch[...], activ_b[...], ((0,), (0,))).astype(jnp.bfloat16)


def wide_momenta(place, summed, moments, grads, moments_new, mine, far):
    low = place[0] < SPLIT // 2
    for part in range(2):
        grads[part] = summed[part].astype(jnp.float32)
        moments_new[part] = momentum_decay * moments[part] + grads[part]
    first, second = moments_new[0].astype(jnp.bfloat16), moments_new[1].astype(jnp.bfloat16)
    mine[...] = jnp.where(low, first, second)
    far[...] = jnp.where(low, second, first)


def join_wide(mine, far, rows):
    hidden = mine.shape[1]
    rows[:, :hidden] = mine[...]
    rows[:, hidden:] = far[...]


def wide_gram(rows, wide, gram):
    gram[...] = dot(rows[...], wide[...], ((1,), (1,))).astype(jnp.bfloat16)


def first_norm(*refs):
    pieces, refs = refs[:SPLIT], refs[SPLIT:]
    d_second, first_in, vec, d_first_in, d_attended, sums = refs
    unit, scale = norm_parts(first_in[...])
    grad = sum_pieces(pieces) + d_second[...]
    d_rows = norm_back(grad, unit, scale, vec[3:4, :])
    d_first_in[...] = d_rows
    d_attended[...] = d_rows.astype(jnp.bfloat16)
    sums[0:1, :] = row_sums(d_attended[...].astype(jnp.float32))
    sums[1:2, :] = row_sums(grad * unit)
    sums[2:3, :] = row_sums(grad)


def split_state(place, kept, other, *refs):
    blocks, (mine,) = refs[:SPLIT], refs[SPLIT:]
    column, even = place[0], place[1] == 0
    own, hidden = blocks[0].shape[1], mine.shape[1]
    far = blocks[SPLIT // 2]
    for step, block in enumerate(blocks):
        there = lax.rem(column + step, SPLIT)
        for at in range(SPLIT):
            lanes = slice(at * own, (at + 1) * own)

            @pl.when(there == at)
            def _():
                block[:, block.shape[1] - own :] = jnp.where(even, kept[:, lanes], other[:, lanes])

    mine[...] = jnp.where(even, other[:, :hidden], kept[:, :hidden])
    far[:, :hidden] = jnp.where(even, other[:, hidden:], kept[:, hidden:])


def new_weights(place, *refs):
    pieces, refs = refs[:SPLIT], refs[SPLIT:]
    mine, qkv_w, out_w, ffn_w, qkv_new, out_new, ffn_new, state = refs
    low = place[0] < SPLIT // 2
    own, hidden = out_w.shape[1], mine.shape[1]
    far = pieces[SPLIT // 2][:, :hidden]
    for step, piece in enumerate(pieces):
        state[source_of(place[0], step)] = piece[:, piece.shape[1] - own :].astype(jnp.float32)
    for at in range(SPLIT - 1):
        qkv_new[at] = qkv_w[at] - muon_rate * state[at]
    out_new[...] = out_w[...] - muon_rate * state[SPLIT - 1]
    rate = muon_rate * (FF / D) ** 0.5
    ffn_new[0] = ffn_w[0] - rate * jnp.where(low, mine[...], far).astype(jnp.float32)
    ffn_new[1] = ffn_w[1] - rate * jnp.where(low, far, mine[...]).astype(jnp.float32)


def probabilities(qkv, rows_at, head, own, id_column, id_row):
    queries = qkv[rows_at, head * HEAD : (head + 1) * HEAD]
    keys = qkv[rows_at, own + head * HEAD : own + (head + 1) * HEAD]
    values = qkv[rows_at, 2 * own + head * HEAD : 2 * own + (head + 1) * HEAD]
    scores = dot(queries, keys, ((1,), (1,))) * HEAD ** (-0.5)
    scores = jnp.where(id_column[rows_at, :] == id_row[:, rows_at], scores, masked_score)
    exponent = jnp.exp(scores - jnp.max(scores, axis=-1, keepdims=True))
    probs = exponent / jnp.sum(exponent, axis=-1, keepdims=True)
    return queries, keys, values, probs


def attention_forward(place, tokens, weight, bias, id_column, id_row, qkv, mixed):
    own = qkv.shape[1] // 3
    proj = weight[:, : 3 * own]
    qkv[...] = (dot(tokens[...], proj, ((1,), (0,))) + bias[...]).astype(jnp.bfloat16)
    for start in range(0, tokens.shape[0], BLOCK):
        rows_at = slice(start, start + BLOCK)
        for head in range(own // HEAD):
            queries, keys, values, probs = probabilities(qkv, rows_at, head, own, id_column, id_row)
            part = dot(probs.astype(jnp.bfloat16), values, ((1,), (0,)))
            at = start // BLOCK * own + head * HEAD
            mixed[:, at : at + HEAD] = part.astype(jnp.bfloat16)


def attention_backward(place, *refs):
    pieces, refs = refs[:SPLIT], refs[SPLIT:]
    out_weight, qkv, id_column, id_row, d_proj, d_columns, d_attended = refs
    rows = qkv.shape[0]
    own = qkv.shape[1] // 3
    column = place[0]
    put_pieces(pieces, column, d_attended)
    out_rows = out_weight[pl.ds(pl.multiple_of(column * own, own), own), :]
    d_mixed = dot(d_attended[...], out_rows, ((1,), (1,))).astype(jnp.bfloat16)
    for start in range(0, rows, BLOCK):
        rows_at = slice(start, start + BLOCK)
        for head in range(own // HEAD):
            queries, keys, values, probs = probabilities(qkv, rows_at, head, own, id_column, id_row)
            d_out = d_mixed[rows_at, head * HEAD : (head + 1) * HEAD]
            d_probs = dot(d_out, values, ((1,), (1,)))
            d_scores = probs * (d_probs - jnp.sum(probs * d_probs, axis=-1, keepdims=True))
            d_scores = d_scores.astype(jnp.bfloat16)
            d_values = dot(probs.astype(jnp.bfloat16), d_out, ((0,), (0,)))
            d_queries = dot(d_scores, keys, ((1,), (0,))) * HEAD ** (-0.5)
            d_keys = dot(d_scores, queries, ((0,), (0,))) * HEAD ** (-0.5)
            for part, value in enumerate((d_queries, d_keys, d_values)):
                at = part * own + head * HEAD
                d_proj[rows_at, at : at + HEAD] = value.astype(jnp.bfloat16)
    for at in range(SPLIT):

        @pl.when(column == at)
        def _():
            d_columns[...] = d_attended[:, at * own : (at + 1) * own]


def square_gradients(place, *refs):
    mixed, refs = refs[:SPLIT], refs[SPLIT:]
    tokens, d_proj, d_columns, sums_one, sums_two, sums_up, kept, sent, sums = refs
    rows, width = tokens.shape
    own = d_columns.shape[1]
    column, core = place[0], place[1]
    d_proj_all = d_proj[...]
    grad_proj = dot(tokens[...], d_proj_all, ((0,), (0,)))
    proj_sums = row_sums(d_proj_all.astype(jnp.float32))
    sums[...] = jnp.zeros_like(sums)
    for at in range(SPLIT):
        lanes = slice(at * own, (at + 1) * own)
        mine = (column == at).astype(jnp.float32)
        sums[0:1, lanes] = proj_sums[:, :own] * mine
        sums[1:2, lanes] = proj_sums[:, 2 * own :] * mine
        sums[8 + at : 9 + at, :] = sums_up[...] * mine
    sums[2:5, :] = sums_one[0:3, :]
    sums[5:8, :] = sums_two[0:3, :]
    depth = kept.shape[1] - sums.shape[0]
    for group in range(width // depth):
        at = slice(group * depth, (group + 1) * depth)

        def put(target, kind):
            target[group // 2, :depth, : 3 * own] = grad_proj[at].astype(kind)
            target[group // 2, depth:, :] = jnp.zeros((sums.shape[0], width), kind)
            target[group // 2, depth:, :depth] = sums[:, at].astype(kind)

        pl.when(core == group % 2)(lambda: put(kept, jnp.float32))
        pl.when(core != group % 2)(lambda: put(sent, jnp.bfloat16))
    for step, piece in enumerate(mixed):
        grad_out = dot(unpack_rows(piece, rows), d_columns[...], ((0,), (0,)))
        source = source_of(column, step)
        for half in range(2):
            block = grad_out[half * depth : (half + 1) * depth]

            def put_out(target, kind):
                target[source, :depth, 3 * own :] = block.astype(kind)

            pl.when(core == half)(lambda: put_out(kept, jnp.float32))
            pl.when(core != half)(lambda: put_out(sent, jnp.bfloat16))


def token_part(d_proj, weight, part):
    proj = weight[:, : d_proj.shape[1]]
    part[...] = dot(d_proj[...], proj, ((1,), (1,))).astype(jnp.bfloat16)


def pair_sum(place, kept, other, total, *blocks):
    chip = place[2]
    total[...] = kept[chip] + other[chip].astype(jnp.float32)
    for step, block in enumerate(blocks):
        at = chip ^ (step + 1)
        block[...] = (kept[at] + other[at].astype(jnp.float32)).astype(jnp.bfloat16)


def square_momenta(place, total, *refs):
    pieces, refs = refs[: SPLIT - 1], refs[SPLIT - 1 :]
    qkv_mom, out_mom, qkv_grad, out_grad, qkv_new, out_new, *refs = refs
    blocks, state = refs[:SPLIT], refs[SPLIT]
    depth, own = out_mom.shape
    whole = sum_pieces([total, *pieces])
    vec_own = depth // SPLIT
    for at in range(SPLIT):
        grad = whole[:depth, at * own : (at + 1) * own]
        if at < SPLIT - 1:
            qkv_grad[at] = grad
            moment = momentum_decay * qkv_mom[at] + grad
            qkv_new[at] = moment
        else:
            out_grad[...] = grad
            moment = momentum_decay * out_mom[...] + grad
            out_new[...] = moment
        state[at, :depth, :] = moment
        state[at, depth:, :] = jnp.zeros((whole.shape[0] - depth, own), jnp.float32)
        state[at, depth:, :vec_own] = whole[depth:, at * vec_own : (at + 1) * vec_own]
    for step, block in enumerate(blocks):
        block[...] = state[lax.rem(place[0] + step, SPLIT)].astype(jnp.bfloat16)


def join_squares(place, *refs):
    pieces, (gram, gram_other, mine, other, sums, rows) = refs[:SPLIT], refs[SPLIT:]
    depth, own = mine.shape[0], pieces[0].shape[1]
    total = jnp.zeros(sums.shape, jnp.float32)
    for step, piece in enumerate(pieces):
        total = total + piece[depth:, :].astype(jnp.float32)
        for at in range(SPLIT):

            @pl.when(source_of(place[0], step) == at)
            def _():
                rows[:, at * own : (at + 1) * own] = piece[:depth, :]

    sums[...] = total
    even = place[1] == 0
    gram_sum = (gram[...].astype(jnp.float32) + gram_other[...].astype(jnp.float32)).astype(jnp.bfloat16)
    mine[...] = jnp.where(even, rows[...], gram_sum)
    other[...] = jnp.where(even, gram_sum, rows[...])


def join_pair(place, mine, other, rows):
    depth = mine.shape[0]
    even = place[1] == 0
    rows[:depth, :] = jnp.where(even, mine[...], other[...])
    rows[depth:, :] = jnp.where(even, other[...], mine[...])


def run_kernel(body, outputs, scalars=0, scratch=(), ties=(), far=(), far_out=(), late=(), lanes={}):
    def call(*operands):
        operands = list(operands)
        count, made = len(operands), len(outputs)

        def whole(*refs):
            inputs, refs = list(refs[:count]), refs[count + len(ties) :]
            results, refs = list(refs[:made]), refs[made:]
            mine, refs = refs[: len(scratch)], refs[len(scratch) :]
            rooms, refs = refs[: len(far)], refs[len(far) :]
            rooms_out, signals = refs[: len(far_out)], refs[len(far_out) :]
            copies = []
            for at, room, signal in zip(far, rooms, signals):
                source = inputs[at].at[:, lanes[at]] if at in lanes else inputs[at]
                copies.append(pltpu.make_async_copy(source, room, signal))
                copies[-1].start()
                inputs[at] = room
            waits = [copy.wait for at, copy in zip(far, copies) if at in late]
            for at, copy in zip(far, copies):
                if at not in late:
                    copy.wait()
            targets = [results[at] for at in far_out]
            for at, room in zip(far_out, rooms_out):
                results[at] = room
            if late:
                body(waits, *inputs, *results, *mine)
            else:
                body(*inputs, *results, *mine)
            copies_out = []
            for room, target, signal in zip(rooms_out, targets, signals[len(far) :]):
                copies_out.append(pltpu.make_async_copy(room, target, signal))
                copies_out[-1].start()
            for copy in copies_out:
                copy.wait()

        rooms = []
        for at in far:
            shape = operands[at].shape
            if at in lanes:
                shape = (shape[0], lanes[at].size)
            rooms.append(pltpu.VMEM(shape, operands[at].dtype))
            operands[at] = pltpu.with_memory_space_constraint(operands[at], pltpu.HBM)
        kinds = list(outputs)
        for at in far_out:
            kinds[at] = pltpu.HBM(kinds[at].shape, kinds[at].dtype)
        spaces = [pltpu.SMEM] * scalars + [pltpu.VMEM] * (count - scalars) + [pl.ANY] * len(ties)
        for at in far:
            spaces[at] = pltpu.HBM
        spaces_out = [pltpu.HBM if at in far_out else pltpu.VMEM for at in range(made)]
        rooms_out = [pltpu.VMEM(outputs[at].shape, outputs[at].dtype) for at in far_out]
        signals = [pltpu.SemaphoreType.DMA] * (len(far) + len(far_out))
        return pl.pallas_call(
            whole,
            out_shape=kinds,
            in_specs=[pl.BlockSpec(memory_space=space) for space in spaces],
            out_specs=[pl.BlockSpec(memory_space=space) for space in spaces_out],
            scratch_shapes=[*scratch, *rooms, *rooms_out, *signals],
            compiler_params=pltpu.CompilerParams(vmem_limit_bytes=24 * 2**20),
        )(*operands, *ties)

    return call


def newton_schulz(waits, place, *refs):
    pieces, refs = refs[:SPLIT], refs[SPLIT:]
    wide, kept, sent, heard, gram, *factors = refs
    chip, core = place[2], place[1]
    width = heard.shape[0]
    for step, piece in enumerate(pieces):
        at = pl.multiple_of((chip ^ step) * piece.shape[0], piece.shape[0])
        heard[pl.ds(at, piece.shape[0]), :] = piece[...]
    depth = kept.shape[0]
    even = core == 0

    @pl.when(even)
    def _():
        gram[...] = dot(heard[...], heard[...], ((1,), (1,)))

    @pl.when(jnp.logical_not(even))
    def _():
        gram[...] = heard[...].astype(jnp.float32)

    at_row = lax.broadcasted_iota(jnp.int32, (width, width), 0)
    at_lane = lax.broadcasted_iota(jnp.int32, (width, width), 1)
    trace = jnp.sum(jnp.where(at_row == at_lane, gram[...], 0.0), keepdims=True)
    scale = jnp.sqrt(trace) + ortho_eps
    gram[...] = gram[...] / (scale * scale)
    count = 2 * depth
    start = pl.multiple_of(chip * count, count)
    for factor in factors:
        gram_b = gram[...].astype(jnp.bfloat16)
        square = dot(gram_b, gram_b, ((1,), (0,)))
        factor[...] = (coef_second * gram[...] + coef_third * square).astype(jnp.bfloat16)
        moved = dot(factor[...], gram_b, ((1,), (0,)))
        twice = dot(factor[...], moved.astype(jnp.bfloat16), ((1,), (0,)))
        gram[...] = coef_first * coef_first * gram[...] + 2.0 * coef_first * moved + twice
    eye = lax.broadcasted_iota(jnp.int32, (count, width), 0) + start
    eye = (eye == lax.broadcasted_iota(jnp.int32, (count, width), 1)).astype(jnp.float32)
    rows = gram[pl.ds(start, count), :]
    square = dot(rows.astype(jnp.bfloat16), gram[...].astype(jnp.bfloat16), ((1,), (0,)))
    rows = coef_first * eye + (coef_second * rows + coef_third * square)
    for factor in factors[::-1]:
        rows = coef_first * rows + dot(rows.astype(jnp.bfloat16), factor[...], ((1,), (0,)))
    waits[0]()
    rows = (rows / scale).astype(jnp.bfloat16)

    @pl.when(even)
    def _():
        state = dot(rows, heard[...], ((1,), (0,))).astype(jnp.bfloat16)
        kept[:, :width] = state[:depth]
        sent[:, :width] = state[depth:]
        kept[:, width:] = jnp.zeros_like(kept[:, width:])
        sent[:, width:] = jnp.zeros_like(sent[:, width:])

    @pl.when(jnp.logical_not(even))
    def _():
        state = dot(rows, wide[...], ((1,), (0,))).astype(jnp.bfloat16)
        kept[...] = state[depth:]
        sent[...] = state[:depth]


def split_device(
    tokens, cotangent, doc_lengths, qkv_w, out_w, ffn_w, vecs, qkv_mom, out_mom, ffn_mom, vec_mom
):
    micro, rows, width = tokens.shape
    shards = lax.axis_size("shard")
    groups = lax.axis_size("dp")
    column = lax.axis_index("shard")
    row = lax.axis_index("dp")
    place = jnp.stack([column, row & 1, row >> 1]).astype(jnp.int32)
    slots = micro * shards
    own = qkv_w.shape[2]
    hidden = ffn_w.shape[2]
    bf16 = jnp.bfloat16

    packed = jnp.concatenate(
        [ffn_w[0], ffn_w[1], qkv_w[0], qkv_w[1], qkv_w[2], jnp.zeros((ffn_w.shape[1], PAD))], axis=1
    ).astype(bf16)
    weights = lax.all_gather(packed, "dp", axis=0, tiled=True)

    flat = tokens.reshape(micro * rows, width)
    vec_rows, vec_own = vecs.shape
    small = jnp.concatenate(
        [vecs.astype(bf16).reshape(-1), doc_lengths.astype(bf16).reshape(-1)]
    )
    small = jnp.pad(small, (0, 8 * width - small.shape[0])).reshape(8, width)
    out_flat = out_w.astype(bf16).reshape(-1, width)
    out_count = out_flat.shape[0]
    heard = gather_direct(jnp.concatenate([flat, out_flat, small], axis=0), "shard")
    tokens_b = heard[:, : micro * rows].reshape(slots * rows, width)
    out_part = heard[:, micro * rows : micro * rows + out_count].reshape(shards, -1, own)
    out_part = out_part.transpose(1, 0, 2).reshape(-1, width)
    small = heard[:, micro * rows + out_count :].reshape(shards, -1)
    lengths = small[:, vecs.size : vecs.size + doc_lengths.size].astype(jnp.int32).reshape(slots, -1)
    small = small[:, : vecs.size].reshape(shards, vec_rows, vec_own).transpose(1, 0, 2).reshape(vec_rows, -1)
    vec = gather_double(small, "dp").transpose(1, 0, 2).reshape(vec_rows, -1).astype(jnp.float32)
    out_b = lax.all_gather(out_part, "dp", axis=0, tiled=True)
    position = jnp.arange(rows, dtype=jnp.int32)[None]
    ends = jnp.cumsum(lengths, axis=1)
    segment = jnp.sum((position[:, :, None] >= ends[:, None, :]).astype(jnp.int32), axis=2)
    valid = position < ends[:, -1:]
    slot = jnp.arange(slots, dtype=jnp.int32)[:, None]
    marks = jnp.where(valid, segment + slot * ends.shape[1], -1 - position - slot * rows)
    id_column, id_row = marks.reshape(-1, 1), marks.reshape(1, -1)
    bias_q = lax.dynamic_slice_in_dim(vec[0], column * own, own, 0)
    bias_v = lax.dynamic_slice_in_dim(vec[1], column * own, own, 0)
    bias_proj = jnp.concatenate([bias_q, jnp.zeros_like(bias_q), bias_v])[None]
    bias_up = lax.dynamic_slice_in_dim(vec[8:].reshape(-1), column * hidden, hidden, 0)[None]

    proj_lanes = pl.ds(2 * hidden, weights.shape[1] - 2 * hidden)
    ffn_lanes = pl.ds(0, 2 * hidden)
    qkv, mixed_own = run_kernel(
        attention_forward,
        [
            jax.ShapeDtypeStruct((slots * rows, 3 * own), bf16),
            jax.ShapeDtypeStruct((BLOCK, slots * rows // BLOCK * own), bf16),
        ],
        scalars=1,
        ties=[vec, bias_up],
        far=(1, 2, 4),
        far_out=(0,),
        lanes={2: proj_lanes},
    )(place, tokens_b, weights, bias_proj, id_column, id_row)

    depth = width // groups
    count = micro * rows
    whole_b = jax.ShapeDtypeStruct((slots * rows, width), bf16)
    own_f = jax.ShapeDtypeStruct((count, width), jnp.float32)
    own_b = jax.ShapeDtypeStruct((count, width), bf16)
    part_kinds = [own_f] + [own_b] * (shards - 1)
    sums_kind = jax.ShapeDtypeStruct((8, width), jnp.float32)
    moving = pltpu.VMEM((slots * rows, width), jnp.float32)

    mixed_pieces = pieces_of(mixed_own, "shard")
    first_b, activ_b, slope, first_in, *parts = run_kernel(
        layer_middle,
        [whole_b, whole_b, jax.ShapeDtypeStruct((slots * rows, hidden), jnp.float32), own_f] + part_kinds,
        scalars=1,
        scratch=[moving],
        far=(5, 6, 8),
        late=(8,),
        lanes={8: ffn_lanes},
    )(place, *mixed_pieces, out_b, tokens_b, vec, weights, bias_up)
    layer_out, d_branch_own, d_second, sums_two = run_kernel(
        second_norm, [own_b, own_b, own_f, sums_kind], scalars=1, far=(7, 8), far_out=(0, 2, 3)
    )(place, *send_parts(parts, "shard"), first_in, vec, cotangent.reshape(count, width), id_column)
    layer_out = layer_out.reshape(tokens.shape)
    d_branch_b, d_inner_b, d_bias_up, *parts = run_kernel(
        inner_backward,
        [whole_b, whole_b, jax.ShapeDtypeStruct((1, hidden), jnp.float32)] + part_kinds,
        scalars=1,
        scratch=[moving],
        far=(6,),
        far_out=(2, 3, 4, 5, 6),
        lanes={6: ffn_lanes},
    )(place, *pieces_of(d_branch_own, "shard"), slope, weights)
    (grads,) = run_kernel(inner_gradients, [jax.ShapeDtypeStruct((2, width, hidden), bf16)], far_out=(0,))(
        first_b, activ_b, d_inner_b, d_branch_b
    )
    summed = lax.psum_scatter(grads, "dp", scatter_dimension=1, tiled=True)
    d_first_in, d_attended_own, sums_one = run_kernel(
        first_norm, [own_f, own_b, sums_kind], far=(0, 4, 5), far_out=(0, 1, 2)
    )(*send_parts(parts, "shard"), d_second, first_in, vec)
    d_attended_pieces = pieces_of(d_attended_own, "shard")
    moment_kind = jax.ShapeDtypeStruct(ffn_mom.shape, ffn_mom.dtype)
    wide_kind = jax.ShapeDtypeStruct((depth, hidden), bf16)
    grad_ffn, new_ffn_mom, mine, far_send = run_kernel(
        wide_momenta,
        [moment_kind, moment_kind, wide_kind, wide_kind],
        scalars=1,
        ties=d_attended_pieces[1:],
        far=(1, 2),
        far_out=(0, 1),
    )(place, summed, ffn_mom)
    far_rows = swap(far_send, "shard", shards // 2)

    packed_rows = depth + 16
    d_proj, d_columns = run_kernel(
        attention_backward,
        [
            jax.ShapeDtypeStruct((slots * rows, 3 * own), bf16),
            jax.ShapeDtypeStruct((slots * rows, own), bf16),
        ],
        scalars=1,
        scratch=[pltpu.VMEM((slots * rows, width), bf16)],
        ties=[far_send],
        far=(1, 2, 3, 4, 5, 6, 7),
        far_out=(0, 1),
    )(place, *d_attended_pieces, out_b, qkv, id_column, id_row)
    (wide_rows,) = run_kernel(
        join_wide, [jax.ShapeDtypeStruct((depth, 2 * hidden), bf16)], ties=[d_proj], far_out=(0,)
    )(mine, far_rows)
    wide = lax.all_gather(wide_rows, "dp", axis=0, tiled=True)
    kept, sent = run_kernel(
        square_gradients,
        [
            jax.ShapeDtypeStruct((groups // 2, packed_rows, width), jnp.float32),
            jax.ShapeDtypeStruct((groups // 2, packed_rows, width), bf16),
        ],
        scalars=1,
        scratch=[pltpu.VMEM((16, width), jnp.float32)],
        ties=[wide_rows],
        far=(1, 2, 3, 4, 5, 6, 7, 8, 9),
        far_out=(0,),
    )(place, *mixed_pieces, tokens_b, d_proj, d_columns, sums_one, sums_two, d_bias_up)
    block_kind = jax.ShapeDtypeStruct((packed_rows, width), bf16)
    total, *blocks = run_kernel(
        pair_sum, [jax.ShapeDtypeStruct((packed_rows, width), jnp.float32)] + [block_kind] * 3, scalars=1, far=(1,)
    )(place, kept, swap(sent, "dp", 1))
    (part,) = run_kernel(
        token_part, [whole_b], ties=[total], far=(0, 1), far_out=(0,), lanes={1: proj_lanes}
    )(d_proj, weights)
    d_tokens = lax.psum_scatter(part, "shard", scatter_dimension=0, tiled=True)
    d_tokens = d_first_in + d_tokens.astype(jnp.float32)
    block_kind = jax.ShapeDtypeStruct((packed_rows, own), bf16)
    like = [jax.ShapeDtypeStruct(each.shape, each.dtype) for each in (qkv_mom, out_mom)]
    grad_qkv, grad_wout, new_qkv_mom, new_out_mom, *blocks = run_kernel(
        square_momenta,
        like + like + [block_kind] * shards,
        scalars=1,
        scratch=[pltpu.VMEM((shards, packed_rows, own), jnp.float32)],
        far=(5, 6),
        far_out=(0, 1, 2, 3),
    )(place, total, *[swap(block, "dp", 2 * at + 2) for at, block in enumerate(blocks)], qkv_mom, out_mom)
    square_pieces = send_parts(blocks, "shard")
    (gram_rows,) = run_kernel(wide_gram, [jax.ShapeDtypeStruct((depth, width), bf16)], ties=square_pieces[1:], far=(0, 1))(
        wide_rows, wide
    )
    row_kind = jax.ShapeDtypeStruct((depth, width), bf16)
    mine, other, grad_vec = run_kernel(
        join_squares,
        [row_kind, row_kind, jax.ShapeDtypeStruct((packed_rows - depth, own), jnp.float32)],
        scalars=1,
        scratch=[pltpu.VMEM((depth, width), bf16)],
    )(place, *square_pieces, gram_rows, swap(gram_rows, "shard", 1))
    grad_vec = grad_vec[:vec_rows, :vec_own]
    d_tokens = d_tokens.reshape(tokens.shape)
    (pair_rows,) = run_kernel(
        join_pair, [jax.ShapeDtypeStruct((2 * depth, width), bf16)], scalars=1
    )(place, mine, swap(other, "dp", 1))
    pair_pieces = [pair_rows] + [swap(pair_rows, "dp", bit) for bit in (2, 4, 6)]
    state_kind = jax.ShapeDtypeStruct((depth, 2 * hidden), bf16)
    kept, sent = run_kernel(
        newton_schulz,
        [state_kind, state_kind],
        scalars=1,
        scratch=[pltpu.VMEM((width, width), bf16), pltpu.VMEM((width, width), jnp.float32)]
        + [pltpu.VMEM((width, width), bf16)] * (NS_STEPS - 1),
        far=(5,),
        late=(5,),
    )(place, *pair_pieces, wide)
    block_kind = jax.ShapeDtypeStruct((depth, own), bf16)
    wide_kind = jax.ShapeDtypeStruct((depth, hidden), bf16)
    kinds = [block_kind] * shards + [wide_kind]
    kinds[shards // 2] = jax.ShapeDtypeStruct((depth, hidden + own), bf16)
    *blocks, mine = run_kernel(
        split_state, kinds, scalars=1
    )(place, kept, swap(sent, "dp", 1))
    qkv_new, out_new, ffn_new = run_kernel(
        new_weights,
        [jax.ShapeDtypeStruct(each.shape, each.dtype) for each in (qkv_w, out_w, ffn_w)],
        scalars=1,
        scratch=[pltpu.VMEM((shards, depth, own), jnp.float32)],
        far=(6, 7, 8),
        far_out=(0, 1, 2),
    )(
        place, *send_parts(blocks, "shard"), mine, qkv_w, out_w, ffn_w
    )

    token_count = micro * rows * groups * shards
    new_vec_mom = momentum_decay * vec_mom + grad_vec
    vec_new = vecs - vec_rate * token_count ** (-0.5) * new_vec_mom
    return (
        layer_out,
        d_tokens,
        grad_qkv,
        grad_wout,
        grad_ffn,
        grad_vec,
        new_qkv_mom,
        new_out_mom,
        new_ffn_mom,
        new_vec_mom,
        qkv_new,
        out_new,
        ffn_new,
        vec_new,
    )


def solution(mesh):
    fits = (mesh.shape["dp"], mesh.shape["shard"]) == (8, 4)
    in_specs = (
        P(("dp", "shard"), None, None),
        P(("dp", "shard"), None, None),
        P(("dp", "shard"), None),
        P(None, "dp", "shard"),
        P("dp", "shard"),
        P(None, "dp", "shard"),
        P(None, ("dp", "shard")),
        P(None, "dp", "shard"),
        P("dp", "shard"),
        P(None, "dp", "shard"),
        P(None, ("dp", "shard")),
    )
    out_specs = (
        P(("dp", "shard"), None, None),
        P(("dp", "shard"), None, None),
        P(None, "dp", "shard"),
        P("dp", "shard"),
        P(None, "dp", "shard"),
        P(None, ("dp", "shard")),
        P(None, "dp", "shard"),
        P("dp", "shard"),
        P(None, "dp", "shard"),
        P(None, ("dp", "shard")),
        P(None, "dp", "shard"),
        P("dp", "shard"),
        P(None, "dp", "shard"),
        P(None, ("dp", "shard")),
    )
    return jax.shard_map(
        split_device if fits else per_device, mesh=mesh, in_specs=in_specs, out_specs=out_specs, check_vma=False
    )
```

```python
import math
import jax
import jax.numpy as jnp
from jax import lax
from jax.experimental import pallas as pl
from jax.experimental.pallas import tpu as pltpu
from jax.sharding import PartitionSpec as P

D = 768
HEADS = 12
HEAD = 64
FF = 3072
NS_STEPS = 3


masked_score = -1e30
norm_eps = 1e-12
momentum_decay = 0.9
muon_rate = 0.8
vec_rate = 0.5
coef_first = 3.4445
coef_second = -4.775
coef_third = 2.0315
ortho_eps = 1e-07


def spread_2(block, axis, owner):
    block = jnp.where(lax.axis_index(axis) == owner, block, jnp.zeros_like(block))
    return lax.psum(block, axis)


def segments(lengths, rows):
    position = jnp.arange(rows, dtype=jnp.int32)
    ends = jnp.cumsum(lengths)
    segment = jnp.sum((position[:, None] >= ends[None, :]).astype(jnp.int32), axis=1)
    valid = position < ends[-1]
    same = segment[:, None] == segment[None, :]
    allowed = same & valid[:, None] | (position[:, None] == position[None, :])
    return (valid, allowed)


def layer_norm(inputs, gain, bias):
    center = inputs - jnp.mean(inputs, axis=-1, keepdims=True)
    spread = jnp.mean(center * center, axis=-1, keepdims=True)
    return center * lax.rsqrt(spread + norm_eps) * gain + bias


def gelu_exact(inputs):
    return jax.nn.gelu(inputs, approximate=False)


def split_heads(matrix):
    return matrix.reshape(matrix.shape[0], HEADS, HEAD)


def gather_weights(qkv_w, out_w, ffn_w, vecs):
    pieces = (
        qkv_w.astype(jnp.bfloat16),
        out_w.astype(jnp.bfloat16),
        ffn_w.astype(jnp.bfloat16),
        vecs.astype(jnp.bfloat16),
    )
    across = (
        lax.all_gather(pieces[0], "shard", axis=2, tiled=True),
        lax.all_gather(pieces[1], "shard", axis=1, tiled=True),
        lax.all_gather(pieces[2], "shard", axis=2, tiled=True),
        lax.all_gather(pieces[3], "shard", axis=1, tiled=True),
    )
    return (
        lax.all_gather(across[0], "dp", axis=1, tiled=True),
        lax.all_gather(across[1], "dp", axis=0, tiled=True),
        lax.all_gather(across[2], "dp", axis=1, tiled=True),
        lax.all_gather(across[3], "dp", axis=1, tiled=True),
    )


def attention_scores(queries_b, keys_b, allowed):
    scores = jnp.einsum(
        "qhd,khd->hqk",
        split_heads(queries_b),
        split_heads(keys_b),
        preferred_element_type=jnp.float32,
    )
    return jnp.where(allowed[None], scores * HEAD ** (-0.5), masked_score)


def forward_pass(tokens_b, lengths, weights):
    qkv_b, out_b, ffn_b, vec_b = weights
    vec = vec_b.astype(jnp.float32)
    rows = tokens_b.shape[0]
    valid, allowed = segments(lengths, rows)
    projected = jnp.einsum("rd,kde->kre", tokens_b, qkv_b, preferred_element_type=jnp.float32)
    queries_b = (projected[0] + vec[0]).astype(jnp.bfloat16)
    keys_b = projected[1].astype(jnp.bfloat16)
    values_b = (projected[2] + vec[1]).astype(jnp.bfloat16)
    scores = attention_scores(queries_b, keys_b, allowed)
    largest = jnp.max(scores, axis=-1, keepdims=True)
    exponent = jnp.exp(scores - largest)
    totals = jnp.sum(exponent, axis=-1, keepdims=True)
    logsum = largest + jnp.log(totals)
    probs_b = (exponent / totals).astype(jnp.bfloat16)
    mixed = jnp.einsum(
        "hqk,khd->qhd", probs_b, split_heads(values_b), preferred_element_type=jnp.float32
    )
    mixed_b = mixed.reshape(rows, -1).astype(jnp.bfloat16)
    attended = jnp.dot(mixed_b, out_b, preferred_element_type=jnp.float32) + vec[2]
    first_in = tokens_b.astype(jnp.float32) + attended
    first = layer_norm(first_in, vec[3], vec[4])
    first_b = first.astype(jnp.bfloat16)
    inner = jnp.dot(first_b, ffn_b[0], preferred_element_type=jnp.float32) + vec[8:].reshape(-1)
    activ_b = gelu_exact(inner).astype(jnp.bfloat16)
    branch = jnp.einsum("rf,df->rd", activ_b, ffn_b[1], preferred_element_type=jnp.float32) + vec[5]
    second_in = first + branch
    result = layer_norm(second_in, vec[6], vec[7]) * valid[:, None].astype(jnp.float32)
    kept = (
        queries_b,
        keys_b,
        values_b,
        logsum,
        mixed_b,
        first_in,
        first_b,
        inner,
        activ_b,
        second_in,
    )
    return (result.astype(jnp.bfloat16), kept)


def backward_pass(cot_b, tokens_b, lengths, weights, kept):
    qkv_b, out_b, ffn_b, vec_b = weights
    vec = vec_b.astype(jnp.float32)
    queries_b, keys_b, values_b, logsum, mixed_b, first_in, first_b, inner, activ_b, second_in = (
        kept
    )
    rows = tokens_b.shape[0]
    valid, allowed = segments(lengths, rows)
    grad_out = cot_b.astype(jnp.float32) * valid[:, None].astype(jnp.float32)
    unused, pull_two = jax.vjp(layer_norm, second_in, vec[6], vec[7])
    d_second, d_gain_two, d_shift_two = pull_two(grad_out)
    d_branch_b = d_second.astype(jnp.bfloat16)
    d_bias_down = jnp.sum(d_branch_b.astype(jnp.float32), axis=0)
    d_activ = jnp.dot(d_branch_b, ffn_b[1], preferred_element_type=jnp.float32)
    unused, pull_gelu = jax.vjp(gelu_exact, inner)
    (d_inner,) = pull_gelu(d_activ)
    d_inner_b = d_inner.astype(jnp.bfloat16)
    d_bias_up = jnp.sum(d_inner_b.astype(jnp.float32), axis=0)
    d_first = d_second + jnp.einsum(
        "rf,df->rd", d_inner_b, ffn_b[0], preferred_element_type=jnp.float32
    )
    unused, pull_one = jax.vjp(layer_norm, first_in, vec[3], vec[4])
    d_first_in, d_gain_one, d_shift_one = pull_one(d_first)
    d_attended_b = d_first_in.astype(jnp.bfloat16)
    d_bias_out = jnp.sum(d_attended_b.astype(jnp.float32), axis=0)
    d_mixed_b = jnp.einsum(
        "re,de->rd", d_attended_b, out_b, preferred_element_type=jnp.float32
    ).astype(jnp.bfloat16)
    scores = attention_scores(queries_b, keys_b, allowed)
    probs = jnp.exp(scores - logsum)
    mixed_heads = split_heads(d_mixed_b)
    d_probs = jnp.einsum(
        "qhd,khd->hqk", mixed_heads, split_heads(values_b), preferred_element_type=jnp.float32
    )
    d_values = jnp.einsum(
        "hqk,qhd->khd", probs.astype(jnp.bfloat16), mixed_heads, preferred_element_type=jnp.float32
    )
    d_scores_b = (probs * (d_probs - jnp.sum(probs * d_probs, axis=-1, keepdims=True))).astype(
        jnp.bfloat16
    )
    d_queries = jnp.einsum(
        "hqk,khd->qhd", d_scores_b, split_heads(keys_b), preferred_element_type=jnp.float32
    ) * HEAD ** (-0.5)
    d_keys = jnp.einsum(
        "hqk,qhd->khd", d_scores_b, split_heads(queries_b), preferred_element_type=jnp.float32
    ) * HEAD ** (-0.5)
    d_proj_b = jnp.stack([d_queries, d_keys, d_values]).reshape(3, rows, -1).astype(jnp.bfloat16)
    d_tokens = d_first_in + jnp.einsum(
        "kre,kde->rd", d_proj_b, qkv_b, preferred_element_type=jnp.float32
    )
    proj_sums = jnp.sum(d_proj_b.astype(jnp.float32), axis=1)
    grad_vec = jnp.concatenate(
        [
            jnp.stack(
                [
                    proj_sums[0],
                    proj_sums[2],
                    d_bias_out,
                    d_gain_one,
                    d_shift_one,
                    d_bias_down,
                    d_gain_two,
                    d_shift_two,
                ]
            ),
            d_bias_up.reshape(-1, vec.shape[1]),
        ],
        axis=0,
    )
    factors = (d_branch_b, activ_b, first_b, d_inner_b, mixed_b, d_attended_b, d_proj_b)
    return (d_tokens, factors, grad_vec)


def orthogonalize_pair(square, wide):
    matrices = (square, wide)
    present = tuple((matrix.astype(jnp.bfloat16) for matrix in matrices))
    states = matrices
    for step in range(NS_STEPS):
        partial_value = tuple(
            (
                jnp.einsum("iw,jw->ij", block, block, preferred_element_type=jnp.float32)
                for block in present
            )
        )
        gram_part = (
            lax.psum_scatter(
                partial_value[0].astype(jnp.bfloat16), "shard", scatter_dimension=0, tiled=True
            ).astype(jnp.float32),
            lax.psum_scatter(
                partial_value[1].astype(jnp.bfloat16), "shard", scatter_dimension=0, tiled=True
            ).astype(jnp.float32),
        )
        grams = (
            lax.all_gather(gram_part[0].astype(jnp.bfloat16), "shard", axis=0, tiled=True).astype(
                jnp.float32
            ),
            lax.all_gather(gram_part[1].astype(jnp.bfloat16), "shard", axis=0, tiled=True).astype(
                jnp.float32
            ),
        )
        if step == 0:
            scales = tuple((jnp.sqrt(jnp.trace(gram)) + ortho_eps for gram in grams))
            grams = tuple((gram / (scale * scale) for gram, scale in zip(grams, scales)))
            present = tuple(
                ((matrix / scale).astype(jnp.bfloat16) for matrix, scale in zip(matrices, scales))
            )
        renewed = []
        for gram, current in zip(grams, present):
            gram_b = gram.astype(jnp.bfloat16)
            once = jnp.dot(gram_b, current, preferred_element_type=jnp.float32)
            twice = jnp.dot(gram_b, once.astype(jnp.bfloat16), preferred_element_type=jnp.float32)
            renewed.append(
                coef_first * current.astype(jnp.float32) + coef_second * once + coef_third * twice
            )
        states = tuple(renewed)
        present = tuple((state.astype(jnp.bfloat16) for state in states))
    return states


def per_device(
    tokens, cotangent, doc_lengths, qkv_w, out_w, ffn_w, vecs, qkv_mom, out_mom, ffn_mom, vec_mom
):
    micro = tokens.shape[0]
    shared = gather_weights(qkv_w, out_w, ffn_w, vecs)
    outputs = []
    stored = []
    for index in range(micro):
        weights = shared
        result_b, kept = forward_pass(tokens[index], doc_lengths[index], weights)
        outputs.append(result_b)
        stored.append(kept)
    grad_rows = [None] * micro
    factor_list = [None] * micro
    vec_total = None
    for index in reversed(range(micro)):
        weights = shared
        d_tokens, factors, vec_part = backward_pass(
            cotangent[index], tokens[index], doc_lengths[index], weights, stored[index]
        )
        grad_rows[index] = d_tokens
        factor_list[index] = factors
        vec_total = vec_part if vec_total is None else vec_total + vec_part
    (
        branch_gradient_rows,
        activation_rows,
        first_norm_rows,
        inner_gradient_rows,
        mixed_all,
        d_attended_all,
        d_proj_all,
    ) = [jnp.stack([factors[place] for factors in factor_list]) for place in range(7)]
    grad_down = jnp.einsum(
        "hzo,hzx->ox", branch_gradient_rows, activation_rows, preferred_element_type=jnp.float32
    )
    up_weight_gradient = jnp.einsum(
        "hzo,hzx->ox", first_norm_rows, inner_gradient_rows, preferred_element_type=jnp.float32
    )
    grad_wout_sum = jnp.einsum(
        "mrd,mre->de", mixed_all, d_attended_all, preferred_element_type=jnp.float32
    )
    grad_qkv_sum = jnp.einsum(
        "mrd,mkre->kde", tokens, d_proj_all, preferred_element_type=jnp.float32
    )
    summed = (grad_qkv_sum, grad_wout_sum, jnp.stack([up_weight_gradient, grad_down]), vec_total)
    reduced = (
        lax.psum_scatter(
            summed[0].astype(jnp.bfloat16), "dp", scatter_dimension=1, tiled=True
        ).astype(jnp.float32),
        lax.psum_scatter(
            summed[1].astype(jnp.bfloat16), "dp", scatter_dimension=0, tiled=True
        ).astype(jnp.float32),
        lax.psum_scatter(
            summed[2].astype(jnp.bfloat16), "dp", scatter_dimension=1, tiled=True
        ).astype(jnp.float32),
        lax.psum_scatter(
            summed[3].astype(jnp.bfloat16), "dp", scatter_dimension=1, tiled=True
        ).astype(jnp.float32),
    )
    grad_qkv, grad_wout, grad_ffn, grad_vec = (
        lax.psum_scatter(
            reduced[0].astype(jnp.bfloat16), "shard", scatter_dimension=2, tiled=True
        ).astype(jnp.float32),
        lax.psum_scatter(
            reduced[1].astype(jnp.bfloat16), "shard", scatter_dimension=1, tiled=True
        ).astype(jnp.float32),
        lax.psum_scatter(
            reduced[2].astype(jnp.bfloat16), "shard", scatter_dimension=2, tiled=True
        ).astype(jnp.float32),
        lax.psum_scatter(
            reduced[3].astype(jnp.bfloat16), "shard", scatter_dimension=1, tiled=True
        ).astype(jnp.float32),
    )
    new_qkv_mom = momentum_decay * qkv_mom + grad_qkv
    new_out_mom = momentum_decay * out_mom + grad_wout
    new_ffn_mom = momentum_decay * ffn_mom + grad_ffn
    square_local = jnp.concatenate([new_qkv_mom, new_out_mom[None]], axis=0)
    square_cols, wide_cols = (
        lax.all_gather(square_local.astype(jnp.bfloat16), "dp", axis=1, tiled=True).astype(
            square_local.dtype
        ),
        lax.all_gather(new_ffn_mom.astype(jnp.bfloat16), "dp", axis=1, tiled=True).astype(
            new_ffn_mom.dtype
        ),
    )
    row = lax.axis_index("dp")
    rows_count = lax.axis_size("dp")
    owners = [place * rows_count // 6 for place in range(6)]
    square_pick = sum(((row == owners[place]).astype(jnp.int32) * place for place in range(4)))
    wide_pick = (row == owners[5]).astype(jnp.int32)
    square_state, wide_state = orthogonalize_pair(
        lax.dynamic_index_in_dim(square_cols, square_pick, 0, keepdims=False),
        lax.dynamic_index_in_dim(wide_cols, wide_pick, 0, keepdims=False),
    )
    depth = qkv_w.shape[1]
    square_rows = []
    for place in range(4):
        whole = spread_2(square_state.astype(jnp.bfloat16), "dp", owners[place]).astype(
            square_state.dtype
        )
        square_rows.append(lax.dynamic_slice_in_dim(whole, row * depth, depth, 0))
    wide_rows = []
    for place in range(4, 6):
        whole = spread_2(wide_state.astype(jnp.bfloat16), "dp", owners[place]).astype(
            wide_state.dtype
        )
        wide_rows.append(lax.dynamic_slice_in_dim(whole, row * depth, depth, 0))
    qkv_new = qkv_w - muon_rate * jnp.stack(square_rows[:3])
    out_new = out_w - muon_rate * square_rows[3]
    ffn_new = ffn_w - muon_rate * (FF / D) ** 0.5 * jnp.stack(wide_rows)
    token_count = tokens.shape[0] * tokens.shape[1] * lax.axis_size("dp") * lax.axis_size("shard")
    new_vec_mom = momentum_decay * vec_mom + grad_vec
    vec_new = vecs - vec_rate * token_count ** (-0.5) * new_vec_mom
    return (
        jnp.stack(outputs),
        jnp.stack(grad_rows),
        grad_qkv,
        grad_wout,
        grad_ffn,
        grad_vec,
        new_qkv_mom,
        new_out_mom,
        new_ffn_mom,
        new_vec_mom,
        qkv_new,
        out_new,
        ffn_new,
        vec_new,
    )


def gather_direct(block, axis):
    count = lax.axis_size(axis)
    me = lax.axis_index(axis)
    whole = jnp.zeros((count,) + block.shape, block.dtype)
    whole = lax.dynamic_update_index_in_dim(whole, block, me, 0)
    for step in range(1, count):
        got = lax.ppermute(block, axis, [(i, (i + step) % count) for i in range(count)])
        whole = lax.dynamic_update_index_in_dim(whole, got, lax.rem(me - step + count, count), 0)
    return whole


def pieces_of(block, axis):
    count = lax.axis_size(axis)
    return [block] + [
        lax.ppermute(block, axis, [(i, (i + step) % count) for i in range(count)])
        for step in range(1, count)
    ]


def send_parts(parts, axis):
    count = lax.axis_size(axis)
    return [parts[0]] + [
        lax.ppermute(parts[step], axis, [(i, (i + step) % count) for i in range(count)])
        for step in range(1, count)
    ]


def swap(block, axis, bit):
    return lax.ppermute(block, axis, [(i, i ^ bit) for i in range(lax.axis_size(axis))])


def gather_double(block, axis):
    me = lax.axis_index(axis)
    bit = 1
    whole = block[None]
    while bit < lax.axis_size(axis):
        other = swap(whole, axis, bit)
        high = (me & bit) != 0
        whole = jnp.concatenate(
            [jnp.where(high, other, whole), jnp.where(high, whole, other)], axis=0
        )
        bit *= 2
    return whole


def dot(left, right, dims):
    return lax.dot_general(left, right, (dims, ((), ())), preferred_element_type=jnp.float32)


def norm_parts(inputs):
    center = inputs - jnp.mean(inputs, axis=-1, keepdims=True)
    spread = jnp.mean(center * center, axis=-1, keepdims=True)
    scale = lax.rsqrt(spread + norm_eps)
    return center * scale, scale


def norm_back(grad, unit, scale, gain):
    scaled = grad * gain
    mean_grad = jnp.mean(scaled, axis=-1, keepdims=True)
    mean_unit = jnp.mean(scaled * unit, axis=-1, keepdims=True)
    return scale * (scaled - mean_grad - unit * mean_unit)


BLOCK = 256
PAD = 64
SPLIT = 4


def source_of(column, step):
    return lax.rem(column - step + SPLIT, SPLIT)


def put_pieces(pieces, column, whole):
    count = pieces[0].shape[0]
    for step, piece in enumerate(pieces):
        at = pl.multiple_of(source_of(column, step) * count, count)
        whole[pl.ds(at, count), :] = piece[...]


def take_parts(whole, column, parts):
    count = parts[0].shape[0]
    for step, part in enumerate(parts):
        at = pl.multiple_of(lax.rem(column + step, SPLIT) * count, count)
        part[...] = whole[pl.ds(at, count), :].astype(part.dtype)


def sum_pieces(pieces):
    total = pieces[0][...]
    for piece in pieces[1:]:
        total = total + piece[...].astype(jnp.float32)
    return total


def row_sums(values):
    return jnp.sum(values, axis=0, keepdims=True)


def unpack_rows(piece, rows):
    count = rows // piece.shape[0]
    own = piece.shape[1] // count
    return jnp.concatenate([piece[:, at * own : (at + 1) * own] for at in range(count)], axis=0)


def layer_middle(waits, place, *refs):
    pieces, refs = refs[:SPLIT], refs[SPLIT:]
    out_weight, tokens, vec, weights, bias_up, first_b, activ_b, slope, first_in, *refs = refs
    parts, (moving,) = refs[:SPLIT], refs[SPLIT:]
    column = place[0]
    attended = vec[2:3, :] + tokens[...].astype(jnp.float32)
    for step, piece in enumerate(pieces):
        rows = unpack_rows(piece, tokens.shape[0])
        own = rows.shape[1]
        at = pl.multiple_of(source_of(column, step) * own, own)
        attended = attended + dot(rows, out_weight[pl.ds(at, own), :], ((1,), (0,)))
    moving[...] = attended
    take_parts(moving, column, [first_in])
    unit, scale = norm_parts(attended)
    first_b[...] = (unit * vec[3:4, :] + vec[4:5, :]).astype(jnp.bfloat16)
    hidden = slope.shape[1]
    waits[0]()
    inner = dot(first_b[...], weights[:, :hidden], ((1,), (0,))) + bias_up[...]
    cdf = 0.5 * (1.0 + lax.erf(inner * 2.0 ** (-0.5)))
    activ_b[...] = (inner * cdf).astype(jnp.bfloat16)
    slope[...] = cdf + inner * jnp.exp(-0.5 * inner * inner) * (2.0 * math.pi) ** (-0.5)
    moving[...] = dot(activ_b[...], weights[:, hidden : 2 * hidden], ((1,), (1,)))
    take_parts(moving, column, parts)


def second_norm(place, *refs):
    pieces, refs = refs[:SPLIT], refs[SPLIT:]
    first_in, vec, cotangent, ids, layer_out, d_branch, d_second, sums = refs
    count = first_in.shape[0]
    at = pl.multiple_of(place[0] * count, count)
    valid = (ids[pl.ds(at, count), :] >= 0).astype(jnp.float32)
    unit, scale = norm_parts(first_in[...])
    first = unit * vec[3:4, :] + vec[4:5, :]
    unit, scale = norm_parts(first + (sum_pieces(pieces) + vec[5:6, :]))
    layer_out[...] = ((unit * vec[6:7, :] + vec[7:8, :]) * valid).astype(jnp.bfloat16)
    grad = cotangent[...].astype(jnp.float32) * valid
    d_rows = norm_back(grad, unit, scale, vec[6:7, :])
    d_second[...] = d_rows
    d_branch[...] = d_rows.astype(jnp.bfloat16)
    sums[0:1, :] = row_sums(d_branch[...].astype(jnp.float32))
    sums[1:2, :] = row_sums(grad * unit)
    sums[2:3, :] = row_sums(grad)


def inner_backward(place, *refs):
    pieces, refs = refs[:SPLIT], refs[SPLIT:]
    slope, weights, d_branch, d_inner, sums, *refs = refs
    parts, (moving,) = refs[:SPLIT], refs[SPLIT:]
    column = place[0]
    put_pieces(pieces, column, d_branch)
    hidden = slope.shape[1]
    d_activ = dot(d_branch[...], weights[:, hidden : 2 * hidden], ((1,), (0,)))
    d_inner[...] = (d_activ * slope[...]).astype(jnp.bfloat16)
    sums[...] = row_sums(d_inner[...].astype(jnp.float32))
    moving[...] = dot(d_inner[...], weights[:, :hidden], ((1,), (1,)))
    take_parts(moving, column, parts)


def inner_gradients(first_b, activ_b, d_inner, d_branch, grads):
    grads[0] = dot(first_b[...], d_inner[...], ((0,), (0,))).astype(jnp.bfloat16)
    grads[1] = dot(d_branch[...], activ_b[...], ((0,), (0,))).astype(jnp.bfloat16)


def wide_momenta(place, summed, moments, grads, moments_new, mine, far):
    low = place[0] < SPLIT // 2
    for part in range(2):
        grads[part] = summed[part].astype(jnp.float32)
        moments_new[part] = momentum_decay * moments[part] + grads[part]
    first, second = moments_new[0].astype(jnp.bfloat16), moments_new[1].astype(jnp.bfloat16)
    mine[...] = jnp.where(low, first, second)
    far[...] = jnp.where(low, second, first)


def join_wide(mine, far, rows):
    hidden = mine.shape[1]
    rows[:, :hidden] = mine[...]
    rows[:, hidden:] = far[...]


def wide_gram(rows, wide, gram):
    gram[...] = dot(rows[...], wide[...], ((1,), (1,))).astype(jnp.bfloat16)


def first_norm(*refs):
    pieces, refs = refs[:SPLIT], refs[SPLIT:]
    d_second, first_in, vec, d_first_in, d_attended, sums = refs
    unit, scale = norm_parts(first_in[...])
    grad = sum_pieces(pieces) + d_second[...]
    d_rows = norm_back(grad, unit, scale, vec[3:4, :])
    d_first_in[...] = d_rows
    d_attended[...] = d_rows.astype(jnp.bfloat16)
    sums[0:1, :] = row_sums(d_attended[...].astype(jnp.float32))
    sums[1:2, :] = row_sums(grad * unit)
    sums[2:3, :] = row_sums(grad)


def split_state(place, kept, other, *refs):
    blocks, (mine,) = refs[:SPLIT], refs[SPLIT:]
    column, even = place[0], place[1] == 0
    own, hidden = blocks[0].shape[1], mine.shape[1]
    far = blocks[SPLIT // 2]
    for step, block in enumerate(blocks):
        there = lax.rem(column + step, SPLIT)
        for at in range(SPLIT):
            lanes = slice(at * own, (at + 1) * own)

            @pl.when(there == at)
            def _():
                block[:, block.shape[1] - own :] = jnp.where(even, kept[:, lanes], other[:, lanes])

    mine[...] = jnp.where(even, other[:, :hidden], kept[:, :hidden])
    far[:, :hidden] = jnp.where(even, other[:, hidden:], kept[:, hidden:])


def new_weights(place, *refs):
    pieces, refs = refs[:SPLIT], refs[SPLIT:]
    mine, qkv_w, out_w, ffn_w, qkv_new, out_new, ffn_new, state = refs
    low = place[0] < SPLIT // 2
    own, hidden = out_w.shape[1], mine.shape[1]
    far = pieces[SPLIT // 2][:, :hidden]
    for step, piece in enumerate(pieces):
        state[source_of(place[0], step)] = piece[:, piece.shape[1] - own :].astype(jnp.float32)
    for at in range(SPLIT - 1):
        qkv_new[at] = qkv_w[at] - muon_rate * state[at]
    out_new[...] = out_w[...] - muon_rate * state[SPLIT - 1]
    rate = muon_rate * (FF / D) ** 0.5
    ffn_new[0] = ffn_w[0] - rate * jnp.where(low, mine[...], far).astype(jnp.float32)
    ffn_new[1] = ffn_w[1] - rate * jnp.where(low, far, mine[...]).astype(jnp.float32)


def probabilities(qkv, rows_at, head, own, id_column, id_row):
    queries = qkv[rows_at, head * HEAD : (head + 1) * HEAD]
    keys = qkv[rows_at, own + head * HEAD : own + (head + 1) * HEAD]
    values = qkv[rows_at, 2 * own + head * HEAD : 2 * own + (head + 1) * HEAD]
    scores = dot(queries, keys, ((1,), (1,))) * HEAD ** (-0.5)
    scores = jnp.where(id_column[rows_at, :] == id_row[:, rows_at], scores, masked_score)
    exponent = jnp.exp(scores - jnp.max(scores, axis=-1, keepdims=True))
    probs = exponent / jnp.sum(exponent, axis=-1, keepdims=True)
    return queries, keys, values, probs


def attention_forward(place, tokens, weight, bias, id_column, id_row, qkv, mixed):
    own = qkv.shape[1] // 3
    proj = weight[:, : 3 * own]
    qkv[...] = (dot(tokens[...], proj, ((1,), (0,))) + bias[...]).astype(jnp.bfloat16)
    for start in range(0, tokens.shape[0], BLOCK):
        rows_at = slice(start, start + BLOCK)
        for head in range(own // HEAD):
            queries, keys, values, probs = probabilities(qkv, rows_at, head, own, id_column, id_row)
            part = dot(probs.astype(jnp.bfloat16), values, ((1,), (0,)))
            at = start // BLOCK * own + head * HEAD
            mixed[:, at : at + HEAD] = part.astype(jnp.bfloat16)


def attention_backward(waits, place, *refs):
    pieces, mixed, refs = refs[:SPLIT], refs[SPLIT : 2 * SPLIT], refs[2 * SPLIT :]
    out_weight, qkv, id_column, id_row, tokens, sums_one, sums_two, sums_up, *refs = refs
    kept, sent, d_proj, d_attended, sums = refs
    rows, width = tokens.shape
    own = qkv.shape[1] // 3
    column, core = place[0], place[1]
    put_pieces(pieces, column, d_attended)
    out_rows = out_weight[pl.ds(pl.multiple_of(column * own, own), own), :]
    d_mixed = dot(d_attended[...], out_rows, ((1,), (1,))).astype(jnp.bfloat16)
    for start in range(0, rows, BLOCK):
        rows_at = slice(start, start + BLOCK)
        for head in range(own // HEAD):
            queries, keys, values, probs = probabilities(qkv, rows_at, head, own, id_column, id_row)
            d_out = d_mixed[rows_at, head * HEAD : (head + 1) * HEAD]
            d_probs = dot(d_out, values, ((1,), (1,)))
            d_scores = probs * (d_probs - jnp.sum(probs * d_probs, axis=-1, keepdims=True))
            d_scores = d_scores.astype(jnp.bfloat16)
            d_values = dot(probs.astype(jnp.bfloat16), d_out, ((0,), (0,)))
            d_queries = dot(d_scores, keys, ((1,), (0,))) * HEAD ** (-0.5)
            d_keys = dot(d_scores, queries, ((0,), (0,))) * HEAD ** (-0.5)
            for part, value in enumerate((d_queries, d_keys, d_values)):
                at = part * own + head * HEAD
                d_proj[rows_at, at : at + HEAD] = value.astype(jnp.bfloat16)
    d_proj_all = d_proj[...]
    d_columns = d_attended[:, :own]
    for place_at in range(1, width // own):
        other = d_attended[:, place_at * own : (place_at + 1) * own]
        d_columns = jnp.where(column == place_at, other, d_columns)
    for wait in waits:
        wait()
    grad_proj = dot(tokens[...], d_proj_all, ((0,), (0,)))
    proj_sums = row_sums(d_proj_all.astype(jnp.float32))
    sums[...] = jnp.zeros_like(sums)
    for at in range(SPLIT):
        lanes = slice(at * own, (at + 1) * own)
        mine = (column == at).astype(jnp.float32)
        sums[0:1, lanes] = proj_sums[:, :own] * mine
        sums[1:2, lanes] = proj_sums[:, 2 * own :] * mine
        sums[8 + at : 9 + at, :] = sums_up[...] * mine
    sums[2:5, :] = sums_one[0:3, :]
    sums[5:8, :] = sums_two[0:3, :]
    depth = kept.shape[1] - sums.shape[0]
    for group in range(width // depth):
        at = slice(group * depth, (group + 1) * depth)

        def put(target, kind):
            target[group // 2, :depth, : 3 * own] = grad_proj[at].astype(kind)
            target[group // 2, depth:, :] = jnp.zeros((sums.shape[0], width), kind)
            target[group // 2, depth:, :depth] = sums[:, at].astype(kind)

        pl.when(core == group % 2)(lambda: put(kept, jnp.float32))
        pl.when(core != group % 2)(lambda: put(sent, jnp.bfloat16))
    for step, piece in enumerate(mixed):
        grad_out = dot(unpack_rows(piece, rows), d_columns, ((0,), (0,)))
        source = source_of(column, step)
        for half in range(2):
            block = grad_out[half * depth : (half + 1) * depth]

            def put_out(target, kind):
                target[source, :depth, 3 * own :] = block.astype(kind)

            pl.when(core == half)(lambda: put_out(kept, jnp.float32))
            pl.when(core != half)(lambda: put_out(sent, jnp.bfloat16))


def token_part(d_proj, weight, part):
    proj = weight[:, : d_proj.shape[1]]
    part[...] = dot(d_proj[...], proj, ((1,), (1,))).astype(jnp.bfloat16)


def add_rows(left, right, total):
    total[...] = left[...] + right[...].astype(jnp.float32)


def pair_sum(place, kept, other, total, *blocks):
    chip = place[2]
    total[...] = kept[chip] + other[chip].astype(jnp.float32)
    for step, block in enumerate(blocks):
        at = chip ^ (step + 1)
        block[...] = (kept[at] + other[at].astype(jnp.float32)).astype(jnp.bfloat16)


def square_momenta(place, total, *refs):
    pieces, refs = refs[: SPLIT - 1], refs[SPLIT - 1 :]
    qkv_mom, out_mom, qkv_grad, out_grad, qkv_new, out_new, *refs = refs
    blocks, state = refs[:SPLIT], refs[SPLIT]
    depth, own = out_mom.shape
    whole = sum_pieces([total, *pieces])
    vec_own = depth // SPLIT
    for at in range(SPLIT):
        grad = whole[:depth, at * own : (at + 1) * own]
        if at < SPLIT - 1:
            qkv_grad[at] = grad
            moment = momentum_decay * qkv_mom[at] + grad
            qkv_new[at] = moment
        else:
            out_grad[...] = grad
            moment = momentum_decay * out_mom[...] + grad
            out_new[...] = moment
        state[at, :depth, :] = moment
        state[at, depth:, :] = jnp.zeros((whole.shape[0] - depth, own), jnp.float32)
        state[at, depth:, :vec_own] = whole[depth:, at * vec_own : (at + 1) * vec_own]
    for step, block in enumerate(blocks):
        block[...] = state[lax.rem(place[0] + step, SPLIT)].astype(jnp.bfloat16)


def join_squares(place, *refs):
    pieces, (gram, gram_other, mine, other, sums, rows) = refs[:SPLIT], refs[SPLIT:]
    depth, own = mine.shape[0], pieces[0].shape[1]
    total = jnp.zeros(sums.shape, jnp.float32)
    for step, piece in enumerate(pieces):
        total = total + piece[depth:, :].astype(jnp.float32)
        for at in range(SPLIT):

            @pl.when(source_of(place[0], step) == at)
            def _():
                rows[:, at * own : (at + 1) * own] = piece[:depth, :]

    sums[...] = total
    even = place[1] == 0
    gram_sum = (gram[...].astype(jnp.float32) + gram_other[...].astype(jnp.float32)).astype(jnp.bfloat16)
    mine[...] = jnp.where(even, rows[...], gram_sum)
    other[...] = jnp.where(even, gram_sum, rows[...])


def join_pair(place, mine, other, rows):
    depth = mine.shape[0]
    even = place[1] == 0
    rows[:depth, :] = jnp.where(even, mine[...], other[...])
    rows[depth:, :] = jnp.where(even, other[...], mine[...])


def run_kernel(body, outputs, scalars=0, scratch=(), ties=(), far=(), far_out=(), late=(), lanes={}):
    def call(*operands):
        operands = list(operands)
        count, made = len(operands), len(outputs)

        def whole(*refs):
            inputs, refs = list(refs[:count]), refs[count + len(ties) :]
            results, refs = list(refs[:made]), refs[made:]
            mine, refs = refs[: len(scratch)], refs[len(scratch) :]
            rooms, refs = refs[: len(far)], refs[len(far) :]
            rooms_out, signals = refs[: len(far_out)], refs[len(far_out) :]
            copies = []
            for at, room, signal in zip(far, rooms, signals):
                source = inputs[at].at[:, lanes[at]] if at in lanes else inputs[at]
                copies.append(pltpu.make_async_copy(source, room, signal))
                copies[-1].start()
                inputs[at] = room
            waits = [copy.wait for at, copy in zip(far, copies) if at in late]
            for at, copy in zip(far, copies):
                if at not in late:
                    copy.wait()
            targets = [results[at] for at in far_out]
            for at, room in zip(far_out, rooms_out):
                results[at] = room
            if late:
                body(waits, *inputs, *results, *mine)
            else:
                body(*inputs, *results, *mine)
            copies_out = []
            for room, target, signal in zip(rooms_out, targets, signals[len(far) :]):
                copies_out.append(pltpu.make_async_copy(room, target, signal))
                copies_out[-1].start()
            for copy in copies_out:
                copy.wait()

        rooms = []
        for at in far:
            shape = operands[at].shape
            if at in lanes:
                shape = (shape[0], lanes[at].size)
            rooms.append(pltpu.VMEM(shape, operands[at].dtype))
            operands[at] = pltpu.with_memory_space_constraint(operands[at], pltpu.HBM)
        kinds = list(outputs)
        for at in far_out:
            kinds[at] = pltpu.HBM(kinds[at].shape, kinds[at].dtype)
        spaces = [pltpu.SMEM] * scalars + [pltpu.VMEM] * (count - scalars) + [pl.ANY] * len(ties)
        for at in far:
            spaces[at] = pltpu.HBM
        spaces_out = [pltpu.HBM if at in far_out else pltpu.VMEM for at in range(made)]
        rooms_out = [pltpu.VMEM(outputs[at].shape, outputs[at].dtype) for at in far_out]
        signals = [pltpu.SemaphoreType.DMA] * (len(far) + len(far_out))
        return pl.pallas_call(
            whole,
            out_shape=kinds,
            in_specs=[pl.BlockSpec(memory_space=space) for space in spaces],
            out_specs=[pl.BlockSpec(memory_space=space) for space in spaces_out],
            scratch_shapes=[*scratch, *rooms, *rooms_out, *signals],
            compiler_params=pltpu.CompilerParams(vmem_limit_bytes=24 * 2**20),
        )(*operands, *ties)

    return call


def newton_schulz(waits, place, *refs):
    pieces, refs = refs[:SPLIT], refs[SPLIT:]
    wide, kept, sent, heard, gram, *factors = refs
    chip, core = place[2], place[1]
    width = heard.shape[0]
    for step, piece in enumerate(pieces):
        at = pl.multiple_of((chip ^ step) * piece.shape[0], piece.shape[0])
        heard[pl.ds(at, piece.shape[0]), :] = piece[...]
    depth = kept.shape[0]
    even = core == 0

    @pl.when(even)
    def _():
        gram[...] = dot(heard[...], heard[...], ((1,), (1,)))

    @pl.when(jnp.logical_not(even))
    def _():
        gram[...] = heard[...].astype(jnp.float32)

    at_row = lax.broadcasted_iota(jnp.int32, (width, width), 0)
    at_lane = lax.broadcasted_iota(jnp.int32, (width, width), 1)
    trace = jnp.sum(jnp.where(at_row == at_lane, gram[...], 0.0), keepdims=True)
    scale = jnp.sqrt(trace) + ortho_eps
    gram[...] = gram[...] / (scale * scale)
    count = 2 * depth
    start = pl.multiple_of(chip * count, count)
    for factor in factors:
        gram_b = gram[...].astype(jnp.bfloat16)
        square = dot(gram_b, gram_b, ((1,), (0,)))
        factor[...] = (coef_second * gram[...] + coef_third * square).astype(jnp.bfloat16)
        moved = dot(factor[...], gram_b, ((1,), (0,)))
        twice = dot(factor[...], moved.astype(jnp.bfloat16), ((1,), (0,)))
        gram[...] = coef_first * coef_first * gram[...] + 2.0 * coef_first * moved + twice
    eye = lax.broadcasted_iota(jnp.int32, (count, width), 0) + start
    eye = (eye == lax.broadcasted_iota(jnp.int32, (count, width), 1)).astype(jnp.float32)
    rows = gram[pl.ds(start, count), :]
    square = dot(rows.astype(jnp.bfloat16), gram[...].astype(jnp.bfloat16), ((1,), (0,)))
    rows = coef_first * eye + (coef_second * rows + coef_third * square)
    for factor in factors[::-1]:
        rows = coef_first * rows + dot(rows.astype(jnp.bfloat16), factor[...], ((1,), (0,)))
    waits[0]()
    rows = (rows / scale).astype(jnp.bfloat16)

    @pl.when(even)
    def _():
        state = dot(rows, heard[...], ((1,), (0,))).astype(jnp.bfloat16)
        kept[:, :width] = state[:depth]
        sent[:, :width] = state[depth:]
        kept[:, width:] = jnp.zeros_like(kept[:, width:])
        sent[:, width:] = jnp.zeros_like(sent[:, width:])

    @pl.when(jnp.logical_not(even))
    def _():
        state = dot(rows, wide[...], ((1,), (0,))).astype(jnp.bfloat16)
        kept[...] = state[depth:]
        sent[...] = state[:depth]


def split_device(
    tokens, cotangent, doc_lengths, qkv_w, out_w, ffn_w, vecs, qkv_mom, out_mom, ffn_mom, vec_mom
):
    micro, rows, width = tokens.shape
    shards = lax.axis_size("shard")
    groups = lax.axis_size("dp")
    column = lax.axis_index("shard")
    row = lax.axis_index("dp")
    place = jnp.stack([column, row & 1, row >> 1]).astype(jnp.int32)
    slots = micro * shards
    own = qkv_w.shape[2]
    hidden = ffn_w.shape[2]
    bf16 = jnp.bfloat16

    packed = jnp.concatenate(
        [ffn_w[0], ffn_w[1], qkv_w[0], qkv_w[1], qkv_w[2], jnp.zeros((ffn_w.shape[1], PAD))], axis=1
    ).astype(bf16)
    weights = lax.all_gather(packed, "dp", axis=0, tiled=True)

    flat = tokens.reshape(micro * rows, width)
    vec_rows, vec_own = vecs.shape
    small = jnp.concatenate(
        [vecs.astype(bf16).reshape(-1), doc_lengths.astype(bf16).reshape(-1)]
    )
    small = jnp.pad(small, (0, 8 * width - small.shape[0])).reshape(8, width)
    out_flat = out_w.astype(bf16).reshape(-1, width)
    out_count = out_flat.shape[0]
    heard = gather_direct(jnp.concatenate([flat, out_flat, small], axis=0), "shard")
    tokens_b = heard[:, : micro * rows].reshape(slots * rows, width)
    out_part = heard[:, micro * rows : micro * rows + out_count].reshape(shards, -1, own)
    out_part = out_part.transpose(1, 0, 2).reshape(-1, width)
    small = heard[:, micro * rows + out_count :].reshape(shards, -1)
    lengths = small[:, vecs.size : vecs.size + doc_lengths.size].astype(jnp.int32).reshape(slots, -1)
    small = small[:, : vecs.size].reshape(shards, vec_rows, vec_own).transpose(1, 0, 2).reshape(vec_rows, -1)
    vec = gather_double(small, "dp").transpose(1, 0, 2).reshape(vec_rows, -1).astype(jnp.float32)
    out_b = lax.all_gather(out_part, "dp", axis=0, tiled=True)
    position = jnp.arange(rows, dtype=jnp.int32)[None]
    ends = jnp.cumsum(lengths, axis=1)
    segment = jnp.sum((position[:, :, None] >= ends[:, None, :]).astype(jnp.int32), axis=2)
    valid = position < ends[:, -1:]
    slot = jnp.arange(slots, dtype=jnp.int32)[:, None]
    marks = jnp.where(valid, segment + slot * ends.shape[1], -1 - position - slot * rows)
    id_column, id_row = marks.reshape(-1, 1), marks.reshape(1, -1)
    bias_q = lax.dynamic_slice_in_dim(vec[0], column * own, own, 0)
    bias_v = lax.dynamic_slice_in_dim(vec[1], column * own, own, 0)
    bias_proj = jnp.concatenate([bias_q, jnp.zeros_like(bias_q), bias_v])[None]
    bias_up = lax.dynamic_slice_in_dim(vec[8:].reshape(-1), column * hidden, hidden, 0)[None]

    proj_lanes = pl.ds(2 * hidden, weights.shape[1] - 2 * hidden)
    ffn_lanes = pl.ds(0, 2 * hidden)
    qkv, mixed_own = run_kernel(
        attention_forward,
        [
            jax.ShapeDtypeStruct((slots * rows, 3 * own), bf16),
            jax.ShapeDtypeStruct((BLOCK, slots * rows // BLOCK * own), bf16),
        ],
        scalars=1,
        ties=[vec, bias_up],
        far=(1, 2, 4),
        far_out=(0,),
        lanes={2: proj_lanes},
    )(place, tokens_b, weights, bias_proj, id_column, id_row)

    depth = width // groups
    count = micro * rows
    whole_b = jax.ShapeDtypeStruct((slots * rows, width), bf16)
    own_f = jax.ShapeDtypeStruct((count, width), jnp.float32)
    own_b = jax.ShapeDtypeStruct((count, width), bf16)
    part_kinds = [own_f] + [own_b] * (shards - 1)
    sums_kind = jax.ShapeDtypeStruct((8, width), jnp.float32)
    moving = pltpu.VMEM((slots * rows, width), jnp.float32)

    mixed_pieces = pieces_of(mixed_own, "shard")
    first_b, activ_b, slope, first_in, *parts = run_kernel(
        layer_middle,
        [whole_b, whole_b, jax.ShapeDtypeStruct((slots * rows, hidden), jnp.float32), own_f] + part_kinds,
        scalars=1,
        scratch=[moving],
        far=(5, 6, 8),
        late=(8,),
        lanes={8: ffn_lanes},
    )(place, *mixed_pieces, out_b, tokens_b, vec, weights, bias_up)
    layer_out, d_branch_own, d_second, sums_two = run_kernel(
        second_norm, [own_b, own_b, own_f, sums_kind], scalars=1, far=(7, 8), far_out=(0, 2, 3)
    )(place, *send_parts(parts, "shard"), first_in, vec, cotangent.reshape(count, width), id_column)
    layer_out = layer_out.reshape(tokens.shape)
    d_branch_b, d_inner_b, d_bias_up, *parts = run_kernel(
        inner_backward,
        [whole_b, whole_b, jax.ShapeDtypeStruct((1, hidden), jnp.float32)] + part_kinds,
        scalars=1,
        scratch=[moving],
        far=(6,),
        far_out=(2, 3, 4, 5, 6),
        lanes={6: ffn_lanes},
    )(place, *pieces_of(d_branch_own, "shard"), slope, weights)
    (grads,) = run_kernel(inner_gradients, [jax.ShapeDtypeStruct((2, width, hidden), bf16)], far_out=(0,))(
        first_b, activ_b, d_inner_b, d_branch_b
    )
    summed = lax.psum_scatter(grads, "dp", scatter_dimension=1, tiled=True)
    d_first_in, d_attended_own, sums_one = run_kernel(
        first_norm, [own_f, own_b, sums_kind], far=(0, 4, 5), far_out=(0, 1, 2)
    )(*send_parts(parts, "shard"), d_second, first_in, vec)
    d_attended_pieces = pieces_of(d_attended_own, "shard")
    moment_kind = jax.ShapeDtypeStruct(ffn_mom.shape, ffn_mom.dtype)
    wide_kind = jax.ShapeDtypeStruct((depth, hidden), bf16)
    grad_ffn, new_ffn_mom, mine, far_send = run_kernel(
        wide_momenta,
        [moment_kind, moment_kind, wide_kind, wide_kind],
        scalars=1,
        ties=d_attended_pieces[1:],
        far=(1, 2),
        far_out=(0, 1),
    )(place, summed, ffn_mom)
    far_rows = swap(far_send, "shard", shards // 2)

    packed_rows = depth + 16
    kept, sent, d_proj = run_kernel(
        attention_backward,
        [
            jax.ShapeDtypeStruct((groups // 2, packed_rows, width), jnp.float32),
            jax.ShapeDtypeStruct((groups // 2, packed_rows, width), bf16),
            jax.ShapeDtypeStruct((slots * rows, 3 * own), bf16),
        ],
        scalars=1,
        scratch=[pltpu.VMEM((slots * rows, width), bf16), pltpu.VMEM((16, width), jnp.float32)],
        far=(1, 2, 3, 4, 9, 10, 11, 5, 6, 7, 8, 13, 14, 15),
        far_out=(0, 2),
        late=(5, 6, 7, 8, 13, 14, 15),
        ties=[far_send],
    )(
        place, *d_attended_pieces, *mixed_pieces, out_b, qkv, id_column, id_row, tokens_b,
        sums_one, sums_two, d_bias_up,
    )
    (wide_rows,) = run_kernel(
        join_wide, [jax.ShapeDtypeStruct((depth, 2 * hidden), bf16)], ties=[kept], far_out=(0,)
    )(mine, far_rows)
    wide = lax.all_gather(wide_rows, "dp", axis=0, tiled=True)
    block_kind = jax.ShapeDtypeStruct((packed_rows, width), bf16)
    total, *blocks = run_kernel(
        pair_sum, [jax.ShapeDtypeStruct((packed_rows, width), jnp.float32)] + [block_kind] * 3, scalars=1, far=(1,)
    )(place, kept, swap(sent, "dp", 1))
    block_kind = jax.ShapeDtypeStruct((packed_rows, own), bf16)
    like = [jax.ShapeDtypeStruct(each.shape, each.dtype) for each in (qkv_mom, out_mom)]
    grad_qkv, grad_wout, new_qkv_mom, new_out_mom, *blocks = run_kernel(
        square_momenta,
        like + like + [block_kind] * shards,
        scalars=1,
        scratch=[pltpu.VMEM((shards, packed_rows, own), jnp.float32)],
        far=(5, 6),
        far_out=(0, 1, 2, 3),
    )(place, total, *[swap(block, "dp", 2 * at + 2) for at, block in enumerate(blocks)], qkv_mom, out_mom)
    square_pieces = send_parts(blocks, "shard")
    (gram_rows,) = run_kernel(wide_gram, [jax.ShapeDtypeStruct((depth, width), bf16)], ties=square_pieces[1:], far=(0, 1))(
        wide_rows, wide
    )
    row_kind = jax.ShapeDtypeStruct((depth, width), bf16)
    mine, other, grad_vec = run_kernel(
        join_squares,
        [row_kind, row_kind, jax.ShapeDtypeStruct((packed_rows - depth, own), jnp.float32)],
        scalars=1,
        scratch=[pltpu.VMEM((depth, width), bf16)],
    )(place, *square_pieces, gram_rows, swap(gram_rows, "shard", 1))
    grad_vec = grad_vec[:vec_rows, :vec_own]
    (part,) = run_kernel(
        token_part, [whole_b], ties=[other], far=(0, 1), far_out=(0,), lanes={1: proj_lanes}
    )(d_proj, weights)
    d_tokens = lax.psum_scatter(part, "shard", scatter_dimension=0, tiled=True)
    (pair_rows,) = run_kernel(
        join_pair, [jax.ShapeDtypeStruct((2 * depth, width), bf16)], scalars=1
    )(place, mine, swap(other, "dp", 1))
    pair_pieces = [pair_rows] + [swap(pair_rows, "dp", bit) for bit in (2, 4, 6)]
    state_kind = jax.ShapeDtypeStruct((depth, 2 * hidden), bf16)
    kept, sent = run_kernel(
        newton_schulz,
        [state_kind, state_kind],
        scalars=1,
        scratch=[pltpu.VMEM((width, width), bf16), pltpu.VMEM((width, width), jnp.float32)]
        + [pltpu.VMEM((width, width), bf16)] * (NS_STEPS - 1),
        far=(5,),
        late=(5,),
    )(place, *pair_pieces, wide)
    block_kind = jax.ShapeDtypeStruct((depth, own), bf16)
    wide_kind = jax.ShapeDtypeStruct((depth, hidden), bf16)
    kinds = [block_kind] * shards + [wide_kind]
    kinds[shards // 2] = jax.ShapeDtypeStruct((depth, hidden + own), bf16)
    *blocks, mine = run_kernel(
        split_state, kinds, scalars=1
    )(place, kept, swap(sent, "dp", 1))
    state_pieces = send_parts(blocks, "shard")
    (d_tokens,) = run_kernel(add_rows, [own_f], ties=[state_pieces[1]], far=(0, 1), far_out=(0,))(
        d_first_in, d_tokens
    )
    d_tokens = d_tokens.reshape(tokens.shape)
    qkv_new, out_new, ffn_new = run_kernel(
        new_weights,
        [jax.ShapeDtypeStruct(each.shape, each.dtype) for each in (qkv_w, out_w, ffn_w)],
        scalars=1,
        scratch=[pltpu.VMEM((shards, depth, own), jnp.float32)],
        far=(6, 7, 8),
        far_out=(0, 1, 2),
    )(
        place, *state_pieces, mine, qkv_w, out_w, ffn_w
    )

    token_count = micro * rows * groups * shards
    new_vec_mom = momentum_decay * vec_mom + grad_vec
    vec_new = vecs - vec_rate * token_count ** (-0.5) * new_vec_mom
    return (
        layer_out,
        d_tokens,
        grad_qkv,
        grad_wout,
        grad_ffn,
        grad_vec,
        new_qkv_mom,
        new_out_mom,
        new_ffn_mom,
        new_vec_mom,
        qkv_new,
        out_new,
        ffn_new,
        vec_new,
    )


def solution(mesh):
    fits = (mesh.shape["dp"], mesh.shape["shard"]) == (8, 4)
    in_specs = (
        P(("dp", "shard"), None, None),
        P(("dp", "shard"), None, None),
        P(("dp", "shard"), None),
        P(None, "dp", "shard"),
        P("dp", "shard"),
        P(None, "dp", "shard"),
        P(None, ("dp", "shard")),
        P(None, "dp", "shard"),
        P("dp", "shard"),
        P(None, "dp", "shard"),
        P(None, ("dp", "shard")),
    )
    out_specs = (
        P(("dp", "shard"), None, None),
        P(("dp", "shard"), None, None),
        P(None, "dp", "shard"),
        P("dp", "shard"),
        P(None, "dp", "shard"),
        P(None, ("dp", "shard")),
        P(None, "dp", "shard"),
        P("dp", "shard"),
        P(None, "dp", "shard"),
        P(None, ("dp", "shard")),
        P(None, "dp", "shard"),
        P("dp", "shard"),
        P(None, "dp", "shard"),
        P(None, ("dp", "shard")),
    )
    return jax.shard_map(
        split_device if fits else per_device, mesh=mesh, in_specs=in_specs, out_specs=out_specs, check_vma=False
    )
```

```python
import math
import jax
import jax.numpy as jnp
from jax import lax
from jax.experimental import pallas as pl
from jax.experimental.pallas import tpu as pltpu
from jax.sharding import PartitionSpec as P

D = 768
HEADS = 12
HEAD = 64
FF = 3072
NS_STEPS = 3


masked_score = -1e30
norm_eps = 1e-12
momentum_decay = 0.9
muon_rate = 0.8
vec_rate = 0.5
coef_first = 3.4445
coef_second = -4.775
coef_third = 2.0315
ortho_eps = 1e-07


def spread_2(block, axis, owner):
    block = jnp.where(lax.axis_index(axis) == owner, block, jnp.zeros_like(block))
    return lax.psum(block, axis)


def segments(lengths, rows):
    position = jnp.arange(rows, dtype=jnp.int32)
    ends = jnp.cumsum(lengths)
    segment = jnp.sum((position[:, None] >= ends[None, :]).astype(jnp.int32), axis=1)
    valid = position < ends[-1]
    same = segment[:, None] == segment[None, :]
    allowed = same & valid[:, None] | (position[:, None] == position[None, :])
    return (valid, allowed)


def layer_norm(inputs, gain, bias):
    center = inputs - jnp.mean(inputs, axis=-1, keepdims=True)
    spread = jnp.mean(center * center, axis=-1, keepdims=True)
    return center * lax.rsqrt(spread + norm_eps) * gain + bias


def gelu_exact(inputs):
    return jax.nn.gelu(inputs, approximate=False)


def split_heads(matrix):
    return matrix.reshape(matrix.shape[0], HEADS, HEAD)


def gather_weights(qkv_w, out_w, ffn_w, vecs):
    pieces = (
        qkv_w.astype(jnp.bfloat16),
        out_w.astype(jnp.bfloat16),
        ffn_w.astype(jnp.bfloat16),
        vecs.astype(jnp.bfloat16),
    )
    across = (
        lax.all_gather(pieces[0], "shard", axis=2, tiled=True),
        lax.all_gather(pieces[1], "shard", axis=1, tiled=True),
        lax.all_gather(pieces[2], "shard", axis=2, tiled=True),
        lax.all_gather(pieces[3], "shard", axis=1, tiled=True),
    )
    return (
        lax.all_gather(across[0], "dp", axis=1, tiled=True),
        lax.all_gather(across[1], "dp", axis=0, tiled=True),
        lax.all_gather(across[2], "dp", axis=1, tiled=True),
        lax.all_gather(across[3], "dp", axis=1, tiled=True),
    )


def attention_scores(queries_b, keys_b, allowed):
    scores = jnp.einsum(
        "qhd,khd->hqk",
        split_heads(queries_b),
        split_heads(keys_b),
        preferred_element_type=jnp.float32,
    )
    return jnp.where(allowed[None], scores * HEAD ** (-0.5), masked_score)


def forward_pass(tokens_b, lengths, weights):
    qkv_b, out_b, ffn_b, vec_b = weights
    vec = vec_b.astype(jnp.float32)
    rows = tokens_b.shape[0]
    valid, allowed = segments(lengths, rows)
    projected = jnp.einsum("rd,kde->kre", tokens_b, qkv_b, preferred_element_type=jnp.float32)
    queries_b = (projected[0] + vec[0]).astype(jnp.bfloat16)
    keys_b = projected[1].astype(jnp.bfloat16)
    values_b = (projected[2] + vec[1]).astype(jnp.bfloat16)
    scores = attention_scores(queries_b, keys_b, allowed)
    largest = jnp.max(scores, axis=-1, keepdims=True)
    exponent = jnp.exp(scores - largest)
    totals = jnp.sum(exponent, axis=-1, keepdims=True)
    logsum = largest + jnp.log(totals)
    probs_b = (exponent / totals).astype(jnp.bfloat16)
    mixed = jnp.einsum(
        "hqk,khd->qhd", probs_b, split_heads(values_b), preferred_element_type=jnp.float32
    )
    mixed_b = mixed.reshape(rows, -1).astype(jnp.bfloat16)
    attended = jnp.dot(mixed_b, out_b, preferred_element_type=jnp.float32) + vec[2]
    first_in = tokens_b.astype(jnp.float32) + attended
    first = layer_norm(first_in, vec[3], vec[4])
    first_b = first.astype(jnp.bfloat16)
    inner = jnp.dot(first_b, ffn_b[0], preferred_element_type=jnp.float32) + vec[8:].reshape(-1)
    activ_b = gelu_exact(inner).astype(jnp.bfloat16)
    branch = jnp.einsum("rf,df->rd", activ_b, ffn_b[1], preferred_element_type=jnp.float32) + vec[5]
    second_in = first + branch
    result = layer_norm(second_in, vec[6], vec[7]) * valid[:, None].astype(jnp.float32)
    kept = (
        queries_b,
        keys_b,
        values_b,
        logsum,
        mixed_b,
        first_in,
        first_b,
        inner,
        activ_b,
        second_in,
    )
    return (result.astype(jnp.bfloat16), kept)


def backward_pass(cot_b, tokens_b, lengths, weights, kept):
    qkv_b, out_b, ffn_b, vec_b = weights
    vec = vec_b.astype(jnp.float32)
    queries_b, keys_b, values_b, logsum, mixed_b, first_in, first_b, inner, activ_b, second_in = (
        kept
    )
    rows = tokens_b.shape[0]
    valid, allowed = segments(lengths, rows)
    grad_out = cot_b.astype(jnp.float32) * valid[:, None].astype(jnp.float32)
    unused, pull_two = jax.vjp(layer_norm, second_in, vec[6], vec[7])
    d_second, d_gain_two, d_shift_two = pull_two(grad_out)
    d_branch_b = d_second.astype(jnp.bfloat16)
    d_bias_down = jnp.sum(d_branch_b.astype(jnp.float32), axis=0)
    d_activ = jnp.dot(d_branch_b, ffn_b[1], preferred_element_type=jnp.float32)
    unused, pull_gelu = jax.vjp(gelu_exact, inner)
    (d_inner,) = pull_gelu(d_activ)
    d_inner_b = d_inner.astype(jnp.bfloat16)
    d_bias_up = jnp.sum(d_inner_b.astype(jnp.float32), axis=0)
    d_first = d_second + jnp.einsum(
        "rf,df->rd", d_inner_b, ffn_b[0], preferred_element_type=jnp.float32
    )
    unused, pull_one = jax.vjp(layer_norm, first_in, vec[3], vec[4])
    d_first_in, d_gain_one, d_shift_one = pull_one(d_first)
    d_attended_b = d_first_in.astype(jnp.bfloat16)
    d_bias_out = jnp.sum(d_attended_b.astype(jnp.float32), axis=0)
    d_mixed_b = jnp.einsum(
        "re,de->rd", d_attended_b, out_b, preferred_element_type=jnp.float32
    ).astype(jnp.bfloat16)
    scores = attention_scores(queries_b, keys_b, allowed)
    probs = jnp.exp(scores - logsum)
    mixed_heads = split_heads(d_mixed_b)
    d_probs = jnp.einsum(
        "qhd,khd->hqk", mixed_heads, split_heads(values_b), preferred_element_type=jnp.float32
    )
    d_values = jnp.einsum(
        "hqk,qhd->khd", probs.astype(jnp.bfloat16), mixed_heads, preferred_element_type=jnp.float32
    )
    d_scores_b = (probs * (d_probs - jnp.sum(probs * d_probs, axis=-1, keepdims=True))).astype(
        jnp.bfloat16
    )
    d_queries = jnp.einsum(
        "hqk,khd->qhd", d_scores_b, split_heads(keys_b), preferred_element_type=jnp.float32
    ) * HEAD ** (-0.5)
    d_keys = jnp.einsum(
        "hqk,qhd->khd", d_scores_b, split_heads(queries_b), preferred_element_type=jnp.float32
    ) * HEAD ** (-0.5)
    d_proj_b = jnp.stack([d_queries, d_keys, d_values]).reshape(3, rows, -1).astype(jnp.bfloat16)
    d_tokens = d_first_in + jnp.einsum(
        "kre,kde->rd", d_proj_b, qkv_b, preferred_element_type=jnp.float32
    )
    proj_sums = jnp.sum(d_proj_b.astype(jnp.float32), axis=1)
    grad_vec = jnp.concatenate(
        [
            jnp.stack(
                [
                    proj_sums[0],
                    proj_sums[2],
                    d_bias_out,
                    d_gain_one,
                    d_shift_one,
                    d_bias_down,
                    d_gain_two,
                    d_shift_two,
                ]
            ),
            d_bias_up.reshape(-1, vec.shape[1]),
        ],
        axis=0,
    )
    factors = (d_branch_b, activ_b, first_b, d_inner_b, mixed_b, d_attended_b, d_proj_b)
    return (d_tokens, factors, grad_vec)


def orthogonalize_pair(square, wide):
    matrices = (square, wide)
    present = tuple((matrix.astype(jnp.bfloat16) for matrix in matrices))
    states = matrices
    for step in range(NS_STEPS):
        partial_value = tuple(
            (
                jnp.einsum("iw,jw->ij", block, block, preferred_element_type=jnp.float32)
                for block in present
            )
        )
        gram_part = (
            lax.psum_scatter(
                partial_value[0].astype(jnp.bfloat16), "shard", scatter_dimension=0, tiled=True
            ).astype(jnp.float32),
            lax.psum_scatter(
                partial_value[1].astype(jnp.bfloat16), "shard", scatter_dimension=0, tiled=True
            ).astype(jnp.float32),
        )
        grams = (
            lax.all_gather(gram_part[0].astype(jnp.bfloat16), "shard", axis=0, tiled=True).astype(
                jnp.float32
            ),
            lax.all_gather(gram_part[1].astype(jnp.bfloat16), "shard", axis=0, tiled=True).astype(
                jnp.float32
            ),
        )
        if step == 0:
            scales = tuple((jnp.sqrt(jnp.trace(gram)) + ortho_eps for gram in grams))
            grams = tuple((gram / (scale * scale) for gram, scale in zip(grams, scales)))
            present = tuple(
                ((matrix / scale).astype(jnp.bfloat16) for matrix, scale in zip(matrices, scales))
            )
        renewed = []
        for gram, current in zip(grams, present):
            gram_b = gram.astype(jnp.bfloat16)
            once = jnp.dot(gram_b, current, preferred_element_type=jnp.float32)
            twice = jnp.dot(gram_b, once.astype(jnp.bfloat16), preferred_element_type=jnp.float32)
            renewed.append(
                coef_first * current.astype(jnp.float32) + coef_second * once + coef_third * twice
            )
        states = tuple(renewed)
        present = tuple((state.astype(jnp.bfloat16) for state in states))
    return states


def per_device(
    tokens, cotangent, doc_lengths, qkv_w, out_w, ffn_w, vecs, qkv_mom, out_mom, ffn_mom, vec_mom
):
    micro = tokens.shape[0]
    shared = gather_weights(qkv_w, out_w, ffn_w, vecs)
    outputs = []
    stored = []
    for index in range(micro):
        weights = shared
        result_b, kept = forward_pass(tokens[index], doc_lengths[index], weights)
        outputs.append(result_b)
        stored.append(kept)
    grad_rows = [None] * micro
    factor_list = [None] * micro
    vec_total = None
    for index in reversed(range(micro)):
        weights = shared
        d_tokens, factors, vec_part = backward_pass(
            cotangent[index], tokens[index], doc_lengths[index], weights, stored[index]
        )
        grad_rows[index] = d_tokens
        factor_list[index] = factors
        vec_total = vec_part if vec_total is None else vec_total + vec_part
    (
        branch_gradient_rows,
        activation_rows,
        first_norm_rows,
        inner_gradient_rows,
        mixed_all,
        d_attended_all,
        d_proj_all,
    ) = [jnp.stack([factors[place] for factors in factor_list]) for place in range(7)]
    grad_down = jnp.einsum(
        "hzo,hzx->ox", branch_gradient_rows, activation_rows, preferred_element_type=jnp.float32
    )
    up_weight_gradient = jnp.einsum(
        "hzo,hzx->ox", first_norm_rows, inner_gradient_rows, preferred_element_type=jnp.float32
    )
    grad_wout_sum = jnp.einsum(
        "mrd,mre->de", mixed_all, d_attended_all, preferred_element_type=jnp.float32
    )
    grad_qkv_sum = jnp.einsum(
        "mrd,mkre->kde", tokens, d_proj_all, preferred_element_type=jnp.float32
    )
    summed = (grad_qkv_sum, grad_wout_sum, jnp.stack([up_weight_gradient, grad_down]), vec_total)
    reduced = (
        lax.psum_scatter(
            summed[0].astype(jnp.bfloat16), "dp", scatter_dimension=1, tiled=True
        ).astype(jnp.float32),
        lax.psum_scatter(
            summed[1].astype(jnp.bfloat16), "dp", scatter_dimension=0, tiled=True
        ).astype(jnp.float32),
        lax.psum_scatter(
            summed[2].astype(jnp.bfloat16), "dp", scatter_dimension=1, tiled=True
        ).astype(jnp.float32),
        lax.psum_scatter(
            summed[3].astype(jnp.bfloat16), "dp", scatter_dimension=1, tiled=True
        ).astype(jnp.float32),
    )
    grad_qkv, grad_wout, grad_ffn, grad_vec = (
        lax.psum_scatter(
            reduced[0].astype(jnp.bfloat16), "shard", scatter_dimension=2, tiled=True
        ).astype(jnp.float32),
        lax.psum_scatter(
            reduced[1].astype(jnp.bfloat16), "shard", scatter_dimension=1, tiled=True
        ).astype(jnp.float32),
        lax.psum_scatter(
            reduced[2].astype(jnp.bfloat16), "shard", scatter_dimension=2, tiled=True
        ).astype(jnp.float32),
        lax.psum_scatter(
            reduced[3].astype(jnp.bfloat16), "shard", scatter_dimension=1, tiled=True
        ).astype(jnp.float32),
    )
    new_qkv_mom = momentum_decay * qkv_mom + grad_qkv
    new_out_mom = momentum_decay * out_mom + grad_wout
    new_ffn_mom = momentum_decay * ffn_mom + grad_ffn
    square_local = jnp.concatenate([new_qkv_mom, new_out_mom[None]], axis=0)
    square_cols, wide_cols = (
        lax.all_gather(square_local.astype(jnp.bfloat16), "dp", axis=1, tiled=True).astype(
            square_local.dtype
        ),
        lax.all_gather(new_ffn_mom.astype(jnp.bfloat16), "dp", axis=1, tiled=True).astype(
            new_ffn_mom.dtype
        ),
    )
    row = lax.axis_index("dp")
    rows_count = lax.axis_size("dp")
    owners = [place * rows_count // 6 for place in range(6)]
    square_pick = sum(((row == owners[place]).astype(jnp.int32) * place for place in range(4)))
    wide_pick = (row == owners[5]).astype(jnp.int32)
    square_state, wide_state = orthogonalize_pair(
        lax.dynamic_index_in_dim(square_cols, square_pick, 0, keepdims=False),
        lax.dynamic_index_in_dim(wide_cols, wide_pick, 0, keepdims=False),
    )
    depth = qkv_w.shape[1]
    square_rows = []
    for place in range(4):
        whole = spread_2(square_state.astype(jnp.bfloat16), "dp", owners[place]).astype(
            square_state.dtype
        )
        square_rows.append(lax.dynamic_slice_in_dim(whole, row * depth, depth, 0))
    wide_rows = []
    for place in range(4, 6):
        whole = spread_2(wide_state.astype(jnp.bfloat16), "dp", owners[place]).astype(
            wide_state.dtype
        )
        wide_rows.append(lax.dynamic_slice_in_dim(whole, row * depth, depth, 0))
    qkv_new = qkv_w - muon_rate * jnp.stack(square_rows[:3])
    out_new = out_w - muon_rate * square_rows[3]
    ffn_new = ffn_w - muon_rate * (FF / D) ** 0.5 * jnp.stack(wide_rows)
    token_count = tokens.shape[0] * tokens.shape[1] * lax.axis_size("dp") * lax.axis_size("shard")
    new_vec_mom = momentum_decay * vec_mom + grad_vec
    vec_new = vecs - vec_rate * token_count ** (-0.5) * new_vec_mom
    return (
        jnp.stack(outputs),
        jnp.stack(grad_rows),
        grad_qkv,
        grad_wout,
        grad_ffn,
        grad_vec,
        new_qkv_mom,
        new_out_mom,
        new_ffn_mom,
        new_vec_mom,
        qkv_new,
        out_new,
        ffn_new,
        vec_new,
    )


def gather_direct(block, axis):
    count = lax.axis_size(axis)
    me = lax.axis_index(axis)
    whole = jnp.zeros((count,) + block.shape, block.dtype)
    whole = lax.dynamic_update_index_in_dim(whole, block, me, 0)
    for step in range(1, count):
        got = lax.ppermute(block, axis, [(i, (i + step) % count) for i in range(count)])
        whole = lax.dynamic_update_index_in_dim(whole, got, lax.rem(me - step + count, count), 0)
    return whole


def pieces_of(block, axis):
    count = lax.axis_size(axis)
    return [block] + [
        lax.ppermute(block, axis, [(i, (i + step) % count) for i in range(count)])
        for step in range(1, count)
    ]


def send_parts(parts, axis):
    count = lax.axis_size(axis)
    return [parts[0]] + [
        lax.ppermute(parts[step], axis, [(i, (i + step) % count) for i in range(count)])
        for step in range(1, count)
    ]


def swap(block, axis, bit):
    return lax.ppermute(block, axis, [(i, i ^ bit) for i in range(lax.axis_size(axis))])


def gather_double(block, axis):
    me = lax.axis_index(axis)
    bit = 1
    whole = block[None]
    while bit < lax.axis_size(axis):
        other = swap(whole, axis, bit)
        high = (me & bit) != 0
        whole = jnp.concatenate(
            [jnp.where(high, other, whole), jnp.where(high, whole, other)], axis=0
        )
        bit *= 2
    return whole


def dot(left, right, dims):
    return lax.dot_general(left, right, (dims, ((), ())), preferred_element_type=jnp.float32)


def norm_parts(inputs):
    center = inputs - jnp.mean(inputs, axis=-1, keepdims=True)
    spread = jnp.mean(center * center, axis=-1, keepdims=True)
    scale = lax.rsqrt(spread + norm_eps)
    return center * scale, scale


def norm_back(grad, unit, scale, gain):
    scaled = grad * gain
    mean_grad = jnp.mean(scaled, axis=-1, keepdims=True)
    mean_unit = jnp.mean(scaled * unit, axis=-1, keepdims=True)
    return scale * (scaled - mean_grad - unit * mean_unit)


BLOCK = 256
PAD = 64
SPLIT = 4


def source_of(column, step):
    return lax.rem(column - step + SPLIT, SPLIT)


def put_pieces(pieces, column, whole):
    count = pieces[0].shape[0]
    for step, piece in enumerate(pieces):
        at = pl.multiple_of(source_of(column, step) * count, count)
        whole[pl.ds(at, count), :] = piece[...]


def take_parts(whole, column, parts):
    count = parts[0].shape[0]
    for step, part in enumerate(parts):
        at = pl.multiple_of(lax.rem(column + step, SPLIT) * count, count)
        part[...] = whole[pl.ds(at, count), :].astype(part.dtype)


def sum_pieces(pieces):
    total = pieces[0][...]
    for piece in pieces[1:]:
        total = total + piece[...].astype(jnp.float32)
    return total


def row_sums(values):
    return jnp.sum(values, axis=0, keepdims=True)


def unpack_rows(piece, rows):
    count = rows // piece.shape[0]
    own = piece.shape[1] // count
    return jnp.concatenate([piece[:, at * own : (at + 1) * own] for at in range(count)], axis=0)


def layer_middle(waits, place, *refs):
    pieces, refs = refs[:SPLIT], refs[SPLIT:]
    out_weight, tokens, vec, weights, bias_up, first_b, activ_b, slope, first_in, *refs = refs
    parts, (moving,) = refs[:SPLIT], refs[SPLIT:]
    column = place[0]
    attended = vec[2:3, :] + tokens[...].astype(jnp.float32)
    for step, piece in enumerate(pieces):
        rows = unpack_rows(piece, tokens.shape[0])
        own = rows.shape[1]
        at = pl.multiple_of(source_of(column, step) * own, own)
        attended = attended + dot(rows, out_weight[pl.ds(at, own), :], ((1,), (0,)))
    moving[...] = attended
    take_parts(moving, column, [first_in])
    unit, scale = norm_parts(attended)
    first_b[...] = (unit * vec[3:4, :] + vec[4:5, :]).astype(jnp.bfloat16)
    hidden = slope.shape[1]
    waits[0]()
    inner = dot(first_b[...], weights[:, :hidden], ((1,), (0,))) + bias_up[...]
    cdf = 0.5 * (1.0 + lax.erf(inner * 2.0 ** (-0.5)))
    activ_b[...] = (inner * cdf).astype(jnp.bfloat16)
    slope[...] = cdf + inner * jnp.exp(-0.5 * inner * inner) * (2.0 * math.pi) ** (-0.5)
    moving[...] = dot(activ_b[...], weights[:, hidden : 2 * hidden], ((1,), (1,)))
    take_parts(moving, column, parts)


def second_norm(place, *refs):
    pieces, refs = refs[:SPLIT], refs[SPLIT:]
    first_in, vec, cotangent, ids, layer_out, d_branch, d_second, sums = refs
    count = first_in.shape[0]
    at = pl.multiple_of(place[0] * count, count)
    valid = (ids[pl.ds(at, count), :] >= 0).astype(jnp.float32)
    unit, scale = norm_parts(first_in[...])
    first = unit * vec[3:4, :] + vec[4:5, :]
    unit, scale = norm_parts(first + (sum_pieces(pieces) + vec[5:6, :]))
    layer_out[...] = ((unit * vec[6:7, :] + vec[7:8, :]) * valid).astype(jnp.bfloat16)
    grad = cotangent[...].astype(jnp.float32) * valid
    d_rows = norm_back(grad, unit, scale, vec[6:7, :])
    d_second[...] = d_rows
    d_branch[...] = d_rows.astype(jnp.bfloat16)
    sums[0:1, :] = row_sums(d_branch[...].astype(jnp.float32))
    sums[1:2, :] = row_sums(grad * unit)
    sums[2:3, :] = row_sums(grad)


def inner_backward(place, *refs):
    pieces, refs = refs[:SPLIT], refs[SPLIT:]
    slope, weights, d_branch, d_inner, sums, *refs = refs
    parts, (moving,) = refs[:SPLIT], refs[SPLIT:]
    column = place[0]
    put_pieces(pieces, column, d_branch)
    hidden = slope.shape[1]
    d_activ = dot(d_branch[...], weights[:, hidden : 2 * hidden], ((1,), (0,)))
    d_inner[...] = (d_activ * slope[...]).astype(jnp.bfloat16)
    sums[...] = row_sums(d_inner[...].astype(jnp.float32))
    moving[...] = dot(d_inner[...], weights[:, :hidden], ((1,), (1,)))
    take_parts(moving, column, parts)


def inner_gradients(first_b, activ_b, d_inner, d_branch, grads):
    grads[0] = dot(first_b[...], d_inner[...], ((0,), (0,))).astype(jnp.bfloat16)
    grads[1] = dot(d_branch[...], activ_b[...], ((0,), (0,))).astype(jnp.bfloat16)


def wide_momenta(place, summed, moments, grads, moments_new, mine, far):
    low = place[0] < SPLIT // 2
    for part in range(2):
        grads[part] = summed[part].astype(jnp.float32)
        moments_new[part] = momentum_decay * moments[part] + grads[part]
    first, second = moments_new[0].astype(jnp.bfloat16), moments_new[1].astype(jnp.bfloat16)
    mine[...] = jnp.where(low, first, second)
    far[...] = jnp.where(low, second, first)


def join_wide(mine, far, rows):
    hidden = mine.shape[1]
    rows[:, :hidden] = mine[...]
    rows[:, hidden:] = far[...]


def wide_gram(rows, wide, gram):
    gram[...] = dot(rows[...], wide[...], ((1,), (1,))).astype(jnp.bfloat16)


def first_norm(*refs):
    pieces, refs = refs[:SPLIT], refs[SPLIT:]
    d_second, first_in, vec, d_first_in, d_attended, sums = refs
    unit, scale = norm_parts(first_in[...])
    grad = sum_pieces(pieces) + d_second[...]
    d_rows = norm_back(grad, unit, scale, vec[3:4, :])
    d_first_in[...] = d_rows
    d_attended[...] = d_rows.astype(jnp.bfloat16)
    sums[0:1, :] = row_sums(d_attended[...].astype(jnp.float32))
    sums[1:2, :] = row_sums(grad * unit)
    sums[2:3, :] = row_sums(grad)


def split_state(place, kept, other, *refs):
    blocks, (mine,) = refs[:SPLIT], refs[SPLIT:]
    column, even = place[0], place[1] == 0
    own, hidden = blocks[0].shape[1], mine.shape[1]
    far = blocks[SPLIT // 2]
    for step, block in enumerate(blocks):
        there = lax.rem(column + step, SPLIT)
        for at in range(SPLIT):
            lanes = slice(at * own, (at + 1) * own)

            @pl.when(there == at)
            def _():
                block[:, block.shape[1] - own :] = jnp.where(even, kept[:, lanes], other[:, lanes])

    mine[...] = jnp.where(even, other[:, :hidden], kept[:, :hidden])
    far[:, :hidden] = jnp.where(even, other[:, hidden:], kept[:, hidden:])


def new_weights(place, *refs):
    pieces, refs = refs[:SPLIT], refs[SPLIT:]
    mine, qkv_w, out_w, ffn_w, qkv_new, out_new, ffn_new, state = refs
    low = place[0] < SPLIT // 2
    own, hidden = out_w.shape[1], mine.shape[1]
    far = pieces[SPLIT // 2][:, :hidden]
    for step, piece in enumerate(pieces):
        state[source_of(place[0], step)] = piece[:, piece.shape[1] - own :].astype(jnp.float32)
    for at in range(SPLIT - 1):
        qkv_new[at] = qkv_w[at] - muon_rate * state[at]
    out_new[...] = out_w[...] - muon_rate * state[SPLIT - 1]
    rate = muon_rate * (FF / D) ** 0.5
    ffn_new[0] = ffn_w[0] - rate * jnp.where(low, mine[...], far).astype(jnp.float32)
    ffn_new[1] = ffn_w[1] - rate * jnp.where(low, far, mine[...]).astype(jnp.float32)


def probabilities(qkv, rows_at, head, own, id_column, id_row):
    queries = qkv[rows_at, head * HEAD : (head + 1) * HEAD]
    keys = qkv[rows_at, own + head * HEAD : own + (head + 1) * HEAD]
    values = qkv[rows_at, 2 * own + head * HEAD : 2 * own + (head + 1) * HEAD]
    scores = dot(queries, keys, ((1,), (1,))) * HEAD ** (-0.5)
    scores = jnp.where(id_column[rows_at, :] == id_row[:, rows_at], scores, masked_score)
    exponent = jnp.exp(scores - jnp.max(scores, axis=-1, keepdims=True))
    probs = exponent / jnp.sum(exponent, axis=-1, keepdims=True)
    return queries, keys, values, probs


def attention_forward(place, tokens, weight, bias, id_column, id_row, qkv, mixed):
    own = qkv.shape[1] // 3
    proj = weight[:, : 3 * own]
    qkv[...] = (dot(tokens[...], proj, ((1,), (0,))) + bias[...]).astype(jnp.bfloat16)
    for start in range(0, tokens.shape[0], BLOCK):
        rows_at = slice(start, start + BLOCK)
        for head in range(own // HEAD):
            queries, keys, values, probs = probabilities(qkv, rows_at, head, own, id_column, id_row)
            part = dot(probs.astype(jnp.bfloat16), values, ((1,), (0,)))
            at = start // BLOCK * own + head * HEAD
            mixed[:, at : at + HEAD] = part.astype(jnp.bfloat16)


def attention_backward(waits, place, *refs):
    pieces, mixed, refs = refs[:SPLIT], refs[SPLIT : 2 * SPLIT], refs[2 * SPLIT :]
    out_weight, qkv, id_column, id_row, tokens, sums_one, sums_two, sums_up, *refs = refs
    kept, sent, d_proj, d_attended, sums = refs
    rows, width = tokens.shape
    own = qkv.shape[1] // 3
    column, core = place[0], place[1]
    put_pieces(pieces, column, d_attended)
    out_rows = out_weight[pl.ds(pl.multiple_of(column * own, own), own), :]
    d_mixed = dot(d_attended[...], out_rows, ((1,), (1,))).astype(jnp.bfloat16)
    for start in range(0, rows, BLOCK):
        rows_at = slice(start, start + BLOCK)
        for head in range(own // HEAD):
            queries, keys, values, probs = probabilities(qkv, rows_at, head, own, id_column, id_row)
            d_out = d_mixed[rows_at, head * HEAD : (head + 1) * HEAD]
            d_probs = dot(d_out, values, ((1,), (1,)))
            d_scores = probs * (d_probs - jnp.sum(probs * d_probs, axis=-1, keepdims=True))
            d_scores = d_scores.astype(jnp.bfloat16)
            d_values = dot(probs.astype(jnp.bfloat16), d_out, ((0,), (0,)))
            d_queries = dot(d_scores, keys, ((1,), (0,))) * HEAD ** (-0.5)
            d_keys = dot(d_scores, queries, ((0,), (0,))) * HEAD ** (-0.5)
            for part, value in enumerate((d_queries, d_keys, d_values)):
                at = part * own + head * HEAD
                d_proj[rows_at, at : at + HEAD] = value.astype(jnp.bfloat16)
    d_proj_all = d_proj[...]
    d_columns = d_attended[:, :own]
    for place_at in range(1, width // own):
        other = d_attended[:, place_at * own : (place_at + 1) * own]
        d_columns = jnp.where(column == place_at, other, d_columns)
    for wait in waits:
        wait()
    grad_proj = dot(tokens[...], d_proj_all, ((0,), (0,)))
    proj_sums = row_sums(d_proj_all.astype(jnp.float32))
    sums[...] = jnp.zeros_like(sums)
    for at in range(SPLIT):
        lanes = slice(at * own, (at + 1) * own)
        mine = (column == at).astype(jnp.float32)
        sums[0:1, lanes] = proj_sums[:, :own] * mine
        sums[1:2, lanes] = proj_sums[:, 2 * own :] * mine
        sums[8 + at : 9 + at, :] = sums_up[...] * mine
    sums[2:5, :] = sums_one[0:3, :]
    sums[5:8, :] = sums_two[0:3, :]
    depth = kept.shape[1] - sums.shape[0]
    for group in range(width // depth):
        at = slice(group * depth, (group + 1) * depth)

        def put(target, kind):
            target[group // 2, :depth, : 3 * own] = grad_proj[at].astype(kind)
            target[group // 2, depth:, :] = jnp.zeros((sums.shape[0], width), kind)
            target[group // 2, depth:, :depth] = sums[:, at].astype(kind)

        pl.when(core == group % 2)(lambda: put(kept, jnp.float32))
        pl.when(core != group % 2)(lambda: put(sent, jnp.bfloat16))
    for step, piece in enumerate(mixed):
        grad_out = dot(unpack_rows(piece, rows), d_columns, ((0,), (0,)))
        source = source_of(column, step)
        for half in range(2):
            block = grad_out[half * depth : (half + 1) * depth]

            def put_out(target, kind):
                target[source, :depth, 3 * own :] = block.astype(kind)

            pl.when(core == half)(lambda: put_out(kept, jnp.float32))
            pl.when(core != half)(lambda: put_out(sent, jnp.bfloat16))


def token_part(d_proj, weight, part):
    proj = weight[:, : d_proj.shape[1]]
    part[...] = dot(d_proj[...], proj, ((1,), (1,))).astype(jnp.bfloat16)


def add_rows(left, right, total):
    total[...] = left[...] + right[...].astype(jnp.float32)


def pair_sum(place, kept, other, total, *blocks):
    chip = place[2]
    total[...] = kept[chip] + other[chip].astype(jnp.float32)
    for step, block in enumerate(blocks):
        at = chip ^ (step + 1)
        block[...] = (kept[at] + other[at].astype(jnp.float32)).astype(jnp.bfloat16)


def square_momenta(place, total, *refs):
    pieces, refs = refs[: SPLIT - 1], refs[SPLIT - 1 :]
    qkv_mom, out_mom, qkv_grad, out_grad, qkv_new, out_new, *refs = refs
    blocks, state = refs[:SPLIT], refs[SPLIT]
    depth, own = out_mom.shape
    whole = sum_pieces([total, *pieces])
    vec_own = depth // SPLIT
    for at in range(SPLIT):
        grad = whole[:depth, at * own : (at + 1) * own]
        if at < SPLIT - 1:
            qkv_grad[at] = grad
            moment = momentum_decay * qkv_mom[at] + grad
            qkv_new[at] = moment
        else:
            out_grad[...] = grad
            moment = momentum_decay * out_mom[...] + grad
            out_new[...] = moment
        state[at, :depth, :] = moment
        state[at, depth:, :] = jnp.zeros((whole.shape[0] - depth, own), jnp.float32)
        state[at, depth:, :vec_own] = whole[depth:, at * vec_own : (at + 1) * vec_own]
    for step, block in enumerate(blocks):
        block[...] = state[lax.rem(place[0] + step, SPLIT)].astype(jnp.bfloat16)


def join_squares(place, *refs):
    pieces, (gram, gram_other, mine, other, sums, rows) = refs[:SPLIT], refs[SPLIT:]
    depth, own = mine.shape[0], pieces[0].shape[1]
    total = jnp.zeros(sums.shape, jnp.float32)
    for step, piece in enumerate(pieces):
        total = total + piece[depth:, :].astype(jnp.float32)
        for at in range(SPLIT):

            @pl.when(source_of(place[0], step) == at)
            def _():
                rows[:, at * own : (at + 1) * own] = piece[:depth, :]

    sums[...] = total
    even = place[1] == 0
    gram_sum = (gram[...].astype(jnp.float32) + gram_other[...].astype(jnp.float32)).astype(jnp.bfloat16)
    mine[...] = jnp.where(even, rows[...], gram_sum)
    other[...] = jnp.where(even, gram_sum, rows[...])


def join_pair(place, mine, other, rows):
    depth = mine.shape[0]
    even = place[1] == 0
    rows[:depth, :] = jnp.where(even, mine[...], other[...])
    rows[depth:, :] = jnp.where(even, other[...], mine[...])


def run_kernel(body, outputs, scalars=0, scratch=(), ties=(), far=(), far_out=(), late=(), lanes={}):
    def call(*operands):
        operands = list(operands)
        count, made = len(operands), len(outputs)

        def whole(*refs):
            inputs, refs = list(refs[:count]), refs[count + len(ties) :]
            results, refs = list(refs[:made]), refs[made:]
            mine, refs = refs[: len(scratch)], refs[len(scratch) :]
            rooms, refs = refs[: len(far)], refs[len(far) :]
            rooms_out, signals = refs[: len(far_out)], refs[len(far_out) :]
            copies = []
            for at, room, signal in zip(far, rooms, signals):
                source = inputs[at].at[:, lanes[at]] if at in lanes else inputs[at]
                copies.append(pltpu.make_async_copy(source, room, signal))
                copies[-1].start()
                inputs[at] = room
            waits = [copy.wait for at, copy in zip(far, copies) if at in late]
            for at, copy in zip(far, copies):
                if at not in late:
                    copy.wait()
            targets = [results[at] for at in far_out]
            for at, room in zip(far_out, rooms_out):
                results[at] = room
            if late:
                body(waits, *inputs, *results, *mine)
            else:
                body(*inputs, *results, *mine)
            copies_out = []
            for room, target, signal in zip(rooms_out, targets, signals[len(far) :]):
                copies_out.append(pltpu.make_async_copy(room, target, signal))
                copies_out[-1].start()
            for copy in copies_out:
                copy.wait()

        rooms = []
        for at in far:
            shape = operands[at].shape
            if at in lanes:
                shape = (shape[0], lanes[at].size)
            rooms.append(pltpu.VMEM(shape, operands[at].dtype))
            operands[at] = pltpu.with_memory_space_constraint(operands[at], pltpu.HBM)
        kinds = list(outputs)
        for at in far_out:
            kinds[at] = pltpu.HBM(kinds[at].shape, kinds[at].dtype)
        spaces = [pltpu.SMEM] * scalars + [pltpu.VMEM] * (count - scalars) + [pl.ANY] * len(ties)
        for at in far:
            spaces[at] = pltpu.HBM
        spaces_out = [pltpu.HBM if at in far_out else pltpu.VMEM for at in range(made)]
        rooms_out = [pltpu.VMEM(outputs[at].shape, outputs[at].dtype) for at in far_out]
        signals = [pltpu.SemaphoreType.DMA] * (len(far) + len(far_out))
        return pl.pallas_call(
            whole,
            out_shape=kinds,
            in_specs=[pl.BlockSpec(memory_space=space) for space in spaces],
            out_specs=[pl.BlockSpec(memory_space=space) for space in spaces_out],
            scratch_shapes=[*scratch, *rooms, *rooms_out, *signals],
            compiler_params=pltpu.CompilerParams(vmem_limit_bytes=24 * 2**20),
        )(*operands, *ties)

    return call


def newton_schulz(waits, place, *refs):
    pieces, refs = refs[:SPLIT], refs[SPLIT:]
    wide, kept, sent, heard, gram, *factors = refs
    chip, core = place[2], place[1]
    width = heard.shape[0]
    for step, piece in enumerate(pieces):
        at = pl.multiple_of((chip ^ step) * piece.shape[0], piece.shape[0])
        heard[pl.ds(at, piece.shape[0]), :] = piece[...]
    depth = kept.shape[0]
    even = core == 0

    @pl.when(even)
    def _():
        gram[...] = dot(heard[...], heard[...], ((1,), (1,)))

    @pl.when(jnp.logical_not(even))
    def _():
        gram[...] = heard[...].astype(jnp.float32)

    at_row = lax.broadcasted_iota(jnp.int32, (width, width), 0)
    at_lane = lax.broadcasted_iota(jnp.int32, (width, width), 1)
    trace = jnp.sum(jnp.where(at_row == at_lane, gram[...], 0.0), keepdims=True)
    scale = jnp.sqrt(trace) + ortho_eps
    gram[...] = gram[...] / (scale * scale)
    count = 2 * depth
    start = pl.multiple_of(chip * count, count)
    for factor in factors:
        gram_b = gram[...].astype(jnp.bfloat16)
        square = dot(gram_b, gram_b, ((1,), (0,)))
        factor[...] = (coef_second * gram[...] + coef_third * square).astype(jnp.bfloat16)
        moved = dot(factor[...], gram_b, ((1,), (0,)))
        twice = dot(factor[...], moved.astype(jnp.bfloat16), ((1,), (0,)))
        gram[...] = coef_first * coef_first * gram[...] + 2.0 * coef_first * moved + twice
    eye = lax.broadcasted_iota(jnp.int32, (count, width), 0) + start
    eye = (eye == lax.broadcasted_iota(jnp.int32, (count, width), 1)).astype(jnp.float32)
    rows = gram[pl.ds(start, count), :]
    square = dot(rows.astype(jnp.bfloat16), gram[...].astype(jnp.bfloat16), ((1,), (0,)))
    rows = coef_first * eye + (coef_second * rows + coef_third * square)
    for factor in factors[::-1]:
        rows = coef_first * rows + dot(rows.astype(jnp.bfloat16), factor[...], ((1,), (0,)))
    waits[0]()
    rows = (rows / scale).astype(jnp.bfloat16)

    @pl.when(even)
    def _():
        state = dot(rows, heard[...], ((1,), (0,))).astype(jnp.bfloat16)
        kept[:, :width] = state[:depth]
        sent[:, :width] = state[depth:]
        kept[:, width:] = jnp.zeros_like(kept[:, width:])
        sent[:, width:] = jnp.zeros_like(sent[:, width:])

    @pl.when(jnp.logical_not(even))
    def _():
        state = dot(rows, wide[...], ((1,), (0,))).astype(jnp.bfloat16)
        kept[...] = state[depth:]
        sent[...] = state[:depth]


def split_device(
    tokens, cotangent, doc_lengths, qkv_w, out_w, ffn_w, vecs, qkv_mom, out_mom, ffn_mom, vec_mom
):
    micro, rows, width = tokens.shape
    shards = lax.axis_size("shard")
    groups = lax.axis_size("dp")
    column = lax.axis_index("shard")
    row = lax.axis_index("dp")
    place = jnp.stack([column, row & 1, row >> 1]).astype(jnp.int32)
    slots = micro * shards
    own = qkv_w.shape[2]
    hidden = ffn_w.shape[2]
    bf16 = jnp.bfloat16

    packed = jnp.concatenate(
        [ffn_w[0], ffn_w[1], qkv_w[0], qkv_w[1], qkv_w[2], jnp.zeros((ffn_w.shape[1], PAD))], axis=1
    ).astype(bf16)
    weights = lax.all_gather(packed, "dp", axis=0, tiled=True)

    flat = tokens.reshape(micro * rows, width)
    vec_rows, vec_own = vecs.shape
    small = jnp.concatenate(
        [vecs.astype(bf16).reshape(-1), doc_lengths.astype(bf16).reshape(-1)]
    )
    small = jnp.pad(small, (0, 8 * width - small.shape[0])).reshape(8, width)
    out_flat = out_w.astype(bf16).reshape(-1, width)
    out_count = out_flat.shape[0]
    heard = gather_direct(jnp.concatenate([flat, out_flat, small], axis=0), "shard")
    tokens_b = heard[:, : micro * rows].reshape(slots * rows, width)
    out_part = heard[:, micro * rows : micro * rows + out_count].reshape(shards, -1, own)
    out_part = out_part.transpose(1, 0, 2).reshape(-1, width)
    small = heard[:, micro * rows + out_count :].reshape(shards, -1)
    lengths = small[:, vecs.size : vecs.size + doc_lengths.size].astype(jnp.int32).reshape(slots, -1)
    small = small[:, : vecs.size].reshape(shards, vec_rows, vec_own).transpose(1, 0, 2).reshape(vec_rows, -1)
    vec = gather_double(small, "dp").transpose(1, 0, 2).reshape(vec_rows, -1).astype(jnp.float32)
    out_b = lax.all_gather(out_part, "dp", axis=0, tiled=True)
    position = jnp.arange(rows, dtype=jnp.int32)[None]
    ends = jnp.cumsum(lengths, axis=1)
    segment = jnp.sum((position[:, :, None] >= ends[:, None, :]).astype(jnp.int32), axis=2)
    valid = position < ends[:, -1:]
    slot = jnp.arange(slots, dtype=jnp.int32)[:, None]
    marks = jnp.where(valid, segment + slot * ends.shape[1], -1 - position - slot * rows)
    id_column, id_row = marks.reshape(-1, 1), marks.reshape(1, -1)
    bias_q = lax.dynamic_slice_in_dim(vec[0], column * own, own, 0)
    bias_v = lax.dynamic_slice_in_dim(vec[1], column * own, own, 0)
    bias_proj = jnp.concatenate([bias_q, jnp.zeros_like(bias_q), bias_v])[None]
    bias_up = lax.dynamic_slice_in_dim(vec[8:].reshape(-1), column * hidden, hidden, 0)[None]

    proj_lanes = pl.ds(2 * hidden, weights.shape[1] - 2 * hidden)
    ffn_lanes = pl.ds(0, 2 * hidden)
    qkv, mixed_own = run_kernel(
        attention_forward,
        [
            jax.ShapeDtypeStruct((slots * rows, 3 * own), bf16),
            jax.ShapeDtypeStruct((BLOCK, slots * rows // BLOCK * own), bf16),
        ],
        scalars=1,
        ties=[vec, bias_up],
        far=(1, 2, 4),
        far_out=(0,),
        lanes={2: proj_lanes},
    )(place, tokens_b, weights, bias_proj, id_column, id_row)

    depth = width // groups
    count = micro * rows
    whole_b = jax.ShapeDtypeStruct((slots * rows, width), bf16)
    own_f = jax.ShapeDtypeStruct((count, width), jnp.float32)
    own_b = jax.ShapeDtypeStruct((count, width), bf16)
    part_kinds = [own_f] + [own_b] * (shards - 1)
    sums_kind = jax.ShapeDtypeStruct((8, width), jnp.float32)
    moving = pltpu.VMEM((slots * rows, width), jnp.float32)

    mixed_pieces = pieces_of(mixed_own, "shard")
    first_b, activ_b, slope, first_in, *parts = run_kernel(
        layer_middle,
        [whole_b, whole_b, jax.ShapeDtypeStruct((slots * rows, hidden), jnp.float32), own_f] + part_kinds,
        scalars=1,
        scratch=[moving],
        far=(5, 6, 8),
        late=(8,),
        lanes={8: ffn_lanes},
    )(place, *mixed_pieces, out_b, tokens_b, vec, weights, bias_up)
    layer_out, d_branch_own, d_second, sums_two = run_kernel(
        second_norm, [own_b, own_b, own_f, sums_kind], scalars=1, far=(7, 8), far_out=(0, 2, 3)
    )(place, *send_parts(parts, "shard"), first_in, vec, cotangent.reshape(count, width), id_column)
    layer_out = layer_out.reshape(tokens.shape)
    d_branch_b, d_inner_b, d_bias_up, *parts = run_kernel(
        inner_backward,
        [whole_b, whole_b, jax.ShapeDtypeStruct((1, hidden), jnp.float32)] + part_kinds,
        scalars=1,
        scratch=[moving],
        far=(6,),
        far_out=(2, 3, 4, 5, 6),
        lanes={6: ffn_lanes},
    )(place, *pieces_of(d_branch_own, "shard"), slope, weights)
    (grads,) = run_kernel(inner_gradients, [jax.ShapeDtypeStruct((2, width, hidden), bf16)], far_out=(0,))(
        first_b, activ_b, d_inner_b, d_branch_b
    )
    summed = lax.psum_scatter(grads, "dp", scatter_dimension=1, tiled=True)
    d_first_in, d_attended_own, sums_one = run_kernel(
        first_norm, [own_f, own_b, sums_kind], far=(0, 4, 5), far_out=(0, 1, 2)
    )(*send_parts(parts, "shard"), d_second, first_in, vec)
    d_attended_pieces = pieces_of(d_attended_own, "shard")
    moment_kind = jax.ShapeDtypeStruct(ffn_mom.shape, ffn_mom.dtype)
    wide_kind = jax.ShapeDtypeStruct((depth, hidden), bf16)
    grad_ffn, new_ffn_mom, mine, far_send = run_kernel(
        wide_momenta,
        [moment_kind, moment_kind, wide_kind, wide_kind],
        scalars=1,
        ties=d_attended_pieces[1:],
        far=(1, 2),
        far_out=(0, 1),
    )(place, summed, ffn_mom)
    far_rows = swap(far_send, "shard", shards // 2)

    packed_rows = depth + 16
    kept, sent, d_proj = run_kernel(
        attention_backward,
        [
            jax.ShapeDtypeStruct((groups // 2, packed_rows, width), jnp.float32),
            jax.ShapeDtypeStruct((groups // 2, packed_rows, width), bf16),
            jax.ShapeDtypeStruct((slots * rows, 3 * own), bf16),
        ],
        scalars=1,
        scratch=[pltpu.VMEM((slots * rows, width), bf16), pltpu.VMEM((16, width), jnp.float32)],
        far=(1, 2, 3, 4, 9, 10, 11, 5, 6, 7, 8, 13, 14, 15),
        far_out=(0, 2),
        late=(5, 6, 7, 8, 13, 14, 15),
        ties=[far_send],
    )(
        place, *d_attended_pieces, *mixed_pieces, out_b, qkv, id_column, id_row, tokens_b,
        sums_one, sums_two, d_bias_up,
    )
    (wide_rows,) = run_kernel(
        join_wide, [jax.ShapeDtypeStruct((depth, 2 * hidden), bf16)], ties=[kept], far_out=(0,)
    )(mine, far_rows)
    wide = lax.all_gather(wide_rows, "dp", axis=0, tiled=True)
    block_kind = jax.ShapeDtypeStruct((packed_rows, width), bf16)
    total, *blocks = run_kernel(
        pair_sum, [jax.ShapeDtypeStruct((packed_rows, width), jnp.float32)] + [block_kind] * 3, scalars=1, far=(1,)
    )(place, kept, swap(sent, "dp", 1))
    block_kind = jax.ShapeDtypeStruct((packed_rows, own), bf16)
    like = [jax.ShapeDtypeStruct(each.shape, each.dtype) for each in (qkv_mom, out_mom)]
    grad_qkv, grad_wout, new_qkv_mom, new_out_mom, *blocks = run_kernel(
        square_momenta,
        like + like + [block_kind] * shards,
        scalars=1,
        scratch=[pltpu.VMEM((shards, packed_rows, own), jnp.float32)],
        far=(5, 6),
        far_out=(0, 1, 2, 3),
    )(place, total, *[swap(block, "dp", 2 * at + 2) for at, block in enumerate(blocks)], qkv_mom, out_mom)
    square_pieces = send_parts(blocks, "shard")
    (gram_rows,) = run_kernel(wide_gram, [jax.ShapeDtypeStruct((depth, width), bf16)], ties=square_pieces[1:], far=(0, 1))(
        wide_rows, wide
    )
    row_kind = jax.ShapeDtypeStruct((depth, width), bf16)
    mine, other, grad_vec = run_kernel(
        join_squares,
        [row_kind, row_kind, jax.ShapeDtypeStruct((packed_rows - depth, own), jnp.float32)],
        scalars=1,
        scratch=[pltpu.VMEM((depth, width), bf16)],
    )(place, *square_pieces, gram_rows, swap(gram_rows, "shard", 1))
    grad_vec = grad_vec[:vec_rows, :vec_own]
    (pair_rows,) = run_kernel(
        join_pair, [jax.ShapeDtypeStruct((2 * depth, width), bf16)], scalars=1
    )(place, mine, swap(other, "dp", 1))
    pair_pieces = [pair_rows] + [swap(pair_rows, "dp", bit) for bit in (2, 4, 6)]
    (part,) = run_kernel(
        token_part, [whole_b], ties=[pair_rows], far=(0, 1), far_out=(0,), lanes={1: proj_lanes}
    )(d_proj, weights)
    d_tokens = lax.psum_scatter(part, "shard", scatter_dimension=0, tiled=True)
    state_kind = jax.ShapeDtypeStruct((depth, 2 * hidden), bf16)
    kept, sent = run_kernel(
        newton_schulz,
        [state_kind, state_kind],
        scalars=1,
        scratch=[pltpu.VMEM((width, width), bf16), pltpu.VMEM((width, width), jnp.float32)]
        + [pltpu.VMEM((width, width), bf16)] * (NS_STEPS - 1),
        far=(5,),
        late=(5,),
    )(place, *pair_pieces, wide)
    block_kind = jax.ShapeDtypeStruct((depth, own), bf16)
    wide_kind = jax.ShapeDtypeStruct((depth, hidden), bf16)
    kinds = [block_kind] * shards + [wide_kind]
    kinds[shards // 2] = jax.ShapeDtypeStruct((depth, hidden + own), bf16)
    *blocks, mine = run_kernel(
        split_state, kinds, scalars=1
    )(place, kept, swap(sent, "dp", 1))
    state_pieces = send_parts(blocks, "shard")
    (d_tokens,) = run_kernel(add_rows, [own_f], ties=[state_pieces[1]], far=(0, 1), far_out=(0,))(
        d_first_in, d_tokens
    )
    qkv_new, out_new, ffn_new = run_kernel(
        new_weights,
        [jax.ShapeDtypeStruct(each.shape, each.dtype) for each in (qkv_w, out_w, ffn_w)],
        scalars=1,
        scratch=[pltpu.VMEM((shards, depth, own), jnp.float32)],
        ties=[d_tokens],
        far=(6, 7, 8),
        far_out=(0, 1, 2),
    )(
        place, *state_pieces, mine, qkv_w, out_w, ffn_w
    )

    d_tokens = d_tokens.reshape(tokens.shape)
    token_count = micro * rows * groups * shards
    new_vec_mom = momentum_decay * vec_mom + grad_vec
    vec_new = vecs - vec_rate * token_count ** (-0.5) * new_vec_mom
    return (
        layer_out,
        d_tokens,
        grad_qkv,
        grad_wout,
        grad_ffn,
        grad_vec,
        new_qkv_mom,
        new_out_mom,
        new_ffn_mom,
        new_vec_mom,
        qkv_new,
        out_new,
        ffn_new,
        vec_new,
    )


def solution(mesh):
    fits = (mesh.shape["dp"], mesh.shape["shard"]) == (8, 4)
    in_specs = (
        P(("dp", "shard"), None, None),
        P(("dp", "shard"), None, None),
        P(("dp", "shard"), None),
        P(None, "dp", "shard"),
        P("dp", "shard"),
        P(None, "dp", "shard"),
        P(None, ("dp", "shard")),
        P(None, "dp", "shard"),
        P("dp", "shard"),
        P(None, "dp", "shard"),
        P(None, ("dp", "shard")),
    )
    out_specs = (
        P(("dp", "shard"), None, None),
        P(("dp", "shard"), None, None),
        P(None, "dp", "shard"),
        P("dp", "shard"),
        P(None, "dp", "shard"),
        P(None, ("dp", "shard")),
        P(None, "dp", "shard"),
        P("dp", "shard"),
        P(None, "dp", "shard"),
        P(None, ("dp", "shard")),
        P(None, "dp", "shard"),
        P("dp", "shard"),
        P(None, "dp", "shard"),
        P(None, ("dp", "shard")),
    )
    return jax.shard_map(
        split_device if fits else per_device, mesh=mesh, in_specs=in_specs, out_specs=out_specs, check_vma=False
    )
```

```python
import math
import jax
import jax.numpy as jnp
from jax import lax
from jax.experimental import pallas as pl
from jax.experimental.pallas import tpu as pltpu
from jax.sharding import PartitionSpec as P

D = 768
HEADS = 12
HEAD = 64
FF = 3072
NS_STEPS = 3


masked_score = -1e30
norm_eps = 1e-12
momentum_decay = 0.9
muon_rate = 0.8
vec_rate = 0.5
coef_first = 3.4445
coef_second = -4.775
coef_third = 2.0315
ortho_eps = 1e-07


def spread_2(block, axis, owner):
    block = jnp.where(lax.axis_index(axis) == owner, block, jnp.zeros_like(block))
    return lax.psum(block, axis)


def segments(lengths, rows):
    position = jnp.arange(rows, dtype=jnp.int32)
    ends = jnp.cumsum(lengths)
    segment = jnp.sum((position[:, None] >= ends[None, :]).astype(jnp.int32), axis=1)
    valid = position < ends[-1]
    same = segment[:, None] == segment[None, :]
    allowed = same & valid[:, None] | (position[:, None] == position[None, :])
    return (valid, allowed)


def layer_norm(inputs, gain, bias):
    center = inputs - jnp.mean(inputs, axis=-1, keepdims=True)
    spread = jnp.mean(center * center, axis=-1, keepdims=True)
    return center * lax.rsqrt(spread + norm_eps) * gain + bias


def gelu_exact(inputs):
    return jax.nn.gelu(inputs, approximate=False)


def split_heads(matrix):
    return matrix.reshape(matrix.shape[0], HEADS, HEAD)


def gather_weights(qkv_w, out_w, ffn_w, vecs):
    pieces = (
        qkv_w.astype(jnp.bfloat16),
        out_w.astype(jnp.bfloat16),
        ffn_w.astype(jnp.bfloat16),
        vecs.astype(jnp.bfloat16),
    )
    across = (
        lax.all_gather(pieces[0], "shard", axis=2, tiled=True),
        lax.all_gather(pieces[1], "shard", axis=1, tiled=True),
        lax.all_gather(pieces[2], "shard", axis=2, tiled=True),
        lax.all_gather(pieces[3], "shard", axis=1, tiled=True),
    )
    return (
        lax.all_gather(across[0], "dp", axis=1, tiled=True),
        lax.all_gather(across[1], "dp", axis=0, tiled=True),
        lax.all_gather(across[2], "dp", axis=1, tiled=True),
        lax.all_gather(across[3], "dp", axis=1, tiled=True),
    )


def attention_scores(queries_b, keys_b, allowed):
    scores = jnp.einsum(
        "qhd,khd->hqk",
        split_heads(queries_b),
        split_heads(keys_b),
        preferred_element_type=jnp.float32,
    )
    return jnp.where(allowed[None], scores * HEAD ** (-0.5), masked_score)


def forward_pass(tokens_b, lengths, weights):
    qkv_b, out_b, ffn_b, vec_b = weights
    vec = vec_b.astype(jnp.float32)
    rows = tokens_b.shape[0]
    valid, allowed = segments(lengths, rows)
    projected = jnp.einsum("rd,kde->kre", tokens_b, qkv_b, preferred_element_type=jnp.float32)
    queries_b = (projected[0] + vec[0]).astype(jnp.bfloat16)
    keys_b = projected[1].astype(jnp.bfloat16)
    values_b = (projected[2] + vec[1]).astype(jnp.bfloat16)
    scores = attention_scores(queries_b, keys_b, allowed)
    largest = jnp.max(scores, axis=-1, keepdims=True)
    exponent = jnp.exp(scores - largest)
    totals = jnp.sum(exponent, axis=-1, keepdims=True)
    logsum = largest + jnp.log(totals)
    probs_b = (exponent / totals).astype(jnp.bfloat16)
    mixed = jnp.einsum(
        "hqk,khd->qhd", probs_b, split_heads(values_b), preferred_element_type=jnp.float32
    )
    mixed_b = mixed.reshape(rows, -1).astype(jnp.bfloat16)
    attended = jnp.dot(mixed_b, out_b, preferred_element_type=jnp.float32) + vec[2]
    first_in = tokens_b.astype(jnp.float32) + attended
    first = layer_norm(first_in, vec[3], vec[4])
    first_b = first.astype(jnp.bfloat16)
    inner = jnp.dot(first_b, ffn_b[0], preferred_element_type=jnp.float32) + vec[8:].reshape(-1)
    activ_b = gelu_exact(inner).astype(jnp.bfloat16)
    branch = jnp.einsum("rf,df->rd", activ_b, ffn_b[1], preferred_element_type=jnp.float32) + vec[5]
    second_in = first + branch
    result = layer_norm(second_in, vec[6], vec[7]) * valid[:, None].astype(jnp.float32)
    kept = (
        queries_b,
        keys_b,
        values_b,
        logsum,
        mixed_b,
        first_in,
        first_b,
        inner,
        activ_b,
        second_in,
    )
    return (result.astype(jnp.bfloat16), kept)


def backward_pass(cot_b, tokens_b, lengths, weights, kept):
    qkv_b, out_b, ffn_b, vec_b = weights
    vec = vec_b.astype(jnp.float32)
    queries_b, keys_b, values_b, logsum, mixed_b, first_in, first_b, inner, activ_b, second_in = (
        kept
    )
    rows = tokens_b.shape[0]
    valid, allowed = segments(lengths, rows)
    grad_out = cot_b.astype(jnp.float32) * valid[:, None].astype(jnp.float32)
    unused, pull_two = jax.vjp(layer_norm, second_in, vec[6], vec[7])
    d_second, d_gain_two, d_shift_two = pull_two(grad_out)
    d_branch_b = d_second.astype(jnp.bfloat16)
    d_bias_down = jnp.sum(d_branch_b.astype(jnp.float32), axis=0)
    d_activ = jnp.dot(d_branch_b, ffn_b[1], preferred_element_type=jnp.float32)
    unused, pull_gelu = jax.vjp(gelu_exact, inner)
    (d_inner,) = pull_gelu(d_activ)
    d_inner_b = d_inner.astype(jnp.bfloat16)
    d_bias_up = jnp.sum(d_inner_b.astype(jnp.float32), axis=0)
    d_first = d_second + jnp.einsum(
        "rf,df->rd", d_inner_b, ffn_b[0], preferred_element_type=jnp.float32
    )
    unused, pull_one = jax.vjp(layer_norm, first_in, vec[3], vec[4])
    d_first_in, d_gain_one, d_shift_one = pull_one(d_first)
    d_attended_b = d_first_in.astype(jnp.bfloat16)
    d_bias_out = jnp.sum(d_attended_b.astype(jnp.float32), axis=0)
    d_mixed_b = jnp.einsum(
        "re,de->rd", d_attended_b, out_b, preferred_element_type=jnp.float32
    ).astype(jnp.bfloat16)
    scores = attention_scores(queries_b, keys_b, allowed)
    probs = jnp.exp(scores - logsum)
    mixed_heads = split_heads(d_mixed_b)
    d_probs = jnp.einsum(
        "qhd,khd->hqk", mixed_heads, split_heads(values_b), preferred_element_type=jnp.float32
    )
    d_values = jnp.einsum(
        "hqk,qhd->khd", probs.astype(jnp.bfloat16), mixed_heads, preferred_element_type=jnp.float32
    )
    d_scores_b = (probs * (d_probs - jnp.sum(probs * d_probs, axis=-1, keepdims=True))).astype(
        jnp.bfloat16
    )
    d_queries = jnp.einsum(
        "hqk,khd->qhd", d_scores_b, split_heads(keys_b), preferred_element_type=jnp.float32
    ) * HEAD ** (-0.5)
    d_keys = jnp.einsum(
        "hqk,qhd->khd", d_scores_b, split_heads(queries_b), preferred_element_type=jnp.float32
    ) * HEAD ** (-0.5)
    d_proj_b = jnp.stack([d_queries, d_keys, d_values]).reshape(3, rows, -1).astype(jnp.bfloat16)
    d_tokens = d_first_in + jnp.einsum(
        "kre,kde->rd", d_proj_b, qkv_b, preferred_element_type=jnp.float32
    )
    proj_sums = jnp.sum(d_proj_b.astype(jnp.float32), axis=1)
    grad_vec = jnp.concatenate(
        [
            jnp.stack(
                [
                    proj_sums[0],
                    proj_sums[2],
                    d_bias_out,
                    d_gain_one,
                    d_shift_one,
                    d_bias_down,
                    d_gain_two,
                    d_shift_two,
                ]
            ),
            d_bias_up.reshape(-1, vec.shape[1]),
        ],
        axis=0,
    )
    factors = (d_branch_b, activ_b, first_b, d_inner_b, mixed_b, d_attended_b, d_proj_b)
    return (d_tokens, factors, grad_vec)


def orthogonalize_pair(square, wide):
    matrices = (square, wide)
    present = tuple((matrix.astype(jnp.bfloat16) for matrix in matrices))
    states = matrices
    for step in range(NS_STEPS):
        partial_value = tuple(
            (
                jnp.einsum("iw,jw->ij", block, block, preferred_element_type=jnp.float32)
                for block in present
            )
        )
        gram_part = (
            lax.psum_scatter(
                partial_value[0].astype(jnp.bfloat16), "shard", scatter_dimension=0, tiled=True
            ).astype(jnp.float32),
            lax.psum_scatter(
                partial_value[1].astype(jnp.bfloat16), "shard", scatter_dimension=0, tiled=True
            ).astype(jnp.float32),
        )
        grams = (
            lax.all_gather(gram_part[0].astype(jnp.bfloat16), "shard", axis=0, tiled=True).astype(
                jnp.float32
            ),
            lax.all_gather(gram_part[1].astype(jnp.bfloat16), "shard", axis=0, tiled=True).astype(
                jnp.float32
            ),
        )
        if step == 0:
            scales = tuple((jnp.sqrt(jnp.trace(gram)) + ortho_eps for gram in grams))
            grams = tuple((gram / (scale * scale) for gram, scale in zip(grams, scales)))
            present = tuple(
                ((matrix / scale).astype(jnp.bfloat16) for matrix, scale in zip(matrices, scales))
            )
        renewed = []
        for gram, current in zip(grams, present):
            gram_b = gram.astype(jnp.bfloat16)
            once = jnp.dot(gram_b, current, preferred_element_type=jnp.float32)
            twice = jnp.dot(gram_b, once.astype(jnp.bfloat16), preferred_element_type=jnp.float32)
            renewed.append(
                coef_first * current.astype(jnp.float32) + coef_second * once + coef_third * twice
            )
        states = tuple(renewed)
        present = tuple((state.astype(jnp.bfloat16) for state in states))
    return states


def per_device(
    tokens, cotangent, doc_lengths, qkv_w, out_w, ffn_w, vecs, qkv_mom, out_mom, ffn_mom, vec_mom
):
    micro = tokens.shape[0]
    shared = gather_weights(qkv_w, out_w, ffn_w, vecs)
    outputs = []
    stored = []
    for index in range(micro):
        weights = shared
        result_b, kept = forward_pass(tokens[index], doc_lengths[index], weights)
        outputs.append(result_b)
        stored.append(kept)
    grad_rows = [None] * micro
    factor_list = [None] * micro
    vec_total = None
    for index in reversed(range(micro)):
        weights = shared
        d_tokens, factors, vec_part = backward_pass(
            cotangent[index], tokens[index], doc_lengths[index], weights, stored[index]
        )
        grad_rows[index] = d_tokens
        factor_list[index] = factors
        vec_total = vec_part if vec_total is None else vec_total + vec_part
    (
        branch_gradient_rows,
        activation_rows,
        first_norm_rows,
        inner_gradient_rows,
        mixed_all,
        d_attended_all,
        d_proj_all,
    ) = [jnp.stack([factors[place] for factors in factor_list]) for place in range(7)]
    grad_down = jnp.einsum(
        "hzo,hzx->ox", branch_gradient_rows, activation_rows, preferred_element_type=jnp.float32
    )
    up_weight_gradient = jnp.einsum(
        "hzo,hzx->ox", first_norm_rows, inner_gradient_rows, preferred_element_type=jnp.float32
    )
    grad_wout_sum = jnp.einsum(
        "mrd,mre->de", mixed_all, d_attended_all, preferred_element_type=jnp.float32
    )
    grad_qkv_sum = jnp.einsum(
        "mrd,mkre->kde", tokens, d_proj_all, preferred_element_type=jnp.float32
    )
    summed = (grad_qkv_sum, grad_wout_sum, jnp.stack([up_weight_gradient, grad_down]), vec_total)
    reduced = (
        lax.psum_scatter(
            summed[0].astype(jnp.bfloat16), "dp", scatter_dimension=1, tiled=True
        ).astype(jnp.float32),
        lax.psum_scatter(
            summed[1].astype(jnp.bfloat16), "dp", scatter_dimension=0, tiled=True
        ).astype(jnp.float32),
        lax.psum_scatter(
            summed[2].astype(jnp.bfloat16), "dp", scatter_dimension=1, tiled=True
        ).astype(jnp.float32),
        lax.psum_scatter(
            summed[3].astype(jnp.bfloat16), "dp", scatter_dimension=1, tiled=True
        ).astype(jnp.float32),
    )
    grad_qkv, grad_wout, grad_ffn, grad_vec = (
        lax.psum_scatter(
            reduced[0].astype(jnp.bfloat16), "shard", scatter_dimension=2, tiled=True
        ).astype(jnp.float32),
        lax.psum_scatter(
            reduced[1].astype(jnp.bfloat16), "shard", scatter_dimension=1, tiled=True
        ).astype(jnp.float32),
        lax.psum_scatter(
            reduced[2].astype(jnp.bfloat16), "shard", scatter_dimension=2, tiled=True
        ).astype(jnp.float32),
        lax.psum_scatter(
            reduced[3].astype(jnp.bfloat16), "shard", scatter_dimension=1, tiled=True
        ).astype(jnp.float32),
    )
    new_qkv_mom = momentum_decay * qkv_mom + grad_qkv
    new_out_mom = momentum_decay * out_mom + grad_wout
    new_ffn_mom = momentum_decay * ffn_mom + grad_ffn
    square_local = jnp.concatenate([new_qkv_mom, new_out_mom[None]], axis=0)
    square_cols, wide_cols = (
        lax.all_gather(square_local.astype(jnp.bfloat16), "dp", axis=1, tiled=True).astype(
            square_local.dtype
        ),
        lax.all_gather(new_ffn_mom.astype(jnp.bfloat16), "dp", axis=1, tiled=True).astype(
            new_ffn_mom.dtype
        ),
    )
    row = lax.axis_index("dp")
    rows_count = lax.axis_size("dp")
    owners = [place * rows_count // 6 for place in range(6)]
    square_pick = sum(((row == owners[place]).astype(jnp.int32) * place for place in range(4)))
    wide_pick = (row == owners[5]).astype(jnp.int32)
    square_state, wide_state = orthogonalize_pair(
        lax.dynamic_index_in_dim(square_cols, square_pick, 0, keepdims=False),
        lax.dynamic_index_in_dim(wide_cols, wide_pick, 0, keepdims=False),
    )
    depth = qkv_w.shape[1]
    square_rows = []
    for place in range(4):
        whole = spread_2(square_state.astype(jnp.bfloat16), "dp", owners[place]).astype(
            square_state.dtype
        )
        square_rows.append(lax.dynamic_slice_in_dim(whole, row * depth, depth, 0))
    wide_rows = []
    for place in range(4, 6):
        whole = spread_2(wide_state.astype(jnp.bfloat16), "dp", owners[place]).astype(
            wide_state.dtype
        )
        wide_rows.append(lax.dynamic_slice_in_dim(whole, row * depth, depth, 0))
    qkv_new = qkv_w - muon_rate * jnp.stack(square_rows[:3])
    out_new = out_w - muon_rate * square_rows[3]
    ffn_new = ffn_w - muon_rate * (FF / D) ** 0.5 * jnp.stack(wide_rows)
    token_count = tokens.shape[0] * tokens.shape[1] * lax.axis_size("dp") * lax.axis_size("shard")
    new_vec_mom = momentum_decay * vec_mom + grad_vec
    vec_new = vecs - vec_rate * token_count ** (-0.5) * new_vec_mom
    return (
        jnp.stack(outputs),
        jnp.stack(grad_rows),
        grad_qkv,
        grad_wout,
        grad_ffn,
        grad_vec,
        new_qkv_mom,
        new_out_mom,
        new_ffn_mom,
        new_vec_mom,
        qkv_new,
        out_new,
        ffn_new,
        vec_new,
    )


def gather_direct(block, axis):
    count = lax.axis_size(axis)
    me = lax.axis_index(axis)
    whole = jnp.zeros((count,) + block.shape, block.dtype)
    whole = lax.dynamic_update_index_in_dim(whole, block, me, 0)
    for step in range(1, count):
        got = lax.ppermute(block, axis, [(i, (i + step) % count) for i in range(count)])
        whole = lax.dynamic_update_index_in_dim(whole, got, lax.rem(me - step + count, count), 0)
    return whole


def pieces_of(block, axis):
    count = lax.axis_size(axis)
    return [block] + [
        lax.ppermute(block, axis, [(i, (i + step) % count) for i in range(count)])
        for step in range(1, count)
    ]


def send_parts(parts, axis):
    count = lax.axis_size(axis)
    return [parts[0]] + [
        lax.ppermute(parts[step], axis, [(i, (i + step) % count) for i in range(count)])
        for step in range(1, count)
    ]


def swap(block, axis, bit):
    return lax.ppermute(block, axis, [(i, i ^ bit) for i in range(lax.axis_size(axis))])


def gather_double(block, axis):
    me = lax.axis_index(axis)
    bit = 1
    whole = block[None]
    while bit < lax.axis_size(axis):
        other = swap(whole, axis, bit)
        high = (me & bit) != 0
        whole = jnp.concatenate(
            [jnp.where(high, other, whole), jnp.where(high, whole, other)], axis=0
        )
        bit *= 2
    return whole


def dot(left, right, dims):
    return lax.dot_general(left, right, (dims, ((), ())), preferred_element_type=jnp.float32)


def norm_parts(inputs):
    center = inputs - jnp.mean(inputs, axis=-1, keepdims=True)
    spread = jnp.mean(center * center, axis=-1, keepdims=True)
    scale = lax.rsqrt(spread + norm_eps)
    return center * scale, scale


def norm_back(grad, unit, scale, gain):
    scaled = grad * gain
    mean_grad = jnp.mean(scaled, axis=-1, keepdims=True)
    mean_unit = jnp.mean(scaled * unit, axis=-1, keepdims=True)
    return scale * (scaled - mean_grad - unit * mean_unit)


BLOCK = 256
PAD = 64
SPLIT = 4


def source_of(column, step):
    return lax.rem(column - step + SPLIT, SPLIT)


def put_pieces(pieces, column, whole):
    count = pieces[0].shape[0]
    for step, piece in enumerate(pieces):
        at = pl.multiple_of(source_of(column, step) * count, count)
        whole[pl.ds(at, count), :] = piece[...]


def take_parts(whole, column, parts):
    count = parts[0].shape[0]
    for step, part in enumerate(parts):
        at = pl.multiple_of(lax.rem(column + step, SPLIT) * count, count)
        part[...] = whole[pl.ds(at, count), :].astype(part.dtype)


def sum_pieces(pieces):
    total = pieces[0][...]
    for piece in pieces[1:]:
        total = total + piece[...].astype(jnp.float32)
    return total


def row_sums(values):
    return jnp.sum(values, axis=0, keepdims=True)


def unpack_rows(piece, rows):
    count = rows // piece.shape[0]
    own = piece.shape[1] // count
    return jnp.concatenate([piece[:, at * own : (at + 1) * own] for at in range(count)], axis=0)


def layer_middle(waits, place, *refs):
    pieces, refs = refs[:SPLIT], refs[SPLIT:]
    out_weight, tokens, vec, weights, bias_up, first_b, activ_b, slope, first_in, *refs = refs
    parts, (moving,) = refs[:SPLIT], refs[SPLIT:]
    column = place[0]
    attended = vec[2:3, :] + tokens[...].astype(jnp.float32)
    for step, piece in enumerate(pieces):
        rows = unpack_rows(piece, tokens.shape[0])
        own = rows.shape[1]
        at = pl.multiple_of(source_of(column, step) * own, own)
        attended = attended + dot(rows, out_weight[pl.ds(at, own), :], ((1,), (0,)))
    moving[...] = attended
    take_parts(moving, column, [first_in])
    unit, scale = norm_parts(attended)
    first_b[...] = (unit * vec[3:4, :] + vec[4:5, :]).astype(jnp.bfloat16)
    hidden = slope.shape[1]
    waits[0]()
    inner = dot(first_b[...], weights[:, :hidden], ((1,), (0,))) + bias_up[...]
    cdf = 0.5 * (1.0 + lax.erf(inner * 2.0 ** (-0.5)))
    activ_b[...] = (inner * cdf).astype(jnp.bfloat16)
    slope[...] = cdf + inner * jnp.exp(-0.5 * inner * inner) * (2.0 * math.pi) ** (-0.5)
    moving[...] = dot(activ_b[...], weights[:, hidden : 2 * hidden], ((1,), (1,)))
    take_parts(moving, column, parts)


def second_norm(place, *refs):
    pieces, refs = refs[:SPLIT], refs[SPLIT:]
    first_in, vec, cotangent, ids, layer_out, d_branch, d_second, sums = refs
    count = first_in.shape[0]
    at = pl.multiple_of(place[0] * count, count)
    valid = (ids[pl.ds(at, count), :] >= 0).astype(jnp.float32)
    unit, scale = norm_parts(first_in[...])
    first = unit * vec[3:4, :] + vec[4:5, :]
    unit, scale = norm_parts(first + (sum_pieces(pieces) + vec[5:6, :]))
    layer_out[...] = ((unit * vec[6:7, :] + vec[7:8, :]) * valid).astype(jnp.bfloat16)
    grad = cotangent[...].astype(jnp.float32) * valid
    d_rows = norm_back(grad, unit, scale, vec[6:7, :])
    d_second[...] = d_rows
    d_branch[...] = d_rows.astype(jnp.bfloat16)
    sums[0:1, :] = row_sums(d_branch[...].astype(jnp.float32))
    sums[1:2, :] = row_sums(grad * unit)
    sums[2:3, :] = row_sums(grad)


def inner_backward(place, *refs):
    pieces, refs = refs[:SPLIT], refs[SPLIT:]
    slope, weights, d_branch, d_inner, sums, *refs = refs
    parts, (moving,) = refs[:SPLIT], refs[SPLIT:]
    column = place[0]
    put_pieces(pieces, column, d_branch)
    hidden = slope.shape[1]
    d_activ = dot(d_branch[...], weights[:, hidden : 2 * hidden], ((1,), (0,)))
    d_inner[...] = (d_activ * slope[...]).astype(jnp.bfloat16)
    sums[...] = row_sums(d_inner[...].astype(jnp.float32))
    moving[...] = dot(d_inner[...], weights[:, :hidden], ((1,), (1,)))
    take_parts(moving, column, parts)


def inner_gradients(first_b, activ_b, d_inner, d_branch, grads):
    grads[0] = dot(first_b[...], d_inner[...], ((0,), (0,))).astype(jnp.bfloat16)
    grads[1] = dot(d_branch[...], activ_b[...], ((0,), (0,))).astype(jnp.bfloat16)


def wide_momenta(place, summed, moments, grads, moments_new, mine, far):
    low = place[0] < SPLIT // 2
    for part in range(2):
        grads[part] = summed[part].astype(jnp.float32)
        moments_new[part] = momentum_decay * moments[part] + grads[part]
    first, second = moments_new[0].astype(jnp.bfloat16), moments_new[1].astype(jnp.bfloat16)
    mine[...] = jnp.where(low, first, second)
    far[...] = jnp.where(low, second, first)


def join_wide(mine, far, rows):
    hidden = mine.shape[1]
    rows[:, :hidden] = mine[...]
    rows[:, hidden:] = far[...]


def wide_gram(rows, wide, gram):
    gram[...] = dot(rows[...], wide[...], ((1,), (1,))).astype(jnp.bfloat16)


def first_norm(*refs):
    pieces, refs = refs[:SPLIT], refs[SPLIT:]
    d_second, first_in, vec, d_first_in, d_attended, sums = refs
    unit, scale = norm_parts(first_in[...])
    grad = sum_pieces(pieces) + d_second[...]
    d_rows = norm_back(grad, unit, scale, vec[3:4, :])
    d_first_in[...] = d_rows
    d_attended[...] = d_rows.astype(jnp.bfloat16)
    sums[0:1, :] = row_sums(d_attended[...].astype(jnp.float32))
    sums[1:2, :] = row_sums(grad * unit)
    sums[2:3, :] = row_sums(grad)


def split_state(place, kept, other, *refs):
    blocks, (mine,) = refs[:SPLIT], refs[SPLIT:]
    column, even = place[0], place[1] == 0
    own, hidden = blocks[0].shape[1], mine.shape[1]
    far = blocks[SPLIT // 2]
    for step, block in enumerate(blocks):
        there = lax.rem(column + step, SPLIT)
        for at in range(SPLIT):
            lanes = slice(at * own, (at + 1) * own)

            @pl.when(there == at)
            def _():
                block[:, block.shape[1] - own :] = jnp.where(even, kept[:, lanes], other[:, lanes])

    mine[...] = jnp.where(even, other[:, :hidden], kept[:, :hidden])
    far[:, :hidden] = jnp.where(even, other[:, hidden:], kept[:, hidden:])


def new_weights(place, *refs):
    pieces, refs = refs[:SPLIT], refs[SPLIT:]
    mine, qkv_w, out_w, ffn_w, qkv_new, out_new, ffn_new, state = refs
    low = place[0] < SPLIT // 2
    own, hidden = out_w.shape[1], mine.shape[1]
    far = pieces[SPLIT // 2][:, :hidden]
    for step, piece in enumerate(pieces):
        state[source_of(place[0], step)] = piece[:, piece.shape[1] - own :].astype(jnp.float32)
    for at in range(SPLIT - 1):
        qkv_new[at] = qkv_w[at] - muon_rate * state[at]
    out_new[...] = out_w[...] - muon_rate * state[SPLIT - 1]
    rate = muon_rate * (FF / D) ** 0.5
    ffn_new[0] = ffn_w[0] - rate * jnp.where(low, mine[...], far).astype(jnp.float32)
    ffn_new[1] = ffn_w[1] - rate * jnp.where(low, far, mine[...]).astype(jnp.float32)


def probabilities(qkv, rows_at, head, own, id_column, id_row):
    queries = qkv[rows_at, head * HEAD : (head + 1) * HEAD]
    keys = qkv[rows_at, own + head * HEAD : own + (head + 1) * HEAD]
    values = qkv[rows_at, 2 * own + head * HEAD : 2 * own + (head + 1) * HEAD]
    scores = dot(queries, keys, ((1,), (1,))) * HEAD ** (-0.5)
    scores = jnp.where(id_column[rows_at, :] == id_row[:, rows_at], scores, masked_score)
    exponent = jnp.exp(scores - jnp.max(scores, axis=-1, keepdims=True))
    probs = exponent / jnp.sum(exponent, axis=-1, keepdims=True)
    return queries, keys, values, probs


def attention_forward(place, tokens, weight, bias, id_column, id_row, qkv, mixed):
    own = qkv.shape[1] // 3
    proj = weight[:, : 3 * own]
    qkv[...] = (dot(tokens[...], proj, ((1,), (0,))) + bias[...]).astype(jnp.bfloat16)
    for start in range(0, tokens.shape[0], BLOCK):
        rows_at = slice(start, start + BLOCK)
        for head in range(own // HEAD):
            queries, keys, values, probs = probabilities(qkv, rows_at, head, own, id_column, id_row)
            part = dot(probs.astype(jnp.bfloat16), values, ((1,), (0,)))
            at = start // BLOCK * own + head * HEAD
            mixed[:, at : at + HEAD] = part.astype(jnp.bfloat16)


def attention_backward(waits, place, *refs):
    pieces, mixed, refs = refs[:SPLIT], refs[SPLIT : 2 * SPLIT], refs[2 * SPLIT :]
    out_weight, qkv, id_column, id_row, tokens, sums_one, sums_two, sums_up, *refs = refs
    kept, sent, d_proj, d_attended, sums = refs
    rows, width = tokens.shape
    own = qkv.shape[1] // 3
    column, core = place[0], place[1]
    put_pieces(pieces, column, d_attended)
    out_rows = out_weight[pl.ds(pl.multiple_of(column * own, own), own), :]
    d_mixed = dot(d_attended[...], out_rows, ((1,), (1,))).astype(jnp.bfloat16)
    for start in range(0, rows, BLOCK):
        rows_at = slice(start, start + BLOCK)
        for head in range(own // HEAD):
            queries, keys, values, probs = probabilities(qkv, rows_at, head, own, id_column, id_row)
            d_out = d_mixed[rows_at, head * HEAD : (head + 1) * HEAD]
            d_probs = dot(d_out, values, ((1,), (1,)))
            d_scores = probs * (d_probs - jnp.sum(probs * d_probs, axis=-1, keepdims=True))
            d_scores = d_scores.astype(jnp.bfloat16)
            d_values = dot(probs.astype(jnp.bfloat16), d_out, ((0,), (0,)))
            d_queries = dot(d_scores, keys, ((1,), (0,))) * HEAD ** (-0.5)
            d_keys = dot(d_scores, queries, ((0,), (0,))) * HEAD ** (-0.5)
            for part, value in enumerate((d_queries, d_keys, d_values)):
                at = part * own + head * HEAD
                d_proj[rows_at, at : at + HEAD] = value.astype(jnp.bfloat16)
    d_proj_all = d_proj[...]
    d_columns = d_attended[:, :own]
    for place_at in range(1, width // own):
        other = d_attended[:, place_at * own : (place_at + 1) * own]
        d_columns = jnp.where(column == place_at, other, d_columns)
    for wait in waits:
        wait()
    grad_proj = dot(tokens[...], d_proj_all, ((0,), (0,)))
    proj_sums = row_sums(d_proj_all.astype(jnp.float32))
    sums[...] = jnp.zeros_like(sums)
    for at in range(SPLIT):
        lanes = slice(at * own, (at + 1) * own)
        mine = (column == at).astype(jnp.float32)
        sums[0:1, lanes] = proj_sums[:, :own] * mine
        sums[1:2, lanes] = proj_sums[:, 2 * own :] * mine
        sums[8 + at : 9 + at, :] = sums_up[...] * mine
    sums[2:5, :] = sums_one[0:3, :]
    sums[5:8, :] = sums_two[0:3, :]
    depth = kept.shape[1] - sums.shape[0]
    for group in range(width // depth):
        at = slice(group * depth, (group + 1) * depth)

        def put(target, kind):
            target[group // 2, :depth, : 3 * own] = grad_proj[at].astype(kind)
            target[group // 2, depth:, :] = jnp.zeros((sums.shape[0], width), kind)
            target[group // 2, depth:, :depth] = sums[:, at].astype(kind)

        pl.when(core == group % 2)(lambda: put(kept, jnp.float32))
        pl.when(core != group % 2)(lambda: put(sent, jnp.bfloat16))
    for step, piece in enumerate(mixed):
        grad_out = dot(unpack_rows(piece, rows), d_columns, ((0,), (0,)))
        source = source_of(column, step)
        for half in range(2):
            block = grad_out[half * depth : (half + 1) * depth]

            def put_out(target, kind):
                target[source, :depth, 3 * own :] = block.astype(kind)

            pl.when(core == half)(lambda: put_out(kept, jnp.float32))
            pl.when(core != half)(lambda: put_out(sent, jnp.bfloat16))


def token_part(d_proj, weight, part):
    proj = weight[:, : d_proj.shape[1]]
    part[...] = dot(d_proj[...], proj, ((1,), (1,))).astype(jnp.bfloat16)


def pack_weights(ffn, qkv, packed):
    hidden, own = ffn.shape[2], qkv.shape[2]
    packed[:, 2 * hidden :] = jnp.zeros_like(packed[:, 2 * hidden :])
    for part in range(2):
        packed[:, part * hidden : (part + 1) * hidden] = ffn[part].astype(jnp.bfloat16)
    for part in range(3):
        at = 2 * hidden + part * own
        packed[:, at : at + own] = qkv[part].astype(jnp.bfloat16)


def add_rows(left, right, total, flag):
    flag[...] = jnp.zeros_like(flag)
    total[...] = left[...] + right[...].astype(jnp.float32)


def pair_sum(place, kept, other, total, *blocks):
    chip = place[2]
    total[...] = kept[chip] + other[chip].astype(jnp.float32)
    for step, block in enumerate(blocks):
        at = chip ^ (step + 1)
        block[...] = (kept[at] + other[at].astype(jnp.float32)).astype(jnp.bfloat16)


def square_momenta(place, total, *refs):
    pieces, refs = refs[: SPLIT - 1], refs[SPLIT - 1 :]
    qkv_mom, out_mom, qkv_grad, out_grad, qkv_new, out_new, *refs = refs
    blocks, state = refs[:SPLIT], refs[SPLIT]
    depth, own = out_mom.shape
    whole = sum_pieces([total, *pieces])
    vec_own = depth // SPLIT
    for at in range(SPLIT):
        grad = whole[:depth, at * own : (at + 1) * own]
        if at < SPLIT - 1:
            qkv_grad[at] = grad
            moment = momentum_decay * qkv_mom[at] + grad
            qkv_new[at] = moment
        else:
            out_grad[...] = grad
            moment = momentum_decay * out_mom[...] + grad
            out_new[...] = moment
        state[at, :depth, :] = moment
        state[at, depth:, :] = jnp.zeros((whole.shape[0] - depth, own), jnp.float32)
        state[at, depth:, :vec_own] = whole[depth:, at * vec_own : (at + 1) * vec_own]
    for step, block in enumerate(blocks):
        block[...] = state[lax.rem(place[0] + step, SPLIT)].astype(jnp.bfloat16)


def join_squares(place, *refs):
    pieces, (gram, gram_other, mine, other, sums, rows) = refs[:SPLIT], refs[SPLIT:]
    depth, own = mine.shape[0], pieces[0].shape[1]
    total = jnp.zeros(sums.shape, jnp.float32)
    for step, piece in enumerate(pieces):
        total = total + piece[depth:, :].astype(jnp.float32)
        for at in range(SPLIT):

            @pl.when(source_of(place[0], step) == at)
            def _():
                rows[:, at * own : (at + 1) * own] = piece[:depth, :]

    sums[...] = total
    even = place[1] == 0
    gram_sum = (gram[...].astype(jnp.float32) + gram_other[...].astype(jnp.float32)).astype(jnp.bfloat16)
    mine[...] = jnp.where(even, rows[...], gram_sum)
    other[...] = jnp.where(even, gram_sum, rows[...])


def join_pair(place, mine, other, rows):
    depth = mine.shape[0]
    even = place[1] == 0
    rows[:depth, :] = jnp.where(even, mine[...], other[...])
    rows[depth:, :] = jnp.where(even, other[...], mine[...])


def run_kernel(body, outputs, scalars=0, scratch=(), ties=(), far=(), far_out=(), late=(), lanes={}):
    def call(*operands):
        operands = list(operands)
        count, made = len(operands), len(outputs)

        def whole(*refs):
            inputs, refs = list(refs[:count]), refs[count + len(ties) :]
            results, refs = list(refs[:made]), refs[made:]
            mine, refs = refs[: len(scratch)], refs[len(scratch) :]
            rooms, refs = refs[: len(far)], refs[len(far) :]
            rooms_out, signals = refs[: len(far_out)], refs[len(far_out) :]
            copies = []
            for at, room, signal in zip(far, rooms, signals):
                source = inputs[at].at[:, lanes[at]] if at in lanes else inputs[at]
                copies.append(pltpu.make_async_copy(source, room, signal))
                copies[-1].start()
                inputs[at] = room
            waits = [copy.wait for at, copy in zip(far, copies) if at in late]
            for at, copy in zip(far, copies):
                if at not in late:
                    copy.wait()
            targets = [results[at] for at in far_out]
            for at, room in zip(far_out, rooms_out):
                results[at] = room
            if late:
                body(waits, *inputs, *results, *mine)
            else:
                body(*inputs, *results, *mine)
            copies_out = []
            for room, target, signal in zip(rooms_out, targets, signals[len(far) :]):
                copies_out.append(pltpu.make_async_copy(room, target, signal))
                copies_out[-1].start()
            for copy in copies_out:
                copy.wait()

        rooms = []
        for at in far:
            shape = operands[at].shape
            if at in lanes:
                shape = (shape[0], lanes[at].size)
            rooms.append(pltpu.VMEM(shape, operands[at].dtype))
            operands[at] = pltpu.with_memory_space_constraint(operands[at], pltpu.HBM)
        kinds = list(outputs)
        for at in far_out:
            kinds[at] = pltpu.HBM(kinds[at].shape, kinds[at].dtype)
        spaces = [pltpu.SMEM] * scalars + [pltpu.VMEM] * (count - scalars) + [pl.ANY] * len(ties)
        for at in far:
            spaces[at] = pltpu.HBM
        spaces_out = [pltpu.HBM if at in far_out else pltpu.VMEM for at in range(made)]
        rooms_out = [pltpu.VMEM(outputs[at].shape, outputs[at].dtype) for at in far_out]
        signals = [pltpu.SemaphoreType.DMA] * (len(far) + len(far_out))
        return pl.pallas_call(
            whole,
            out_shape=kinds,
            in_specs=[pl.BlockSpec(memory_space=space) for space in spaces],
            out_specs=[pl.BlockSpec(memory_space=space) for space in spaces_out],
            scratch_shapes=[*scratch, *rooms, *rooms_out, *signals],
            compiler_params=pltpu.CompilerParams(vmem_limit_bytes=24 * 2**20),
        )(*operands, *ties)

    return call


def newton_schulz(waits, place, *refs):
    pieces, refs = refs[:SPLIT], refs[SPLIT:]
    wide, kept, sent, heard, gram, *factors = refs
    chip, core = place[2], place[1]
    width = heard.shape[0]
    for step, piece in enumerate(pieces):
        at = pl.multiple_of((chip ^ step) * piece.shape[0], piece.shape[0])
        heard[pl.ds(at, piece.shape[0]), :] = piece[...]
    depth = kept.shape[0]
    even = core == 0

    @pl.when(even)
    def _():
        gram[...] = dot(heard[...], heard[...], ((1,), (1,)))

    @pl.when(jnp.logical_not(even))
    def _():
        gram[...] = heard[...].astype(jnp.float32)

    at_row = lax.broadcasted_iota(jnp.int32, (width, width), 0)
    at_lane = lax.broadcasted_iota(jnp.int32, (width, width), 1)
    trace = jnp.sum(jnp.where(at_row == at_lane, gram[...], 0.0), keepdims=True)
    scale = jnp.sqrt(trace) + ortho_eps
    gram[...] = gram[...] / (scale * scale)
    count = 2 * depth
    start = pl.multiple_of(chip * count, count)
    for factor in factors:
        gram_b = gram[...].astype(jnp.bfloat16)
        square = dot(gram_b, gram_b, ((1,), (0,)))
        factor[...] = (coef_second * gram[...] + coef_third * square).astype(jnp.bfloat16)
        moved = dot(factor[...], gram_b, ((1,), (0,)))
        twice = dot(factor[...], moved.astype(jnp.bfloat16), ((1,), (0,)))
        gram[...] = coef_first * coef_first * gram[...] + 2.0 * coef_first * moved + twice
    eye = lax.broadcasted_iota(jnp.int32, (count, width), 0) + start
    eye = (eye == lax.broadcasted_iota(jnp.int32, (count, width), 1)).astype(jnp.float32)
    rows = gram[pl.ds(start, count), :]
    square = dot(rows.astype(jnp.bfloat16), gram[...].astype(jnp.bfloat16), ((1,), (0,)))
    rows = coef_first * eye + (coef_second * rows + coef_third * square)
    for factor in factors[::-1]:
        rows = coef_first * rows + dot(rows.astype(jnp.bfloat16), factor[...], ((1,), (0,)))
    waits[0]()
    rows = (rows / scale).astype(jnp.bfloat16)

    @pl.when(even)
    def _():
        state = dot(rows, heard[...], ((1,), (0,))).astype(jnp.bfloat16)
        kept[:, :width] = state[:depth]
        sent[:, :width] = state[depth:]
        kept[:, width:] = jnp.zeros_like(kept[:, width:])
        sent[:, width:] = jnp.zeros_like(sent[:, width:])

    @pl.when(jnp.logical_not(even))
    def _():
        state = dot(rows, wide[...], ((1,), (0,))).astype(jnp.bfloat16)
        kept[...] = state[depth:]
        sent[...] = state[:depth]


def split_device(
    tokens, cotangent, doc_lengths, qkv_w, out_w, ffn_w, vecs, qkv_mom, out_mom, ffn_mom, vec_mom
):
    micro, rows, width = tokens.shape
    shards = lax.axis_size("shard")
    groups = lax.axis_size("dp")
    column = lax.axis_index("shard")
    row = lax.axis_index("dp")
    place = jnp.stack([column, row & 1, row >> 1]).astype(jnp.int32)
    slots = micro * shards
    own = qkv_w.shape[2]
    hidden = ffn_w.shape[2]
    bf16 = jnp.bfloat16

    packed_kind = jax.ShapeDtypeStruct((ffn_w.shape[1], 2 * hidden + 3 * own + PAD), bf16)
    (packed,) = run_kernel(pack_weights, [packed_kind], far=(0, 1), far_out=(0,))(ffn_w, qkv_w)
    weights = lax.all_gather(packed, "dp", axis=0, tiled=True)

    flat = tokens.reshape(micro * rows, width)
    vec_rows, vec_own = vecs.shape
    small = jnp.concatenate(
        [vecs.astype(bf16).reshape(-1), doc_lengths.astype(bf16).reshape(-1)]
    )
    small = jnp.pad(small, (0, 8 * width - small.shape[0])).reshape(8, width)
    out_flat = out_w.astype(bf16).reshape(-1, width)
    out_count = out_flat.shape[0]
    heard = gather_direct(jnp.concatenate([flat, out_flat, small], axis=0), "shard")
    tokens_b = heard[:, : micro * rows].reshape(slots * rows, width)
    out_part = heard[:, micro * rows : micro * rows + out_count].reshape(shards, -1, own)
    out_part = out_part.transpose(1, 0, 2).reshape(-1, width)
    small = heard[:, micro * rows + out_count :].reshape(shards, -1)
    lengths = small[:, vecs.size : vecs.size + doc_lengths.size].astype(jnp.int32).reshape(slots, -1)
    small = small[:, : vecs.size].reshape(shards, vec_rows, vec_own).transpose(1, 0, 2).reshape(vec_rows, -1)
    vec = gather_double(small, "dp").transpose(1, 0, 2).reshape(vec_rows, -1).astype(jnp.float32)
    out_b = lax.all_gather(out_part, "dp", axis=0, tiled=True)
    position = jnp.arange(rows, dtype=jnp.int32)[None]
    ends = jnp.cumsum(lengths, axis=1)
    segment = jnp.sum((position[:, :, None] >= ends[:, None, :]).astype(jnp.int32), axis=2)
    valid = position < ends[:, -1:]
    slot = jnp.arange(slots, dtype=jnp.int32)[:, None]
    marks = jnp.where(valid, segment + slot * ends.shape[1], -1 - position - slot * rows)
    id_column, id_row = marks.reshape(-1, 1), marks.reshape(1, -1)
    bias_q = lax.dynamic_slice_in_dim(vec[0], column * own, own, 0)
    bias_v = lax.dynamic_slice_in_dim(vec[1], column * own, own, 0)
    bias_proj = jnp.concatenate([bias_q, jnp.zeros_like(bias_q), bias_v])[None]
    bias_up = lax.dynamic_slice_in_dim(vec[8:].reshape(-1), column * hidden, hidden, 0)[None]

    proj_lanes = pl.ds(2 * hidden, weights.shape[1] - 2 * hidden)
    ffn_lanes = pl.ds(0, 2 * hidden)
    qkv, mixed_own = run_kernel(
        attention_forward,
        [
            jax.ShapeDtypeStruct((slots * rows, 3 * own), bf16),
            jax.ShapeDtypeStruct((BLOCK, slots * rows // BLOCK * own), bf16),
        ],
        scalars=1,
        ties=[vec, bias_up],
        far=(1, 2, 4),
        far_out=(0,),
        lanes={2: proj_lanes},
    )(place, tokens_b, weights, bias_proj, id_column, id_row)

    depth = width // groups
    count = micro * rows
    whole_b = jax.ShapeDtypeStruct((slots * rows, width), bf16)
    own_f = jax.ShapeDtypeStruct((count, width), jnp.float32)
    own_b = jax.ShapeDtypeStruct((count, width), bf16)
    part_kinds = [own_f] + [own_b] * (shards - 1)
    sums_kind = jax.ShapeDtypeStruct((8, width), jnp.float32)
    moving = pltpu.VMEM((slots * rows, width), jnp.float32)

    mixed_pieces = pieces_of(mixed_own, "shard")
    first_b, activ_b, slope, first_in, *parts = run_kernel(
        layer_middle,
        [whole_b, whole_b, jax.ShapeDtypeStruct((slots * rows, hidden), jnp.float32), own_f] + part_kinds,
        scalars=1,
        scratch=[moving],
        far=(5, 6, 8),
        late=(8,),
        lanes={8: ffn_lanes},
    )(place, *mixed_pieces, out_b, tokens_b, vec, weights, bias_up)
    layer_out, d_branch_own, d_second, sums_two = run_kernel(
        second_norm, [own_b, own_b, own_f, sums_kind], scalars=1, far=(7, 8), far_out=(0, 2, 3)
    )(place, *send_parts(parts, "shard"), first_in, vec, cotangent.reshape(count, width), id_column)
    layer_out = layer_out.reshape(tokens.shape)
    d_branch_b, d_inner_b, d_bias_up, *parts = run_kernel(
        inner_backward,
        [whole_b, whole_b, jax.ShapeDtypeStruct((1, hidden), jnp.float32)] + part_kinds,
        scalars=1,
        scratch=[moving],
        far=(6,),
        far_out=(2, 3, 4, 5, 6),
        lanes={6: ffn_lanes},
    )(place, *pieces_of(d_branch_own, "shard"), slope, weights)
    (grads,) = run_kernel(inner_gradients, [jax.ShapeDtypeStruct((2, width, hidden), bf16)], far_out=(0,))(
        first_b, activ_b, d_inner_b, d_branch_b
    )
    summed = lax.psum_scatter(grads, "dp", scatter_dimension=1, tiled=True)
    d_first_in, d_attended_own, sums_one = run_kernel(
        first_norm, [own_f, own_b, sums_kind], far=(0, 4, 5), far_out=(0, 1, 2)
    )(*send_parts(parts, "shard"), d_second, first_in, vec)
    d_attended_pieces = pieces_of(d_attended_own, "shard")
    moment_kind = jax.ShapeDtypeStruct(ffn_mom.shape, ffn_mom.dtype)
    wide_kind = jax.ShapeDtypeStruct((depth, hidden), bf16)
    grad_ffn, new_ffn_mom, mine, far_send = run_kernel(
        wide_momenta,
        [moment_kind, moment_kind, wide_kind, wide_kind],
        scalars=1,
        ties=d_attended_pieces[1:],
        far=(1, 2),
        far_out=(0, 1),
    )(place, summed, ffn_mom)
    far_rows = swap(far_send, "shard", shards // 2)

    packed_rows = depth + 16
    kept, sent, d_proj = run_kernel(
        attention_backward,
        [
            jax.ShapeDtypeStruct((groups // 2, packed_rows, width), jnp.float32),
            jax.ShapeDtypeStruct((groups // 2, packed_rows, width), bf16),
            jax.ShapeDtypeStruct((slots * rows, 3 * own), bf16),
        ],
        scalars=1,
        scratch=[pltpu.VMEM((slots * rows, width), bf16), pltpu.VMEM((16, width), jnp.float32)],
        far=(1, 2, 3, 4, 9, 10, 11, 5, 6, 7, 8, 13, 14, 15),
        far_out=(0, 2),
        late=(5, 6, 7, 8, 13, 14, 15),
        ties=[far_send],
    )(
        place, *d_attended_pieces, *mixed_pieces, out_b, qkv, id_column, id_row, tokens_b,
        sums_one, sums_two, d_bias_up,
    )
    (wide_rows,) = run_kernel(
        join_wide, [jax.ShapeDtypeStruct((depth, 2 * hidden), bf16)], ties=[kept], far_out=(0,)
    )(mine, far_rows)
    wide = lax.all_gather(wide_rows, "dp", axis=0, tiled=True)
    block_kind = jax.ShapeDtypeStruct((packed_rows, width), bf16)
    total, *blocks = run_kernel(
        pair_sum, [jax.ShapeDtypeStruct((packed_rows, width), jnp.float32)] + [block_kind] * 3, scalars=1, far=(1,)
    )(place, kept, swap(sent, "dp", 1))
    block_kind = jax.ShapeDtypeStruct((packed_rows, own), bf16)
    like = [jax.ShapeDtypeStruct(each.shape, each.dtype) for each in (qkv_mom, out_mom)]
    grad_qkv, grad_wout, new_qkv_mom, new_out_mom, *blocks = run_kernel(
        square_momenta,
        like + like + [block_kind] * shards,
        scalars=1,
        scratch=[pltpu.VMEM((shards, packed_rows, own), jnp.float32)],
        far=(5, 6),
        far_out=(0, 1, 2, 3),
    )(place, total, *[swap(block, "dp", 2 * at + 2) for at, block in enumerate(blocks)], qkv_mom, out_mom)
    square_pieces = send_parts(blocks, "shard")
    (gram_rows,) = run_kernel(wide_gram, [jax.ShapeDtypeStruct((depth, width), bf16)], ties=square_pieces[1:], far=(0, 1))(
        wide_rows, wide
    )
    row_kind = jax.ShapeDtypeStruct((depth, width), bf16)
    mine, other, grad_vec = run_kernel(
        join_squares,
        [row_kind, row_kind, jax.ShapeDtypeStruct((packed_rows - depth, own), jnp.float32)],
        scalars=1,
        scratch=[pltpu.VMEM((depth, width), bf16)],
    )(place, *square_pieces, gram_rows, swap(gram_rows, "shard", 1))
    grad_vec = grad_vec[:vec_rows, :vec_own]
    (pair_rows,) = run_kernel(
        join_pair, [jax.ShapeDtypeStruct((2 * depth, width), bf16)], scalars=1
    )(place, mine, swap(other, "dp", 1))
    pair_pieces = [pair_rows] + [swap(pair_rows, "dp", bit) for bit in (2, 4, 6)]
    (part,) = run_kernel(
        token_part, [whole_b], ties=[pair_rows], far=(0, 1), far_out=(0,), lanes={1: proj_lanes}
    )(d_proj, weights)
    d_tokens = lax.psum_scatter(part, "shard", scatter_dimension=0, tiled=True)
    state_kind = jax.ShapeDtypeStruct((depth, 2 * hidden), bf16)
    kept, sent = run_kernel(
        newton_schulz,
        [state_kind, state_kind],
        scalars=1,
        scratch=[pltpu.VMEM((width, width), bf16), pltpu.VMEM((width, width), jnp.float32)]
        + [pltpu.VMEM((width, width), bf16)] * (NS_STEPS - 1),
        far=(5,),
        late=(5,),
    )(place, *pair_pieces, wide)
    block_kind = jax.ShapeDtypeStruct((depth, own), bf16)
    wide_kind = jax.ShapeDtypeStruct((depth, hidden), bf16)
    kinds = [block_kind] * shards + [wide_kind]
    kinds[shards // 2] = jax.ShapeDtypeStruct((depth, hidden + own), bf16)
    *blocks, mine = run_kernel(
        split_state, kinds, scalars=1
    )(place, kept, swap(sent, "dp", 1))
    state_pieces = send_parts(blocks, "shard")
    flag_kind = jax.ShapeDtypeStruct((8, 128), jnp.float32)
    d_tokens, flag = run_kernel(add_rows, [own_f, flag_kind], ties=[state_pieces[1]], far=(0, 1), far_out=(0,))(
        d_first_in, d_tokens
    )
    qkv_new, out_new, ffn_new = run_kernel(
        new_weights,
        [jax.ShapeDtypeStruct(each.shape, each.dtype) for each in (qkv_w, out_w, ffn_w)],
        scalars=1,
        scratch=[pltpu.VMEM((shards, depth, own), jnp.float32)],
        ties=[flag],
        far=(6, 7, 8),
        far_out=(0, 1, 2),
    )(
        place, *state_pieces, mine, qkv_w, out_w, ffn_w
    )

    d_tokens = d_tokens.reshape(tokens.shape)
    token_count = micro * rows * groups * shards
    new_vec_mom = momentum_decay * vec_mom + grad_vec
    vec_new = vecs - vec_rate * token_count ** (-0.5) * new_vec_mom
    return (
        layer_out,
        d_tokens,
        grad_qkv,
        grad_wout,
        grad_ffn,
        grad_vec,
        new_qkv_mom,
        new_out_mom,
        new_ffn_mom,
        new_vec_mom,
        qkv_new,
        out_new,
        ffn_new,
        vec_new,
    )


def solution(mesh):
    fits = (mesh.shape["dp"], mesh.shape["shard"]) == (8, 4)
    in_specs = (
        P(("dp", "shard"), None, None),
        P(("dp", "shard"), None, None),
        P(("dp", "shard"), None),
        P(None, "dp", "shard"),
        P("dp", "shard"),
        P(None, "dp", "shard"),
        P(None, ("dp", "shard")),
        P(None, "dp", "shard"),
        P("dp", "shard"),
        P(None, "dp", "shard"),
        P(None, ("dp", "shard")),
    )
    out_specs = (
        P(("dp", "shard"), None, None),
        P(("dp", "shard"), None, None),
        P(None, "dp", "shard"),
        P("dp", "shard"),
        P(None, "dp", "shard"),
        P(None, ("dp", "shard")),
        P(None, "dp", "shard"),
        P("dp", "shard"),
        P(None, "dp", "shard"),
        P(None, ("dp", "shard")),
        P(None, "dp", "shard"),
        P("dp", "shard"),
        P(None, "dp", "shard"),
        P(None, ("dp", "shard")),
    )
    return jax.shard_map(
        split_device if fits else per_device, mesh=mesh, in_specs=in_specs, out_specs=out_specs, check_vma=False
    )
```
